32 devices in a mesh: ctx: 8 (over z, y), fsdp: 4 (over x, core).
Axes of the slice: x: 2, y: 2, z: 4, core: 2. Of those that a mesh axis runs over, the one named last changes fastest.
Arguments:
- inputs: bfloat16 [4, 1024, 1024], P('fsdp', 'ctx'), may hold values from -6 to 6
- out_grad: bfloat16 [4, 1024, 1024], P('fsdp', 'ctx'), may hold values from -6 to 6
- segments: int32 [4, 1024], P('fsdp', 'ctx'), may hold values from 0 to 1, never falling along the last dimension, each value on 1 to 768 neighbouring positions
- pairs: int32 [4, 8], P('fsdp', 'ctx'), may hold values from 0 to 7, each once within a row
- w_qkv: float32 [1024, 3072], P(('ctx', 'fsdp')), may hold values from -0.1875 to 0.1875
- w_out: float32 [1024, 1024], P(('ctx', 'fsdp')), may hold values from -0.5 to 0.5
- w_up: float32 [1024, 4096], P(('ctx', 'fsdp'))
- w_down: float32 [4096, 1024], P(('ctx', 'fsdp')), may hold values from -0.09375 to 0.09375
- up_bias: float32 [4096], P(('ctx', 'fsdp'))
- vectors: float32 [8, 1024], P(None, ('ctx', 'fsdp')), as said below
- first_qkv: float32 [1024, 3072], P(('ctx', 'fsdp'))
- first_out: float32 [1024, 1024], P(('ctx', 'fsdp'))
- first_up: float32 [1024, 4096], P(('ctx', 'fsdp'))
- first_down: float32 [4096, 1024], P(('ctx', 'fsdp'))
- first_bias: float32 [4096], P(('ctx', 'fsdp'))
- first_vectors: float32 [8, 1024], P(None, ('ctx', 'fsdp'))
- second_qkv: float32 [1024, 3072], P(('ctx', 'fsdp')), as said below
- second_out: float32 [1024, 1024], P(('ctx', 'fsdp')), as said below
- second_up: float32 [1024, 4096], P(('ctx', 'fsdp')), as said below
- second_down: float32 [4096, 1024], P(('ctx', 'fsdp')), as said below
- second_bias: float32 [4096], P(('ctx', 'fsdp')), as said below
- second_vectors: float32 [8, 1024], P(None, ('ctx', 'fsdp')), as said below
Outputs:
- outputs: bfloat16 [4, 1024, 1024], P('fsdp', 'ctx')
- in_grad: float32 [4, 1024, 1024], P('fsdp', 'ctx')
- grad_norm: float32 [], replicated
- grad_qkv: float32 [1024, 3072], P(('ctx', 'fsdp'))
- update_qkv: float32 [1024, 3072], P(('ctx', 'fsdp'))
- next_first_qkv: float32 [1024, 3072], P(('ctx', 'fsdp'))
- next_second_qkv: float32 [1024, 3072], P(('ctx', 'fsdp'))
- grad_out: float32 [1024, 1024], P(('ctx', 'fsdp'))
- update_out: float32 [1024, 1024], P(('ctx', 'fsdp'))
- next_first_out: float32 [1024, 1024], P(('ctx', 'fsdp'))
- next_second_out: float32 [1024, 1024], P(('ctx', 'fsdp'))
- grad_up: float32 [1024, 4096], P(('ctx', 'fsdp'))
- update_up: float32 [1024, 4096], P(('ctx', 'fsdp'))
- next_first_up: float32 [1024, 4096], P(('ctx', 'fsdp'))
- next_second_up: float32 [1024, 4096], P(('ctx', 'fsdp'))
- grad_down: float32 [4096, 1024], P(('ctx', 'fsdp'))
- update_down: float32 [4096, 1024], P(('ctx', 'fsdp'))
- next_first_down: float32 [4096, 1024], P(('ctx', 'fsdp'))
- next_second_down: float32 [4096, 1024], P(('ctx', 'fsdp'))
- grad_bias: float32 [4096], P(('ctx', 'fsdp'))
- update_bias: float32 [4096], P(('ctx', 'fsdp'))
- next_first_bias: float32 [4096], P(('ctx', 'fsdp'))
- next_second_bias: float32 [4096], P(('ctx', 'fsdp'))
- grad_vectors: float32 [8, 1024], P(None, ('ctx', 'fsdp'))
- update_vectors: float32 [8, 1024], P(None, ('ctx', 'fsdp'))
- next_first_vectors: float32 [8, 1024], P(None, ('ctx', 'fsdp'))
- next_second_vectors: float32 [8, 1024], P(None, ('ctx', 'fsdp'))
The draws below stay inside these ranges and needn't reach their ends.
Inputs may be any that keep to these rules, and one draw needn't show every extreme that they name: `segments`: in each sequence the numbers never fall; every document spans 1 to 768 positions. `pairs`: each row is a permutation. `vectors`: rows 0 and 2 are positive. `second_qkv`: positive. `second_out`: positive. `second_up`: positive. `second_down`: positive. `second_bias`: positive. `second_vectors`: positive.
All inputs are finite; a program needn't handle non-finite values.
Results may differ from the reference program's by a relative error of at most 0.023.
Values may be sent and summed in bfloat16 or wider, within the bound.
No kernel may reach another device: no remote copies, remote signals or barrier semaphores. Data moves between devices by JAX's collectives and lax.ppermute only.
A program may use at most 256 MiB of HBM per device.

```python
import math
import jax
import jax.numpy as jnp
import numpy as np
from jax import lax

D = 1024
HEADS = 16
HD = 64
FF = 4096
BLOCK = 64
SEQ = 1024
SEQS = 4
DOCS = 2
DOC_MOST = 768
NPAR = 12595200
N_CTX = 8


def first_moment(key, tag, shape):
    return 0.11 * NPAR ** (-0.5) * jax.random.normal(jax.random.fold_in(key, tag), shape, jnp.float32)


def second_moment(key, tag, shape):
    level = jax.random.uniform(jax.random.fold_in(key, tag), shape, jnp.float32, math.log(0.02), math.log(0.1))
    return jnp.exp(level) / NPAR


def draw_w_up(key, part):
    key = jax.random.fold_in(key, 303)
    key_column, key_noise = jax.random.split(key)
    column = D ** (-0.5) * jax.random.normal(key_column, (FF,), jnp.float32)
    noise = jax.random.normal(key_noise, (D, FF), jnp.float32)
    return noise * D ** (-0.5) + column[None, :]


def draw_vectors(key, part):
    key_rough, key_base = jax.random.split(jax.random.fold_in(key, 101))
    frac = jnp.arange(D).astype(jnp.float32) / max(D - 1, 1)
    ramp = 0.5 + frac
    rough = jax.random.uniform(key_rough, (8, D), jnp.float32, 0.8, 1.2)
    base = 0.25 * jax.random.normal(key_base, (8, D), jnp.float32)
    rows = jnp.arange(8)[:, None]
    gains = (rows == 0) | (rows == 2)
    return jnp.where(gains, ramp[None, :] * rough, base)


def draw_up_bias(key, part):
    frac = jnp.arange(FF).astype(jnp.float32) / max(FF - 1, 1)
    inner = jax.random.fold_in(key, 202)
    return -1.0 + 2.5 * frac + 0.3 * jax.random.normal(inner, (FF,), jnp.float32)


def draw_first_qkv(key, part):
    return first_moment(key, 11, (D, 3 * D))


def draw_first_out(key, part):
    return first_moment(key, 12, (D, D))


def draw_first_up(key, part):
    return first_moment(key, 13, (D, FF))


def draw_first_down(key, part):
    return first_moment(key, 14, (FF, D))


def draw_first_bias(key, part):
    return first_moment(key, 15, (FF,))


def draw_first_vectors(key, part):
    return first_moment(key, 16, (8, D))


def draw_second_qkv(key, part):
    return second_moment(key, 21, (D, 3 * D))


def draw_second_out(key, part):
    return second_moment(key, 22, (D, D))


def draw_second_up(key, part):
    return second_moment(key, 23, (D, FF))


def draw_second_down(key, part):
    return second_moment(key, 24, (FF, D))


def draw_second_bias(key, part):
    return second_moment(key, 25, (FF,))


def draw_second_vectors(key, part):
    return second_moment(key, 26, (8, D))


def levels(own_key, dims, cuts, low, top_value):
    def one(dim, parts):
        steps = jax.random.uniform(jax.random.fold_in(jax.random.fold_in(own_key, 6), dim), (parts,), jnp.float32, low / len(cuts), top_value / len(cuts))
        return jnp.repeat(jnp.exp(steps), dims[dim] // parts).reshape((-1,) + (1,) * (len(dims) - dim - 1))

    factor_of = one(*cuts[0])
    for cut in cuts[1:]:
        factor_of = factor_of * one(*cut)
    return factor_of


def split_up(amount, total, limit, lean):
    weights = [(1 << 20) // math.isqrt(rank ** lean) + 1 for rank in range(2, amount + 1)]
    rest, given = total - limit - (amount - 1), [1] * (amount - 1)
    while rest > 0:
        candidates = [i for i in range(amount - 1) if given[i] < limit]
        pool, remaining = sum([weights[i] for i in candidates]), rest
        for i in candidates:
            more = min(limit - given[i], max(1, remaining * weights[i] // pool), rest)
            given[i] = given[i] + more
            rest = rest - more
    return np.array([limit] + given)


def ragged(rng, count, total, reach, skew):
    if count == 2:
        one = jax.random.randint(rng, (), max(1, total - reach), min(reach, total - 1) + 1)
        return jnp.stack([one, total - one])
    sizes = jnp.asarray(split_up(count, total, reach, skew), jnp.int32)
    couples = (count - 1) // 2
    source_of, receiver = sizes[1:1 + 2 * couples:2], sizes[2:2 + 2 * couples:2]
    margin = jnp.minimum(source_of - 1, reach - receiver)
    passed = jax.random.randint(jax.random.fold_in(rng, 1), (couples,), 0, 1 << 20) % (margin + 1)
    sizes = sizes.at[1:1 + 2 * couples:2].set(source_of - passed).at[2:2 + 2 * couples:2].set(receiver + passed)
    return sizes[jax.random.permutation(jax.random.fold_in(rng, 2), count)]


def gaussian(stream_key, dims, scale, reach, cuts=(), kind=jnp.bfloat16):
    values = scale * jax.random.normal(stream_key, dims, jnp.float32)
    if cuts:
        values = values * levels(stream_key, dims, cuts, -0.22, 0.18)
    return jnp.clip(values, -reach, reach).astype(kind)


def setup_inputs(seed: int = 0) -> dict:
    key_list = jax.random.split(jax.random.key(seed), 23)
    return {
        "inputs": gaussian(key_list[0], (SEQS, SEQ, D), 1.0, 6.0, ((0, 4), (1, 8))),
        "out_grad": gaussian(key_list[1], (SEQS, SEQ, D), 1.0, 6.0, ((0, 4), (1, 8))),
        "segments": jax.vmap(lambda own: jnp.searchsorted(jnp.cumsum(ragged(own, DOCS, SEQ, DOC_MOST, 1)), jnp.arange(SEQ), side="right"))(jax.random.split(key_list[2], SEQS)).reshape((SEQS, SEQ)).astype(jnp.int32),
        "pairs": jax.vmap(lambda own: jax.random.permutation(own, N_CTX))(jax.random.split(key_list[3], SEQS)).reshape((SEQS, N_CTX)).astype(jnp.int32),
        "w_qkv": gaussian(key_list[4], (D, 3 * D), D ** -0.5, 0.1875, ((0, 32),), jnp.float32),
        "w_out": gaussian(key_list[5], (D, D), (D // 8) ** -0.5, 0.5, ((0, 32),), jnp.float32),
        "w_up": draw_w_up(jax.random.fold_in(key_list[22], 71), 0),
        "w_down": gaussian(key_list[7], (FF, D), FF ** -0.5, 0.09375, ((0, 32),), jnp.float32),
        "up_bias": draw_up_bias(jax.random.fold_in(key_list[22], 71), 0),
        "vectors": draw_vectors(jax.random.fold_in(key_list[22], 71), 0),
        "first_qkv": draw_first_qkv(jax.random.fold_in(key_list[22], 71), 0),
        "first_out": draw_first_out(jax.random.fold_in(key_list[22], 71), 0),
        "first_up": draw_first_up(jax.random.fold_in(key_list[22], 71), 0),
        "first_down": draw_first_down(jax.random.fold_in(key_list[22], 71), 0),
        "first_bias": draw_first_bias(jax.random.fold_in(key_list[22], 71), 0),
        "first_vectors": draw_first_vectors(jax.random.fold_in(key_list[22], 71), 0),
        "second_qkv": draw_second_qkv(jax.random.fold_in(key_list[22], 71), 0),
        "second_out": draw_second_out(jax.random.fold_in(key_list[22], 71), 0),
        "second_up": draw_second_up(jax.random.fold_in(key_list[22], 71), 0),
        "second_down": draw_second_down(jax.random.fold_in(key_list[22], 71), 0),
        "second_bias": draw_second_bias(jax.random.fold_in(key_list[22], 71), 0),
        "second_vectors": draw_second_vectors(jax.random.fold_in(key_list[22], 71), 0),
    }


norm_eps = 1e-05
beta_one = 0.9
beta_two = 0.95
adam_eps = 1e-08
learn_rate = 0.02
weight_decay = 0.1
adam_step = 10
max_norm = 1.0
masked = -1e+30
highest = lax.Precision.HIGHEST

@jax.custom_vjp
def low(v):
    return lax.optimization_barrier(v.astype(jnp.bfloat16)).astype(jnp.float32)

@jax.custom_vjp
def low_back(v):
    return v

def low_keep(v):
    return (low(v), None)

def low_pass(kept, grad):
    return (grad,)

def back_keep(v):
    return (v, None)

def back_low(kept, grad):
    return (low(grad),)
low.defvjp(low_keep, low_pass)
low_back.defvjp(back_keep, back_low)

def layer_norm(field, gain, shift):
    center = field - lax.optimization_barrier(jnp.mean(field, -1, keepdims=True))
    spread = lax.optimization_barrier(jnp.mean(center * center, -1, keepdims=True))
    return center * lax.rsqrt(spread + norm_eps) * gain + shift

def place(pair_row):
    blocks = jnp.stack([pair_row, 2 * N_CTX - 1 - pair_row], 1).reshape(-1)
    offsets = jnp.arange(BLOCK, dtype=jnp.int32)
    return (blocks[:, None] * BLOCK + offsets[None, :]).reshape(-1).astype(jnp.int32)

def layer(field, params, position, document):
    w_qkv, w_out, w_up, w_down, up_bias, vectors = [low(item) for item in params]
    normed = low(layer_norm(field, vectors[0], vectors[1]))
    mixed = jnp.dot(normed, w_qkv, precision=highest)
    query = low_back(low(mixed[:, :D] + vectors[4]))
    keys = low_back(low(mixed[:, D:2 * D]))
    values = low_back(low(mixed[:, 2 * D:] + vectors[5]))
    key_heads = keys.reshape(SEQ, HEADS, HD)
    value_heads = values.reshape(SEQ, HEADS, HD)
    slope = 2.0 ** (-8.0 * (jnp.arange(HEADS).astype(jnp.float32) + 1.0) / HEADS)
    rows = 512 if SEQ % 512 == 0 else SEQ
    count = SEQ // rows

    def attend(items):
        query_block, pos_block, doc_block = items
        raw = jnp.einsum('rhe,khe->hrk', query_block, key_heads, precision=highest) * HD ** (-0.5)
        offsets = (position[None, :] - pos_block[:, None]).astype(jnp.float32)
        raw = low_back(raw + slope[:, None, None] * offsets[None])
        allowed = (doc_block[:, None] == document[None, :]) & (position[None, :] <= pos_block[:, None])
        scores = jnp.where(allowed[None], raw, masked)
        top = lax.optimization_barrier(jnp.max(scores, -1, keepdims=True))
        expo = jnp.exp(scores - top)
        probs = expo / lax.optimization_barrier(jnp.sum(expo, -1, keepdims=True))
        return jnp.einsum('hrk,khe->rhe', low(probs), value_heads, precision=highest)
    attended = lax.map(jax.checkpoint(attend), (query.reshape(count, rows, HEADS, HD), position.reshape(count, rows), document.reshape(count, rows)))
    attended = low_back(low(attended.reshape(SEQ, D)))
    resid = field + low_back(jnp.dot(attended, w_out, precision=highest)) + vectors[6]
    normed_two = low(layer_norm(resid, vectors[2], vectors[3]))
    pre = low_back(jnp.dot(normed_two, w_up, precision=highest) + up_bias)
    hidden = low(jax.nn.gelu(pre, approximate=False))
    return resid + jnp.dot(hidden, w_down, precision=highest) + vectors[7]

def adamw(weight, grad, first, second, clip):
    clipped = grad * clip
    first_new = beta_one * first + (1.0 - beta_one) * clipped
    second_new = beta_two * second + (1.0 - beta_two) * clipped * clipped
    first_hat = first_new / (1.0 - beta_one ** adam_step)
    second_hat = second_new / (1.0 - beta_two ** adam_step)
    update = -learn_rate * (first_hat / (jnp.sqrt(second_hat) + adam_eps) + weight_decay * weight)
    return (update, first_new, second_new)

def reference(inputs, out_grad, segments, pairs, w_qkv, w_out, w_up, w_down, up_bias, vectors, first_qkv, first_out, first_up, first_down, first_bias, first_vectors, second_qkv, second_out, second_up, second_down, second_bias, second_vectors):
    params = (w_qkv, w_out, w_up, w_down, up_bias, vectors)

    def one_sequence(total, items):
        field, cotangent, seg_row, pair_row = items
        position = place(pair_row)
        document = jnp.take(seg_row, position)
        result, back = jax.vjp(lambda v, p: layer(v, p, position, document), field.astype(jnp.float32), params)
        grad_field, grad_params = back(cotangent.astype(jnp.float32))
        total = jax.tree.map(lambda a, b: a + b, total, grad_params)
        return (total, (result.astype(jnp.bfloat16), grad_field))
    zeros = jax.tree.map(lambda a: jnp.zeros(a.shape, jnp.float32), params)
    grads, (outputs, in_grad) = lax.scan(one_sequence, zeros, (inputs, out_grad, segments, pairs))
    squares = sum([jnp.sum(item * item) for item in grads])
    grad_norm = jnp.sqrt(squares)
    clip = jnp.minimum(1.0, max_norm / (grad_norm + 1e-06))
    firsts = (first_qkv, first_out, first_up, first_down, first_bias, first_vectors)
    seconds = (second_qkv, second_out, second_up, second_down, second_bias, second_vectors)
    results = []
    for weight, grad, first, second in zip(params, grads, firsts, seconds):
        update, first_new, second_new = adamw(weight, grad, first, second, clip)
        results = results + [grad, update, first_new, second_new]
    return (outputs, in_grad, grad_norm, results[0], results[1], results[2], results[3], results[4], results[5], results[6], results[7], results[8], results[9], results[10], results[11], results[12], results[13], results[14], results[15], results[16], results[17], results[18], results[19], results[20], results[21], results[22], results[23])
```

```python
import jax
import jax.numpy as jnp
from jax import lax
from jax.sharding import Mesh
from jax.sharding import PartitionSpec as P

HEADS = 16
HD = 64


norm_eps = 1e-05
beta_one = 0.9
beta_two = 0.95
adam_eps = 1e-08
learn_rate = 0.02
weight_decay = 0.1
adam_step = 10
max_norm = 1.0
masked = -1e30
group_heads = 2


def layer_norm(field, gain, shift):
    center = field - jnp.mean(field, -1, keepdims=True)
    spread = jnp.mean(center * center, -1, keepdims=True)
    return center * lax.rsqrt(spread + norm_eps) * gain + shift


def gelu_exact(field):
    return jax.nn.gelu(field, approximate=False)


def contract(left, right, left_dim, right_dim):
    return lax.dot_general(
        left, right, (((left_dim,), (right_dim,)), ((), ())), preferred_element_type=jnp.float32
    )


def place(pair_ids, block, n_ctx):
    blocks = jnp.stack([pair_ids, 2 * n_ctx - 1 - pair_ids], 1).reshape(-1)
    offsets = jnp.arange(block, dtype=jnp.int32)
    return (blocks[:, None] * block + offsets[None, :]).reshape(-1)


def pick(array, first):
    return lax.dynamic_slice_in_dim(array, first, group_heads, 1)


def adamw(weight, grad, first, second, clip):
    clipped = grad * clip
    first_new = beta_one * first + (1.0 - beta_one) * clipped
    second_new = beta_two * second + (1.0 - beta_two) * clipped * clipped
    first_hat = first_new / (1.0 - beta_one**adam_step)
    second_hat = second_new / (1.0 - beta_two**adam_step)
    update = -learn_rate * (first_hat / (jnp.sqrt(second_hat) + adam_eps) + weight_decay * weight)
    return (update, first_new, second_new)


def local(
    inputs,
    out_grad,
    segments,
    pairs,
    w_qkv,
    w_out,
    w_up,
    w_down,
    up_bias,
    vectors,
    first_qkv,
    first_out,
    first_up,
    first_down,
    first_bias,
    first_vectors,
    second_qkv,
    second_out,
    second_up,
    second_down,
    second_bias,
    second_vectors,
):
    low_type = jnp.bfloat16
    n_ctx = lax.axis_size("ctx")
    field = inputs[0].astype(jnp.float32)
    tokens = field.shape[0]
    block = tokens // 2
    width = field.shape[1]
    seq_len = tokens * n_ctx
    scale = HD ** (-0.5)
    groups = HEADS // group_heads
    slope = 2.0 ** (-8.0 * (jnp.arange(HEADS, dtype=jnp.float32) + 1.0) / HEADS)
    qkv_w, out_w, vec_low = (
        lax.all_gather(w_qkv.astype(low_type), ("ctx", "fsdp"), axis=0, tiled=True),
        lax.all_gather(w_out.astype(low_type), ("ctx", "fsdp"), axis=0, tiled=True),
        lax.all_gather(vectors.astype(low_type), ("ctx", "fsdp"), axis=1, tiled=True),
    )
    vec = vec_low.astype(jnp.float32)
    gain_one, shift_one, gain_two, shift_two = (vec[0], vec[1], vec[2], vec[3])
    bias_query, bias_value, bias_out, bias_down = (vec[4], vec[5], vec[6], vec[7])
    normed_one = layer_norm(field, gain_one, shift_one)
    attn_in = normed_one.astype(low_type)
    mixed = jnp.dot(attn_in, qkv_w, preferred_element_type=jnp.float32)
    query = (mixed[:, :width] + bias_query).astype(low_type)
    keys = mixed[:, width : 2 * width].astype(low_type)
    values = (mixed[:, 2 * width :] + bias_value).astype(low_type)
    pair_ids = pairs[0]
    kv_all, pair_all, seg_all = (
        lax.all_gather(jnp.concatenate([keys, values], 1), "ctx", axis=0, tiled=True),
        lax.all_gather(pair_ids, "ctx", axis=0, tiled=True),
        lax.all_gather(segments[0], "ctx", axis=0, tiled=True),
    )
    pos_query = place(pair_ids, block, n_ctx)
    pos_key = place(pair_all, block, n_ctx)
    seg_query = jnp.take(seg_all, pos_query)
    seg_key = jnp.take(seg_all, pos_key)
    relative = (pos_key[None, :] - pos_query[:, None]).astype(jnp.float32)
    allowed = (seg_query[:, None] == seg_key[None, :]) & (pos_key[None, :] <= pos_query[:, None])
    query_heads = query.reshape(tokens, HEADS, HD)
    key_heads = kv_all[:, :width].reshape(seq_len, HEADS, HD)
    value_heads = kv_all[:, width:].reshape(seq_len, HEADS, HD)

    def scores_of(query_part, key_part, first, offsets, visible):
        slopes = lax.dynamic_slice_in_dim(slope, first, group_heads, 0)
        raw = (
            jnp.einsum("rhe,khe->hrk", query_part, key_part, preferred_element_type=jnp.float32)
            * scale
        )
        raw = raw + slopes[:, None, None] * offsets[None]
        return jnp.where(visible[None], raw, masked)

    def forward_group(index, carry):
        attended, log_total = carry
        first = index * group_heads
        scores = scores_of(
            pick(query_heads, first), pick(key_heads, first), first, relative, allowed
        )
        top = jnp.max(scores, -1, keepdims=True)
        expo = jnp.exp(scores - top)
        total = jnp.sum(expo, -1, keepdims=True)
        chance_low = (expo / total).astype(low_type)
        part_out = jnp.einsum(
            "hrk,khe->rhe", chance_low, pick(value_heads, first), preferred_element_type=jnp.float32
        )
        attended = lax.dynamic_update_slice_in_dim(attended, part_out, first, 1)
        log_total = lax.dynamic_update_slice_in_dim(
            log_total, (top + jnp.log(total))[:, :, 0].T, first, 1
        )
        return (attended, log_total)

    attended, log_total = lax.fori_loop(
        0,
        groups,
        forward_group,
        (jnp.zeros((tokens, HEADS, HD), jnp.float32), jnp.zeros((tokens, HEADS), jnp.float32)),
    )
    attended_low = attended.reshape(tokens, width).astype(low_type)
    resid = field + jnp.dot(attended_low, out_w, preferred_element_type=jnp.float32) + bias_out
    normed_two = layer_norm(resid, gain_two, shift_two)
    mlp_in = normed_two.astype(low_type)
    up_w, down_w, up_low = (
        lax.all_gather(w_up.astype(low_type), ("ctx", "fsdp"), axis=0, tiled=True),
        lax.all_gather(w_down.astype(low_type), ("ctx", "fsdp"), axis=0, tiled=True),
        lax.all_gather(up_bias.astype(low_type), ("ctx", "fsdp"), axis=0, tiled=True),
    )
    pre = jnp.dot(mlp_in, up_w, preferred_element_type=jnp.float32) + up_low.astype(jnp.float32)
    hidden = gelu_exact(pre).astype(low_type)
    result = resid + jnp.dot(hidden, down_w, preferred_element_type=jnp.float32) + bias_down
    cotangent_low = out_grad[0]
    cotangent = cotangent_low.astype(jnp.float32)
    up_back, down_back = (
        lax.all_gather(w_up.astype(low_type), ("ctx", "fsdp"), axis=0, tiled=True),
        lax.all_gather(w_down.astype(low_type), ("ctx", "fsdp"), axis=0, tiled=True),
    )
    grad_down_term = contract(hidden, cotangent_low, 0, 0)
    grad_bias_down = jnp.sum(cotangent, 0)
    grad_hidden = contract(cotangent_low, down_back, 1, 1)
    gelu_back = jax.vjp(gelu_exact, pre)[1]
    grad_pre = gelu_back(grad_hidden)[0].astype(low_type)
    grad_up_bias = jnp.sum(grad_pre.astype(jnp.float32), 0)
    grad_up_term = contract(mlp_in, grad_pre, 0, 0)
    grad_normed_two = contract(grad_pre, up_back, 1, 1)
    norm_two_back = jax.vjp(layer_norm, resid, gain_two, shift_two)[1]
    grad_resid_norm, grad_gain_two, grad_shift_two = norm_two_back(grad_normed_two)
    grad_resid = cotangent + grad_resid_norm
    grad_up_own, grad_down_own, grad_bias_own = (
        lax.psum_scatter(grad_up_term, ("ctx", "fsdp"), scatter_dimension=0, tiled=True),
        lax.psum_scatter(grad_down_term, ("ctx", "fsdp"), scatter_dimension=0, tiled=True),
        lax.psum_scatter(grad_up_bias, ("ctx", "fsdp"), scatter_dimension=0, tiled=True),
    )
    qkv_back, out_back = (
        lax.all_gather(w_qkv.astype(low_type), ("ctx", "fsdp"), axis=0, tiled=True),
        lax.all_gather(w_out.astype(low_type), ("ctx", "fsdp"), axis=0, tiled=True),
    )
    grad_bias_out = jnp.sum(grad_resid, 0)
    resid_low = grad_resid.astype(low_type)
    grad_out_term = contract(attended_low, resid_low, 0, 0)
    back_low = contract(resid_low, out_back, 1, 1).astype(low_type)
    back_heads = back_low.reshape(tokens, HEADS, HD)

    def backward_group(index, carry):
        grad_query, grad_key, grad_value = carry
        first = index * group_heads
        query_part = pick(query_heads, first)
        key_part = pick(key_heads, first)
        value_part = pick(value_heads, first)
        back_part = pick(back_heads, first)
        scores = scores_of(query_part, key_part, first, relative, allowed)
        logsum = lax.dynamic_slice_in_dim(log_total, first, group_heads, 1).T
        chance = jnp.exp(scores - logsum[:, :, None])
        pushed = jnp.einsum(
            "rhe,khe->hrk", back_part, value_part, preferred_element_type=jnp.float32
        )
        centre = jnp.sum(chance * pushed, -1, keepdims=True)
        dscore = (chance * (pushed - centre)).astype(low_type)
        chance_low = chance.astype(low_type)
        part_query = (
            jnp.einsum("hrk,khe->rhe", dscore, key_part, preferred_element_type=jnp.float32) * scale
        )
        part_key = (
            jnp.einsum("hrk,rhe->khe", dscore, query_part, preferred_element_type=jnp.float32)
            * scale
        )
        part_value = jnp.einsum(
            "hrk,rhe->khe", chance_low, back_part, preferred_element_type=jnp.float32
        )
        grad_query = lax.dynamic_update_slice_in_dim(grad_query, part_query, first, 1)
        grad_key = lax.dynamic_update_slice_in_dim(grad_key, part_key, first, 1)
        grad_value = lax.dynamic_update_slice_in_dim(grad_value, part_value, first, 1)
        return (grad_query, grad_key, grad_value)

    zero_keys = jnp.zeros((seq_len, HEADS, HD), jnp.float32)
    grad_query, grad_key, grad_value = lax.fori_loop(
        0,
        groups,
        backward_group,
        (jnp.zeros((tokens, HEADS, HD), jnp.float32), zero_keys, zero_keys),
    )
    own_key, own_value = (
        lax.psum_scatter(
            grad_key.reshape(seq_len, width).astype(jnp.bfloat16),
            "ctx",
            scatter_dimension=0,
            tiled=True,
        ).astype(jnp.float32),
        lax.psum_scatter(
            grad_value.reshape(seq_len, width).astype(jnp.bfloat16),
            "ctx",
            scatter_dimension=0,
            tiled=True,
        ).astype(jnp.float32),
    )
    grad_query_low = grad_query.reshape(tokens, width).astype(low_type)
    grad_key_low = own_key.astype(low_type)
    grad_value_low = own_value.astype(low_type)
    grad_mixed = jnp.concatenate([grad_query_low, grad_key_low, grad_value_low], 1)
    grad_bias_query = jnp.sum(grad_query_low.astype(jnp.float32), 0)
    grad_bias_value = jnp.sum(grad_value_low.astype(jnp.float32), 0)
    grad_qkv_term = contract(attn_in, grad_mixed, 0, 0)
    grad_normed_one = contract(grad_mixed, qkv_back, 1, 1)
    norm_one_back = jax.vjp(layer_norm, field, gain_one, shift_one)[1]
    grad_field_norm, grad_gain_one, grad_shift_one = norm_one_back(grad_normed_one)
    in_grad = grad_resid + grad_field_norm
    grad_vec_term = jnp.stack(
        [
            grad_gain_one,
            grad_shift_one,
            grad_gain_two,
            grad_shift_two,
            grad_bias_query,
            grad_bias_value,
            grad_bias_out,
            grad_bias_down,
        ],
        0,
    )
    grad_qkv_own, grad_out_own, grad_vec_own = (
        lax.psum_scatter(grad_qkv_term, ("ctx", "fsdp"), scatter_dimension=0, tiled=True),
        lax.psum_scatter(grad_out_term, ("ctx", "fsdp"), scatter_dimension=0, tiled=True),
        lax.psum_scatter(grad_vec_term, ("ctx", "fsdp"), scatter_dimension=1, tiled=True),
    )
    grads = (grad_qkv_own, grad_out_own, grad_up_own, grad_down_own, grad_bias_own, grad_vec_own)
    local_squares = sum([jnp.sum(item * item) for item in grads])
    grad_norm = jnp.sqrt(lax.psum(local_squares, ("ctx", "fsdp")))
    clip = jnp.minimum(1.0, max_norm / (grad_norm + 1e-06))
    masters = (w_qkv, w_out, w_up, w_down, up_bias, vectors)
    firsts = (first_qkv, first_out, first_up, first_down, first_bias, first_vectors)
    seconds = (second_qkv, second_out, second_up, second_down, second_bias, second_vectors)
    results = []
    for weight, grad, first, second in zip(masters, grads, firsts, seconds):
        update, first_new, second_new = adamw(weight, grad, first, second, clip)
        results = results + [grad, update, first_new, second_new]
    return (
        result.astype(low_type)[None],
        in_grad[None],
        grad_norm,
        results[0],
        results[1],
        results[2],
        results[3],
        results[4],
        results[5],
        results[6],
        results[7],
        results[8],
        results[9],
        results[10],
        results[11],
        results[12],
        results[13],
        results[14],
        results[15],
        results[16],
        results[17],
        results[18],
        results[19],
        results[20],
        results[21],
        results[22],
        results[23],
    )


def exchange(v, axis):
    return lax.ppermute(v, axis, [(0, 1), (1, 0)])


def swap(v, axes):
    return lax.all_to_all(v, axes, 0, 0, tiled=True)


def gather_plane(v):
    mine = swap(jnp.broadcast_to(v[None], (4,) + v.shape), ("y", "x"))
    mine = mine.reshape((4 * v.shape[0],) + v.shape[1:])
    return jnp.concatenate([mine, exchange(mine, "c")], 0)


def scatter_plane(part):
    half = part.shape[0] // 2
    other = exchange(part[half:].astype(jnp.bfloat16), "c")
    mine = (part[:half] + other.astype(jnp.float32)).astype(jnp.bfloat16)
    mine = swap(mine.reshape((4, half // 4) + part.shape[1:]), ("y", "x"))
    return jnp.sum(mine.astype(jnp.float32), 0)


def gather_line(v, n_line, axis):
    me = lax.axis_index(axis)
    parts = [v]
    for k in range(1, n_line):
        parts.append(lax.ppermute(v, axis, [(i, (i + k) % n_line) for i in range(n_line)]))
    out = jnp.zeros((n_line,) + v.shape, v.dtype)
    for k in range(n_line):
        out = lax.dynamic_update_slice_in_dim(out, parts[k][None], (me - k) % n_line, 0)
    return out


def local_split(
    inputs, out_grad, segments, pairs,
    w_qkv, w_out, w_up, w_down, up_bias, vectors,
    first_qkv, first_out, first_up, first_down, first_bias, first_vectors,
    second_qkv, second_out, second_up, second_down, second_bias, second_vectors,
):
    low = jnp.bfloat16
    f32 = jnp.float32
    nz = lax.axis_size("z")
    n_ctx = 2 * nz
    every = ("z", "y", "x", "c")
    ctx = ("z", "y")
    plane = ("y", "x", "c")
    zi, yi, xi, ci = (lax.axis_index(a) for a in every)
    ctx_i = zi * 2 + yi
    tokens, width = inputs.shape[1:]
    block = tokens // 2
    seq_len = tokens * n_ctx
    heads_own = HEADS // n_ctx
    cols = heads_own * HD
    rows = w_qkv.shape[0]
    ff_own = w_down.shape[0]
    scale = HD ** (-0.5)
    field_low = inputs[0]
    field = field_low.astype(f32)

    qkv_parts = w_qkv.astype(low).reshape(rows, 3, n_ctx, cols).transpose(2, 0, 1, 3).reshape(n_ctx, rows, 3 * cols)
    seg_cols = tokens // rows
    extra = jnp.concatenate(
        [
            vectors.astype(low).T,
            segments[0].reshape(rows, seg_cols).astype(low),
            jnp.broadcast_to(pairs[0].astype(low)[None], (rows, 1)),
        ],
        1,
    )
    extra = jnp.pad(extra, ((0, 0), (0, 128 - extra.shape[1])))
    first_send = jnp.concatenate([qkv_parts, jnp.broadcast_to(extra[None], (n_ctx,) + extra.shape)], 2)
    first_got = swap(first_send, ctx)
    meta = first_got[:, :, 3 * cols + 8 :]
    seg_all = meta[:, :, :seg_cols].reshape(seq_len).astype(jnp.int32)
    pair_all = meta[:, 0, seg_cols].astype(jnp.int32)
    first_all = lax.all_gather(first_got, ("x", "c"), axis=0)
    first_all = first_all.transpose(1, 0, 2, 3).reshape(width, 3 * cols + 128)
    qkv_w = first_all[:, : 3 * cols]
    vec = first_all[:, 3 * cols : 3 * cols + 8].T.astype(f32)
    gain_one, shift_one, gain_two, shift_two = (vec[0], vec[1], vec[2], vec[3])
    bias_query, bias_value, bias_out, bias_down = (vec[4], vec[5], vec[6], vec[7])

    line = gather_line(field_low, nz, "z")
    pair_line = exchange(line, "y")
    both = jnp.stack([line, pair_line], 1)
    flip = jnp.stack([pair_line, line], 1)
    seq_low = jnp.where(yi == 0, both, flip).reshape(seq_len, width)
    seq_field = seq_low.astype(f32)

    up_send = w_up.astype(low).reshape(rows, nz, 8, ff_own).transpose(2, 0, 1, 3).reshape(8, rows, nz * ff_own)
    up_part = swap(up_send, plane).reshape(8 * rows, nz * ff_own)
    up_w = gather_line(up_part, nz, "z").reshape(width, nz * ff_own)
    down_w = gather_line(w_down.astype(low), nz, "z").reshape(nz * ff_own, width)
    up_low = gather_line(up_bias.astype(low), nz, "z").reshape(nz * ff_own)
    out_w = lax.all_gather(w_out.astype(low), every, axis=0, tiled=True)
    cot_low = gather_plane(out_grad[0])

    normed_one = layer_norm(seq_field, gain_one, shift_one)
    attn_in = normed_one.astype(low)
    mixed = jnp.dot(attn_in, qkv_w, preferred_element_type=f32)
    own_q = lax.dynamic_slice_in_dim(bias_query, ctx_i * cols, cols, 0)
    own_v = lax.dynamic_slice_in_dim(bias_value, ctx_i * cols, cols, 0)
    query = (mixed[:, :cols] + own_q).astype(low)
    keys = mixed[:, cols : 2 * cols].astype(low)
    values = (mixed[:, 2 * cols :] + own_v).astype(low)
    position = place(pair_all, block, n_ctx)
    seg_key = jnp.take(seg_all, position)
    relative = (position[None, :] - position[:, None]).astype(f32)
    allowed = (seg_key[:, None] == seg_key[None, :]) & (position[None, :] <= position[:, None])
    head_ids = (ctx_i * heads_own + jnp.arange(heads_own)).astype(f32)
    slopes = jnp.exp2(-8.0 * (head_ids + 1.0) / HEADS)
    q_h = query.reshape(seq_len, heads_own, HD)
    k_h = keys.reshape(seq_len, heads_own, HD)
    v_h = values.reshape(seq_len, heads_own, HD)
    raw = jnp.einsum("rhe,khe->hrk", q_h, k_h, preferred_element_type=f32) * scale
    scores = jnp.where(allowed[None], raw + slopes[:, None, None] * relative[None], masked)
    top = jnp.max(scores, -1, keepdims=True)
    expo = jnp.exp(scores - top)
    chance = expo / jnp.sum(expo, -1, keepdims=True)
    chance_low = chance.astype(low)
    attended = jnp.einsum("hrk,khe->rhe", chance_low, v_h, preferred_element_type=f32)
    attended = attended.reshape(n_ctx, tokens, cols).astype(low)
    attended_low = swap(attended, ctx).transpose(1, 0, 2).reshape(tokens, width)

    resid = field + jnp.dot(attended_low, out_w, preferred_element_type=f32) + bias_out
    normed_two = layer_norm(resid, gain_two, shift_two)
    mlp_in = gather_plane(normed_two.astype(low))
    pre = jnp.dot(mlp_in, up_w, preferred_element_type=f32) + up_low.astype(f32)
    hidden = gelu_exact(pre).astype(low)
    grad_hidden = contract(cot_low, down_w, 1, 1)
    gelu_back = jax.vjp(gelu_exact, pre)[1]
    grad_pre = gelu_back(grad_hidden)[0].astype(low)
    grad_normed_two = scatter_plane(contract(grad_pre, up_w, 1, 1))
    result = resid + scatter_plane(jnp.dot(hidden, down_w, preferred_element_type=f32)) + bias_down

    cotangent = out_grad[0].astype(f32)
    grad_bias_down = jnp.sum(cotangent, 0)
    grad_up_bias = jnp.sum(grad_pre.astype(f32), 0)
    up_terms = contract(mlp_in, grad_pre, 0, 0).astype(low).reshape(nz, 8 * rows, nz * ff_own)
    down_terms = contract(hidden, cot_low, 0, 0).astype(low).reshape(nz, ff_own, width)
    up_sum = jnp.sum(swap(up_terms, "z").astype(f32), 0)
    grad_down_own = jnp.sum(swap(down_terms, "z").astype(f32), 0)
    up_got = swap(up_sum.astype(low).reshape(8, rows, nz * ff_own), plane)
    grad_up_own = up_got.reshape(8, rows, nz, ff_own).transpose(1, 2, 0, 3).reshape(rows, nz * 8 * ff_own).astype(f32)

    norm_two_back = jax.vjp(layer_norm, resid, gain_two, shift_two)[1]
    grad_resid_norm, grad_gain_two, grad_shift_two = norm_two_back(grad_normed_two)
    grad_resid = cotangent + grad_resid_norm
    grad_bias_out = jnp.sum(grad_resid, 0)
    resid_low = grad_resid.astype(low)
    back_low = contract(resid_low, out_w, 1, 1).astype(low)
    back_all = swap(back_low.reshape(tokens, n_ctx, cols).transpose(1, 0, 2), ctx)
    back_h = back_all.reshape(seq_len, heads_own, HD)

    out_terms = contract(attended_low, resid_low, 0, 0).reshape(n_ctx, 2, 2, rows, width)
    out_keep = lax.dynamic_index_in_dim(out_terms, ci, 2, keepdims=False)
    out_give = lax.dynamic_index_in_dim(out_terms, 1 - ci, 2, keepdims=False)
    out_pair = out_keep + exchange(out_give.astype(low), "c").astype(f32)
    out_got = swap(out_pair.astype(low).reshape(2 * n_ctx, rows, width), ("z", "y", "x"))
    grad_out_own = jnp.sum(out_got.astype(f32), 0)

    pushed = jnp.einsum("rhe,khe->hrk", back_h, v_h, preferred_element_type=f32)
    centre = jnp.sum(chance * pushed, -1, keepdims=True)
    dscore = (chance * (pushed - centre)).astype(low)
    grad_query = jnp.einsum("hrk,khe->rhe", dscore, k_h, preferred_element_type=f32) * scale
    grad_key = jnp.einsum("hrk,rhe->khe", dscore, q_h, preferred_element_type=f32) * scale
    grad_value = jnp.einsum("hrk,rhe->khe", chance_low, back_h, preferred_element_type=f32)
    grad_mixed = jnp.concatenate([g.reshape(seq_len, cols).astype(low) for g in (grad_query, grad_key, grad_value)], 1)
    mixed_sum = jnp.sum(grad_mixed.astype(f32), 0)
    qkv_terms = contract(attn_in, grad_mixed, 0, 0).astype(low).reshape(4 * n_ctx, rows, 3 * cols)
    qkv_got = swap(qkv_terms, every).astype(f32).reshape(n_ctx, 4, rows, 3, cols)
    grad_qkv_own = jnp.sum(qkv_got, 1).transpose(1, 2, 0, 3).reshape(rows, 3 * width)

    grad_normed_one = contract(grad_mixed, qkv_w, 1, 1)
    norm_seq_back = jax.vjp(lambda g, s: layer_norm(seq_field, g, s), gain_one, shift_one)[1]
    grad_gain_one, grad_shift_one = norm_seq_back(grad_normed_one)
    own_normed_grad = jnp.sum(swap(grad_normed_one.astype(low).reshape(n_ctx, tokens, width), ctx).astype(f32), 0)
    norm_one_back = jax.vjp(lambda v: layer_norm(v, gain_one, shift_one), field)[1]
    in_grad = grad_resid + norm_one_back(own_normed_grad)[0]

    blank = jnp.zeros((width,), f32)
    grad_bias_query = lax.dynamic_update_slice_in_dim(blank, mixed_sum[:cols], ctx_i * cols, 0)
    grad_bias_value = lax.dynamic_update_slice_in_dim(blank, mixed_sum[2 * cols :], ctx_i * cols, 0)
    vec_term = jnp.stack(
        [grad_gain_one, grad_shift_one, grad_gain_two, grad_shift_two,
         grad_bias_query, grad_bias_value, grad_bias_out, grad_bias_down], 0)
    vec_send = vec_term.reshape(8, 4 * n_ctx, rows).transpose(1, 0, 2).reshape(4 * n_ctx, 8 * rows)
    rank = yi * 4 + xi * 2 + ci
    bias_send = jnp.where(
        (jnp.arange(8) == rank)[None, :, None], grad_up_bias.reshape(nz, 1, ff_own), 0.0
    ).reshape(4 * n_ctx, ff_own)
    small = jnp.sum(swap(jnp.concatenate([vec_send, bias_send], 1), every), 0)
    grad_vec_own = small[: 8 * rows].reshape(8, rows)
    grad_bias_own = small[8 * rows :]

    grads = (grad_qkv_own, grad_out_own, grad_up_own, grad_down_own, grad_bias_own, grad_vec_own)
    local_squares = sum([jnp.sum(item * item) for item in grads])
    squares = swap(jnp.broadcast_to(local_squares, (4 * n_ctx, 128)), every)
    grad_norm = jnp.sqrt(jnp.sum(squares[:, 0]))
    clip = jnp.minimum(1.0, max_norm / (grad_norm + 1e-06))
    masters = (w_qkv, w_out, w_up, w_down, up_bias, vectors)
    firsts = (first_qkv, first_out, first_up, first_down, first_bias, first_vectors)
    seconds = (second_qkv, second_out, second_up, second_down, second_bias, second_vectors)
    results = []
    for weight, grad, first, second in zip(masters, grads, firsts, seconds):
        update, first_new, second_new = adamw(weight, grad, first, second, clip)
        results = results + [grad, update, first_new, second_new]
    return (result.astype(low)[None], in_grad[None], grad_norm, *results)


def solution(mesh):
    n_ctx = mesh.shape["ctx"]
    if HEADS % n_ctx == 0 and n_ctx % 2 == 0 and mesh.shape["fsdp"] == 4:
        body = local_split
        ctx, fsdp = ("z", "y"), ("x", "c")
        mesh = Mesh(mesh.devices.reshape(n_ctx // 2, 2, 2, 2), ctx + fsdp)
    else:
        body = local
        ctx, fsdp = ("ctx",), ("fsdp",)
    rows = P(fsdp, ctx, None)
    flat = P(fsdp, ctx)
    mat = P(ctx + fsdp, None)
    vec = P(ctx + fsdp)
    wide = P(None, ctx + fsdp)
    group = (mat, mat, mat, mat, vec, wide)
    outs = ()
    for spec in group:
        outs = outs + (spec,) * 4
    return jax.shard_map(
        body,
        mesh=mesh,
        in_specs=(rows, rows, flat, flat) + group * 3,
        out_specs=(rows, rows, P()) + outs,
        check_vma=False,
    )
```

```python
import functools
import math

import jax
import jax.numpy as jnp
from jax import lax
from jax.experimental import pallas as pl
from jax.experimental.pallas import tpu as pltpu
from jax.sharding import Mesh
from jax.sharding import PartitionSpec as P

HEADS = 16
HD = 64


norm_eps = 1e-05
beta_one = 0.9
beta_two = 0.95
adam_eps = 1e-08
learn_rate = 0.02
weight_decay = 0.1
adam_step = 10
max_norm = 1.0
masked = -1e30
group_heads = 2


def layer_norm(field, gain, shift):
    center = field - jnp.mean(field, -1, keepdims=True)
    spread = jnp.mean(center * center, -1, keepdims=True)
    return center * lax.rsqrt(spread + norm_eps) * gain + shift


def gelu_exact(field):
    return jax.nn.gelu(field, approximate=False)


def contract(left, right, left_dim, right_dim):
    return lax.dot_general(
        left, right, (((left_dim,), (right_dim,)), ((), ())), preferred_element_type=jnp.float32
    )


def place(pair_ids, block, n_ctx):
    blocks = jnp.stack([pair_ids, 2 * n_ctx - 1 - pair_ids], 1).reshape(-1)
    offsets = jnp.arange(block, dtype=jnp.int32)
    return (blocks[:, None] * block + offsets[None, :]).reshape(-1)


def pick(array, first):
    return lax.dynamic_slice_in_dim(array, first, group_heads, 1)


def adamw(weight, grad, first, second, clip):
    clipped = grad * clip
    first_new = beta_one * first + (1.0 - beta_one) * clipped
    second_new = beta_two * second + (1.0 - beta_two) * clipped * clipped
    first_hat = first_new / (1.0 - beta_one**adam_step)
    second_hat = second_new / (1.0 - beta_two**adam_step)
    update = -learn_rate * (first_hat / (jnp.sqrt(second_hat) + adam_eps) + weight_decay * weight)
    return (update, first_new, second_new)


def local(
    inputs,
    out_grad,
    segments,
    pairs,
    w_qkv,
    w_out,
    w_up,
    w_down,
    up_bias,
    vectors,
    first_qkv,
    first_out,
    first_up,
    first_down,
    first_bias,
    first_vectors,
    second_qkv,
    second_out,
    second_up,
    second_down,
    second_bias,
    second_vectors,
):
    low_type = jnp.bfloat16
    n_ctx = lax.axis_size("ctx")
    field = inputs[0].astype(jnp.float32)
    tokens = field.shape[0]
    block = tokens // 2
    width = field.shape[1]
    seq_len = tokens * n_ctx
    scale = HD ** (-0.5)
    groups = HEADS // group_heads
    slope = 2.0 ** (-8.0 * (jnp.arange(HEADS, dtype=jnp.float32) + 1.0) / HEADS)
    qkv_w, out_w, vec_low = (
        lax.all_gather(w_qkv.astype(low_type), ("ctx", "fsdp"), axis=0, tiled=True),
        lax.all_gather(w_out.astype(low_type), ("ctx", "fsdp"), axis=0, tiled=True),
        lax.all_gather(vectors.astype(low_type), ("ctx", "fsdp"), axis=1, tiled=True),
    )
    vec = vec_low.astype(jnp.float32)
    gain_one, shift_one, gain_two, shift_two = (vec[0], vec[1], vec[2], vec[3])
    bias_query, bias_value, bias_out, bias_down = (vec[4], vec[5], vec[6], vec[7])
    normed_one = layer_norm(field, gain_one, shift_one)
    attn_in = normed_one.astype(low_type)
    mixed = jnp.dot(attn_in, qkv_w, preferred_element_type=jnp.float32)
    query = (mixed[:, :width] + bias_query).astype(low_type)
    keys = mixed[:, width : 2 * width].astype(low_type)
    values = (mixed[:, 2 * width :] + bias_value).astype(low_type)
    pair_ids = pairs[0]
    kv_all, pair_all, seg_all = (
        lax.all_gather(jnp.concatenate([keys, values], 1), "ctx", axis=0, tiled=True),
        lax.all_gather(pair_ids, "ctx", axis=0, tiled=True),
        lax.all_gather(segments[0], "ctx", axis=0, tiled=True),
    )
    pos_query = place(pair_ids, block, n_ctx)
    pos_key = place(pair_all, block, n_ctx)
    seg_query = jnp.take(seg_all, pos_query)
    seg_key = jnp.take(seg_all, pos_key)
    relative = (pos_key[None, :] - pos_query[:, None]).astype(jnp.float32)
    allowed = (seg_query[:, None] == seg_key[None, :]) & (pos_key[None, :] <= pos_query[:, None])
    query_heads = query.reshape(tokens, HEADS, HD)
    key_heads = kv_all[:, :width].reshape(seq_len, HEADS, HD)
    value_heads = kv_all[:, width:].reshape(seq_len, HEADS, HD)

    def scores_of(query_part, key_part, first, offsets, visible):
        slopes = lax.dynamic_slice_in_dim(slope, first, group_heads, 0)
        raw = (
            jnp.einsum("rhe,khe->hrk", query_part, key_part, preferred_element_type=jnp.float32)
            * scale
        )
        raw = raw + slopes[:, None, None] * offsets[None]
        return jnp.where(visible[None], raw, masked)

    def forward_group(index, carry):
        attended, log_total = carry
        first = index * group_heads
        scores = scores_of(
            pick(query_heads, first), pick(key_heads, first), first, relative, allowed
        )
        top = jnp.max(scores, -1, keepdims=True)
        expo = jnp.exp(scores - top)
        total = jnp.sum(expo, -1, keepdims=True)
        chance_low = (expo / total).astype(low_type)
        part_out = jnp.einsum(
            "hrk,khe->rhe", chance_low, pick(value_heads, first), preferred_element_type=jnp.float32
        )
        attended = lax.dynamic_update_slice_in_dim(attended, part_out, first, 1)
        log_total = lax.dynamic_update_slice_in_dim(
            log_total, (top + jnp.log(total))[:, :, 0].T, first, 1
        )
        return (attended, log_total)

    attended, log_total = lax.fori_loop(
        0,
        groups,
        forward_group,
        (jnp.zeros((tokens, HEADS, HD), jnp.float32), jnp.zeros((tokens, HEADS), jnp.float32)),
    )
    attended_low = attended.reshape(tokens, width).astype(low_type)
    resid = field + jnp.dot(attended_low, out_w, preferred_element_type=jnp.float32) + bias_out
    normed_two = layer_norm(resid, gain_two, shift_two)
    mlp_in = normed_two.astype(low_type)
    up_w, down_w, up_low = (
        lax.all_gather(w_up.astype(low_type), ("ctx", "fsdp"), axis=0, tiled=True),
        lax.all_gather(w_down.astype(low_type), ("ctx", "fsdp"), axis=0, tiled=True),
        lax.all_gather(up_bias.astype(low_type), ("ctx", "fsdp"), axis=0, tiled=True),
    )
    pre = jnp.dot(mlp_in, up_w, preferred_element_type=jnp.float32) + up_low.astype(jnp.float32)
    hidden = gelu_exact(pre).astype(low_type)
    result = resid + jnp.dot(hidden, down_w, preferred_element_type=jnp.float32) + bias_down
    cotangent_low = out_grad[0]
    cotangent = cotangent_low.astype(jnp.float32)
    up_back, down_back = (
        lax.all_gather(w_up.astype(low_type), ("ctx", "fsdp"), axis=0, tiled=True),
        lax.all_gather(w_down.astype(low_type), ("ctx", "fsdp"), axis=0, tiled=True),
    )
    grad_down_term = contract(hidden, cotangent_low, 0, 0)
    grad_bias_down = jnp.sum(cotangent, 0)
    grad_hidden = contract(cotangent_low, down_back, 1, 1)
    gelu_back = jax.vjp(gelu_exact, pre)[1]
    grad_pre = gelu_back(grad_hidden)[0].astype(low_type)
    grad_up_bias = jnp.sum(grad_pre.astype(jnp.float32), 0)
    grad_up_term = contract(mlp_in, grad_pre, 0, 0)
    grad_normed_two = contract(grad_pre, up_back, 1, 1)
    norm_two_back = jax.vjp(layer_norm, resid, gain_two, shift_two)[1]
    grad_resid_norm, grad_gain_two, grad_shift_two = norm_two_back(grad_normed_two)
    grad_resid = cotangent + grad_resid_norm
    grad_up_own, grad_down_own, grad_bias_own = (
        lax.psum_scatter(grad_up_term, ("ctx", "fsdp"), scatter_dimension=0, tiled=True),
        lax.psum_scatter(grad_down_term, ("ctx", "fsdp"), scatter_dimension=0, tiled=True),
        lax.psum_scatter(grad_up_bias, ("ctx", "fsdp"), scatter_dimension=0, tiled=True),
    )
    qkv_back, out_back = (
        lax.all_gather(w_qkv.astype(low_type), ("ctx", "fsdp"), axis=0, tiled=True),
        lax.all_gather(w_out.astype(low_type), ("ctx", "fsdp"), axis=0, tiled=True),
    )
    grad_bias_out = jnp.sum(grad_resid, 0)
    resid_low = grad_resid.astype(low_type)
    grad_out_term = contract(attended_low, resid_low, 0, 0)
    back_low = contract(resid_low, out_back, 1, 1).astype(low_type)
    back_heads = back_low.reshape(tokens, HEADS, HD)

    def backward_group(index, carry):
        grad_query, grad_key, grad_value = carry
        first = index * group_heads
        query_part = pick(query_heads, first)
        key_part = pick(key_heads, first)
        value_part = pick(value_heads, first)
        back_part = pick(back_heads, first)
        scores = scores_of(query_part, key_part, first, relative, allowed)
        logsum = lax.dynamic_slice_in_dim(log_total, first, group_heads, 1).T
        chance = jnp.exp(scores - logsum[:, :, None])
        pushed = jnp.einsum(
            "rhe,khe->hrk", back_part, value_part, preferred_element_type=jnp.float32
        )
        centre = jnp.sum(chance * pushed, -1, keepdims=True)
        dscore = (chance * (pushed - centre)).astype(low_type)
        chance_low = chance.astype(low_type)
        part_query = (
            jnp.einsum("hrk,khe->rhe", dscore, key_part, preferred_element_type=jnp.float32) * scale
        )
        part_key = (
            jnp.einsum("hrk,rhe->khe", dscore, query_part, preferred_element_type=jnp.float32)
            * scale
        )
        part_value = jnp.einsum(
            "hrk,rhe->khe", chance_low, back_part, preferred_element_type=jnp.float32
        )
        grad_query = lax.dynamic_update_slice_in_dim(grad_query, part_query, first, 1)
        grad_key = lax.dynamic_update_slice_in_dim(grad_key, part_key, first, 1)
        grad_value = lax.dynamic_update_slice_in_dim(grad_value, part_value, first, 1)
        return (grad_query, grad_key, grad_value)

    zero_keys = jnp.zeros((seq_len, HEADS, HD), jnp.float32)
    grad_query, grad_key, grad_value = lax.fori_loop(
        0,
        groups,
        backward_group,
        (jnp.zeros((tokens, HEADS, HD), jnp.float32), zero_keys, zero_keys),
    )
    own_key, own_value = (
        lax.psum_scatter(
            grad_key.reshape(seq_len, width).astype(jnp.bfloat16),
            "ctx",
            scatter_dimension=0,
            tiled=True,
        ).astype(jnp.float32),
        lax.psum_scatter(
            grad_value.reshape(seq_len, width).astype(jnp.bfloat16),
            "ctx",
            scatter_dimension=0,
            tiled=True,
        ).astype(jnp.float32),
    )
    grad_query_low = grad_query.reshape(tokens, width).astype(low_type)
    grad_key_low = own_key.astype(low_type)
    grad_value_low = own_value.astype(low_type)
    grad_mixed = jnp.concatenate([grad_query_low, grad_key_low, grad_value_low], 1)
    grad_bias_query = jnp.sum(grad_query_low.astype(jnp.float32), 0)
    grad_bias_value = jnp.sum(grad_value_low.astype(jnp.float32), 0)
    grad_qkv_term = contract(attn_in, grad_mixed, 0, 0)
    grad_normed_one = contract(grad_mixed, qkv_back, 1, 1)
    norm_one_back = jax.vjp(layer_norm, field, gain_one, shift_one)[1]
    grad_field_norm, grad_gain_one, grad_shift_one = norm_one_back(grad_normed_one)
    in_grad = grad_resid + grad_field_norm
    grad_vec_term = jnp.stack(
        [
            grad_gain_one,
            grad_shift_one,
            grad_gain_two,
            grad_shift_two,
            grad_bias_query,
            grad_bias_value,
            grad_bias_out,
            grad_bias_down,
        ],
        0,
    )
    grad_qkv_own, grad_out_own, grad_vec_own = (
        lax.psum_scatter(grad_qkv_term, ("ctx", "fsdp"), scatter_dimension=0, tiled=True),
        lax.psum_scatter(grad_out_term, ("ctx", "fsdp"), scatter_dimension=0, tiled=True),
        lax.psum_scatter(grad_vec_term, ("ctx", "fsdp"), scatter_dimension=1, tiled=True),
    )
    grads = (grad_qkv_own, grad_out_own, grad_up_own, grad_down_own, grad_bias_own, grad_vec_own)
    local_squares = sum([jnp.sum(item * item) for item in grads])
    grad_norm = jnp.sqrt(lax.psum(local_squares, ("ctx", "fsdp")))
    clip = jnp.minimum(1.0, max_norm / (grad_norm + 1e-06))
    masters = (w_qkv, w_out, w_up, w_down, up_bias, vectors)
    firsts = (first_qkv, first_out, first_up, first_down, first_bias, first_vectors)
    seconds = (second_qkv, second_out, second_up, second_down, second_bias, second_vectors)
    results = []
    for weight, grad, first, second in zip(masters, grads, firsts, seconds):
        update, first_new, second_new = adamw(weight, grad, first, second, clip)
        results = results + [grad, update, first_new, second_new]
    return (
        result.astype(low_type)[None],
        in_grad[None],
        grad_norm,
        results[0],
        results[1],
        results[2],
        results[3],
        results[4],
        results[5],
        results[6],
        results[7],
        results[8],
        results[9],
        results[10],
        results[11],
        results[12],
        results[13],
        results[14],
        results[15],
        results[16],
        results[17],
        results[18],
        results[19],
        results[20],
        results[21],
        results[22],
        results[23],
    )


def exchange(v, axis):
    return lax.ppermute(v, axis, [(0, 1), (1, 0)])


def shift(v, axis, n_line, k):
    return lax.ppermute(v, axis, [(i, (i - k) % n_line) for i in range(n_line)])


def swap(v, axes):
    return lax.all_to_all(v, axes, 0, 0, tiled=True)


def gate(*values):
    return lax.optimization_barrier(values)


def after(v, *others):
    return lax.optimization_barrier((v,) + others)[0]


def order_two(own, other, axis, dim):
    first = lax.axis_index(axis) == 0
    return jnp.stack([jnp.where(first, own, other), jnp.where(first, other, own)], dim)


def split_two(part, axis, dim):
    me = lax.axis_index(axis)
    keep = lax.dynamic_index_in_dim(part, me, dim, keepdims=False)
    return keep, lax.dynamic_index_in_dim(part, 1 - me, dim, keepdims=False)


def add_low(keep, got):
    return (keep.astype(jnp.float32) + got.astype(jnp.float32)).astype(jnp.bfloat16)


def line_gives(part, axis, n_line):
    me = lax.axis_index(axis)
    blocks = [lax.dynamic_index_in_dim(part, (me + k) % n_line, 0, keepdims=False) for k in range(n_line)]
    return blocks[0], [shift(blocks[k], axis, n_line, -k) for k in range(1, n_line)]


def line_order(parts, axis):
    n_line = len(parts)
    first = (n_line - lax.axis_index(axis)) % n_line
    return lax.dynamic_slice_in_dim(jnp.concatenate([jnp.stack(parts)] * 2, 0), first, n_line, 0)


def lanes_of(head, shape):
    return lax.broadcasted_iota(jnp.int32, shape, 1) // HD == head


def head_parts(query, keys, slope, head):
    seq = keys.shape[0]
    lane = lax.broadcasted_iota(jnp.int32, keys.shape, 1)
    own = lane // HD == head
    spot = lane - (1 - head) * HD
    bias = lax.broadcasted_iota(jnp.int32, (seq, 1), 0).astype(jnp.float32) * (slope * HD**0.5)
    high = bias.astype(jnp.bfloat16)
    rest = bias - high.astype(jnp.float32)
    middle = rest.astype(jnp.bfloat16)
    small = (rest - middle.astype(jnp.float32)).astype(jnp.bfloat16)
    zero = jnp.zeros_like(keys)
    extra = jnp.where(spot == 0, high, jnp.where(spot == 1, middle, jnp.where(spot == 2, small, zero)))
    ones = jnp.where((spot >= 0) & (spot <= 2), jnp.ones_like(keys), zero)
    return jnp.where(own, query, ones), jnp.where(own, keys, extra)


def visible(start, tile, at, size):
    key = lax.broadcasted_iota(jnp.int32, (size, tile), 0)
    seen = key >= start
    return seen & (key <= lax.broadcasted_iota(jnp.int32, (size, tile), 1) + at)


def forward_kernel(n_refs, meta, slopes, *refs):
    pieces = refs[n_refs : n_refs + 3]
    start_ref = refs[n_refs + 3]
    att_ref, att_t, qkv_ref, lse_ref, normed, x_ref, w_ref, vec_ref, extra = refs[n_refs + 4 :]
    blocks = []
    for ref in refs[:n_refs]:
        blocks = blocks + ([ref] if len(ref.shape) == 2 else [ref.at[k] for k in range(ref.shape[0])])
    n_blocks = len(blocks)
    f32, low = jnp.float32, jnp.bfloat16
    n_ctx, rows, _ = pieces[0].shape
    tokens, width = blocks[0].shape
    half = tokens // 2
    seq = tokens * n_blocks
    cols = qkv_ref.shape[1] // 3
    spans = 2 * n_blocks
    for c in range(n_ctx):
        for p in range(4):
            piece = pieces[p][c] if p < 2 else pieces[2][p - 2, c]
            to = pl.ds(pl.multiple_of(c * 4 * rows + meta[2 * spans + p] * rows, rows), rows)
            w_ref[to, :] = piece[:, : 3 * cols]
            extra[to, :] = piece[:, 3 * cols :]
    pick_rows = (
        lax.broadcasted_iota(jnp.int32, (8, 128), 0) == lax.broadcasted_iota(jnp.int32, (8, 128), 1)
    ).astype(low)
    vec = contract(pick_rows, extra[...], 1, 1)
    vec_ref[...] = vec
    gain, move = vec[0:1], vec[1:2]
    for j in range(spans):
        part = blocks[j // 2][(j % 2) * half : (j % 2 + 1) * half, :]
        to = pl.ds(pl.multiple_of(meta[j] * half, half), half)
        x_ref[to, :] = part
        normed[to, :] = layer_norm(part.astype(f32), gain, move).astype(low)
    at = pl.ds(pl.multiple_of(meta[2 * spans + 4] * cols, cols), cols)
    bias_q, bias_v = vec_ref[4:5, at], vec_ref[5:6, at]
    tile = min(256, seq)
    for t in range(seq // tile):
        span = pl.ds(t * tile, tile)
        mixed = jnp.dot(normed[span, :], w_ref[...], preferred_element_type=f32)
        qkv_ref[span, :cols] = (mixed[:, :cols] + bias_q).astype(low)
        qkv_ref[span, cols : 2 * cols] = mixed[:, cols : 2 * cols].astype(low)
        qkv_ref[span, 2 * cols :] = (mixed[:, 2 * cols :] + bias_v).astype(low)
    factor = HD**-0.5 * 1.4426950408889634
    query, keys, values = qkv_ref[:, :cols], qkv_ref[:, cols : 2 * cols], qkv_ref[:, 2 * cols :]
    lse_ref[...] = jnp.zeros_like(lse_ref)
    for h in range(cols // HD):
        q_h, k_h = head_parts(query, keys, slopes[h], h)
        v_h = jnp.where(lanes_of(h, values.shape), values, jnp.zeros_like(values))
        for t in range(seq // tile):
            size = (t + 1) * tile
            span = slice(t * tile, (t + 1) * tile)
            score = contract(k_h[:size], q_h[span], 1, 1) * factor
            score = jnp.where(visible(start_ref[:, span], tile, t * tile, size), score, masked)
            top = jnp.max(score, 0, keepdims=True)
            expo = jnp.exp2(score - top)
            total = jnp.sum(expo, 0, keepdims=True)
            lse_ref[h : h + 1, span] = top + jnp.log2(total)
            part = contract(v_h[:size], expo.astype(low), 0, 0) / total
            att_t[:, span] = part if h == 0 else att_t[:, span] + part
    for t in range(seq // tile):
        span = slice(t * tile, (t + 1) * tile)
        x_tile = att_t[:, span].T.astype(low)
        for u in range(tile // half):
            b = t * (tile // half) + u
            to = meta[spans + b]
            att_ref[pl.ds(pl.multiple_of(to * half, half), half), :] = x_tile[u * half : (u + 1) * half]


def pack_kernel(pairs, w_qkv, vectors, segments, up_bias, w_up, w_down, w_out, first_ref, up_ref, down_ref, out_ref):
    low, f32 = jnp.bfloat16, jnp.float32
    n_ctx, rows, wide = first_ref.shape
    cols = (wide - 128) // 3
    width = n_ctx * cols
    row = lax.broadcasted_iota(jnp.int32, (rows, 128), 0)
    lane = lax.broadcasted_iota(jnp.int32, (rows, 128), 1)
    one_hot = lax.broadcasted_iota(jnp.int32, (8, 128), 0) == lax.broadcasted_iota(jnp.int32, (8, 128), 1)
    columns = contract(vectors[...].astype(low), one_hot.astype(low), 0, 0)
    seg, bias = segments[...].astype(f32), up_bias[...]
    lines = [pltpu.roll(seg, 64, 1), seg, pltpu.roll(bias, 64, 1), bias]
    extra = jnp.where(lane < 8, columns, 0.0)
    for k in range(4):
        extra = jnp.where((row == k) & (lane >= 64), lines[k], extra)
    extra = jnp.where((row == 4) & (lane >= 64), pairs[0, 0].astype(f32), extra).astype(low)
    for c in range(n_ctx):
        for k in range(3):
            first_ref[c, :, k * cols : (k + 1) * cols] = w_qkv[:, k * width + c * cols : k * width + (c + 1) * cols].astype(low)
        first_ref[c, :, 3 * cols :] = extra
    n_plane, _, ff = up_ref.shape
    own = ff // (n_ctx // 2)
    for r in range(n_plane):
        for k in range(n_ctx // 2):
            up_ref[r, :, k * own : (k + 1) * own] = w_up[:, (k * n_plane + r) * own : (k * n_plane + r + 1) * own].astype(low)
    for k in range(down_ref.shape[0]):
        down_ref[k] = w_down[:, k * ff : (k + 1) * ff].astype(low)
    out_ref[...] = w_out[...].astype(low)


def spot_of(table, spans, z, y, x, c):
    n_line = spans // 4
    at = 2 * spans + 5
    return (
        lax.rem(z + n_line - table[at], n_line),
        lax.rem(y + table[at + 1], 2),
        lax.rem(x + table[at + 2], 2),
        lax.rem(c + table[at + 3], 2),
    )


def project_kernel(table, att, own_ref, other_ref, field, vec, resid_ref, mlp_ref, w_ref):
    low, f32 = jnp.bfloat16, jnp.float32
    n_ctx, tokens, cols = att.shape
    rows = own_ref.shape[2]
    n_line = own_ref.shape[1]
    at = 4 * n_ctx + 5
    zi, yi, xi, ci = (table[at + k] for k in range(4))
    for c, ref in enumerate((own_ref, other_ref)):
        for q in range(4):
            for k in range(n_line):
                z = lax.rem(zi + k, n_line)
                y = lax.rem(yi + q % 2, 2)
                x = lax.rem(xi + q // 2, 2)
                to = ((z * 2 + y) * 4 + x * 2 + lax.rem(ci + c, 2)) * rows
                w_ref[pl.ds(pl.multiple_of(to, rows), rows), :] = ref[q, k]
    heads = jnp.concatenate([att[c] for c in range(n_ctx)], 1)
    moved = jnp.dot(heads, w_ref[...], preferred_element_type=f32)
    resid = field[...].astype(f32) + moved + vec[6:7]
    resid_ref[...] = resid
    mlp_ref[...] = layer_norm(resid, vec[2:3], vec[3:4]).astype(low)


def down_of(ff_all, down):
    n_line, own = ff_all.shape[0], down.shape[0] // ff_all.shape[0]
    ff = down.shape[0]
    up_rows = ff_all.shape[1] - down.shape[1] * own // ff
    for k in range(n_line):
        for h in range(down.shape[1] // ff):
            down[k * own : (k + 1) * own, h * ff : (h + 1) * ff] = ff_all[k, up_rows + h * own : up_rows + (h + 1) * own, :]


def feed_kernel(*refs):
    low, f32 = jnp.bfloat16, jnp.float32
    m_own, m_y, m_x, m_d0, m_d1, m_c, m_cyx, m_cd, cot_own, cot_other, ff_all, bias = refs[:12]
    keep_ref, give_ref, hidden_ref, pre_ref, mlp_ref, down, up = refs[12:]
    tokens, width = m_own.shape
    half = tokens // 2
    ff = hidden_ref.shape[1]
    n_line = ff_all.shape[0]
    up_rows = width // n_line
    for k in range(n_line):
        up[k * up_rows : (k + 1) * up_rows, :] = ff_all[k, :up_rows, :]
    down_of(ff_all, down)
    blocks = (m_own[...], m_y[...], m_x[...], None, m_c[...], m_cyx[0], m_cyx[1])
    for b, block in enumerate(blocks):
        if block is not None:
            mlp_ref[b * tokens : (b + 1) * tokens, :] = block
    mlp_ref[3 * tokens : 3 * tokens + half, :] = m_d0[...]
    mlp_ref[3 * tokens + half : 4 * tokens, :] = m_d1[...]
    mlp_ref[7 * tokens : 7 * tokens + half, :] = m_cd[0]
    mlp_ref[7 * tokens + half : 8 * tokens, :] = m_cd[1]
    for t in range(4):
        span = slice(2 * t * tokens, 2 * (t + 1) * tokens)
        pre = jnp.dot(mlp_ref[span, :], up[...], preferred_element_type=f32) + bias[...]
        cdf = 0.5 * (1.0 + lax.erf(pre * 0.7071067811865476))
        pdf = jnp.exp(-0.5 * pre * pre) * 0.3989422804014327
        hidden_ref[span, :] = (pre * cdf).astype(low)
        cot_ref = cot_own if t < 2 else cot_other
        cot = cot_ref[2 * (t % 2) : 2 * (t % 2) + 2].reshape(2 * tokens, width)
        grad = (contract(cot, down[...], 1, 1) * (cdf + pre * pdf)).astype(low)
        pre_ref[span, :] = grad
        part = contract(grad, up[...], 1, 1).astype(low).reshape(2, tokens, width)
        to = keep_ref if t < 2 else give_ref
        to[2 * (t % 2) : 2 * (t % 2) + 2] = part


def feed_grad_kernel(mlp_ref, pre_ref, hidden_ref, cot_own, cot_other, ff_all, terms_ref, keep_ref, give_ref, down):
    low, f32 = jnp.bfloat16, jnp.float32
    seq, width = mlp_ref.shape
    ff = pre_ref.shape[1]
    n_line = ff_all.shape[0]
    own, up_rows, tokens = ff // n_line, width // n_line, seq // 8
    n_half = width // ff
    down_of(ff_all, down)
    for k in range(n_line):
        up = contract(mlp_ref[:, k * up_rows : (k + 1) * up_rows], pre_ref[...], 0, 0)
        terms_ref[k, :up_rows, :] = up.astype(low)
        for h in range(n_half):
            part = slice(k * own, (k + 1) * own)
            cut = slice(h * ff, (h + 1) * ff)
            total = contract(hidden_ref[: seq // 2, part], cot_own[:, :, cut].reshape(seq // 2, ff), 0, 0)
            total = total + contract(hidden_ref[seq // 2 :, part], cot_other[:, :, cut].reshape(seq // 2, ff), 0, 0)
            terms_ref[k, up_rows + h * own : up_rows + (h + 1) * own, :] = total.astype(low)
    sums = jnp.sum(pre_ref[...].astype(f32), 0, keepdims=True)
    pad = terms_ref.shape[1] - up_rows - n_half * own
    for k in range(n_line):
        line = jnp.concatenate([sums[:, k * own : (k + 1) * own], jnp.zeros((1, ff - own), f32)], 1)
        terms_ref[k, up_rows + n_half * own :, :] = jnp.broadcast_to(line, (pad, ff)).astype(low)
    for t in range(4):
        span = slice(2 * t * tokens, 2 * (t + 1) * tokens)
        part = jnp.dot(hidden_ref[span, :], down[...], preferred_element_type=f32)
        to = keep_ref if t < 2 else give_ref
        to[2 * (t % 2) : 2 * (t % 2) + 2] = part.astype(low).reshape(2, tokens, width)


def norm_back_kernel(own, got_x, got_y, resid_ref, cot_ref, vec, w_ref, grad_ref, low_ref, back_ref, sums_ref):
    low, f32 = jnp.bfloat16, jnp.float32
    grad = own[...].astype(f32) + got_x[...].astype(f32) + got_y[...].astype(f32)
    resid = resid_ref[...]
    center = resid - jnp.mean(resid, -1, keepdims=True)
    sharp = lax.rsqrt(jnp.mean(center * center, -1, keepdims=True) + norm_eps)
    unit = center * sharp
    scaled = grad * vec[2:3]
    inner = scaled - jnp.mean(scaled, -1, keepdims=True) - unit * jnp.mean(scaled * unit, -1, keepdims=True)
    cot = cot_ref[...].astype(f32)
    total = cot + inner * sharp
    grad_ref[...] = total
    rounded = total.astype(low)
    low_ref[...] = rounded
    back = contract(rounded, w_ref[...], 1, 1).astype(low)
    n_ctx, _, cols = back_ref.shape
    for c in range(n_ctx):
        back_ref[c] = back[:, c * cols : (c + 1) * cols]
    row = lax.broadcasted_iota(jnp.int32, sums_ref.shape, 0)
    sums = jnp.where(row == 2, jnp.sum(grad * unit, 0, keepdims=True), 0.0)
    sums = jnp.where(row == 3, jnp.sum(grad, 0, keepdims=True), sums)
    sums = jnp.where(row == 6, jnp.sum(total, 0, keepdims=True), sums)
    sums_ref[...] = jnp.where(row == 7, jnp.sum(cot, 0, keepdims=True), sums)


def out_grad_kernel(table, att, low_ref, terms_ref):
    n_ctx = att.shape[0]
    rows = terms_ref.shape[4]
    for c in range(n_ctx):
        part = contract(att[c], low_ref[...], 0, 0).astype(jnp.bfloat16)
        for f in range(4):
            dz, dy, dx, dc = spot_of(table, 2 * n_ctx, c // 2, c % 2, f // 2, f % 2)
            terms_ref[dc, dx, dy, dz] = part[f * rows : (f + 1) * rows]


def backward_kernel(table, slopes, back_ref, qkv_ref, att_t, lse_ref, start_ref, normed, mixed_ref, sums_ref, terms_ref, back, d_key, d_value):
    f32, low = jnp.float32, jnp.bfloat16
    seq, cols = back_ref.shape
    n_ctx, rows = terms_ref.shape[2:4]
    spans = 2 * n_ctx
    half = seq // spans
    for b in range(spans):
        back[b * half : (b + 1) * half, :] = back_ref[pl.ds(pl.multiple_of(table[spans + b] * half, half), half), :]
    factor = HD**-0.5 * 1.4426950408889634
    query, keys, values = qkv_ref[:, :cols], qkv_ref[:, cols : 2 * cols], qkv_ref[:, 2 * cols :]
    grads = back[...]
    product = att_t[...] * grads.astype(f32).T
    tile = min(256, seq)
    d_query = [None] * (seq // tile)
    for h in range(cols // HD):
        q_h, k_h = head_parts(query, keys, slopes[h], h)
        own = lanes_of(h, values.shape)
        zero = jnp.zeros_like(values)
        v_h, g_h = jnp.where(own, values, zero), jnp.where(own, grads, zero)
        qq_h, kk_h = jnp.where(own, query, zero), jnp.where(own, keys, zero)
        delta = jnp.sum(product[h * HD : (h + 1) * HD], 0, keepdims=True)
        for t in reversed(range(seq // tile)):
            size = (t + 1) * tile
            span = slice(t * tile, (t + 1) * tile)
            score = contract(k_h[:size], q_h[span], 1, 1) * factor
            score = jnp.where(visible(start_ref[:, span], tile, t * tile, size), score, masked)
            chance = jnp.exp2(score - lse_ref[h : h + 1, span])
            pushed = contract(v_h[:size], g_h[span], 1, 1)
            dscore = (chance * (pushed - delta[:, span])).astype(low)
            part_v = jnp.dot(chance.astype(low), g_h[span], preferred_element_type=f32)
            part_k = jnp.dot(dscore, qq_h[span], preferred_element_type=f32)
            if h == 0 and t == seq // tile - 1:
                d_value[...] = part_v
                d_key[...] = part_k
            else:
                d_value[:size, :] += part_v
                d_key[:size, :] += part_k
            part_q = contract(kk_h[:size], dscore, 0, 0)
            d_query[t] = part_q if h == 0 else d_query[t] + part_q
    scale = HD**-0.5
    for t in range(seq // tile):
        mixed_ref[t * tile : (t + 1) * tile, :cols] = (d_query[t] * scale).T.astype(low)
    mixed_ref[:, cols : 2 * cols] = (d_key[...] * scale).astype(low)
    mixed_ref[:, 2 * cols :] = d_value[...].astype(low)
    mixed = mixed_ref[...]
    sums_ref[...] = jnp.broadcast_to(jnp.sum(mixed.astype(f32), 0, keepdims=True), sums_ref.shape)
    terms = contract(mixed, normed[...], 0, 0)
    for c in range(n_ctx):
        part = terms[:, c * 4 * rows : (c + 1) * 4 * rows].T.astype(low)
        for f in range(4):
            _, _, dx, dc = spot_of(table, spans, 0, 0, f // 2, f % 2)
            terms_ref[dc, dx, c] = part[f * rows : (f + 1) * rows]


def first_grad_kernel(table, mixed_ref, w_ref, x_ref, mixed_sums, other_sums, out_ref, send_ref):
    f32, low = jnp.float32, jnp.bfloat16
    seq, width = x_ref.shape
    _, _, n_line, half, _ = out_ref.shape
    spans = 4 * n_line
    tile = min(256, seq)
    gain_sum = jnp.zeros((1, width), f32)
    shift_sum = jnp.zeros((1, width), f32)
    for t in range(seq // tile):
        grad = contract(mixed_ref[t * tile : (t + 1) * tile, :], w_ref[...], 1, 1)
        field = x_ref[t * tile : (t + 1) * tile, :].astype(f32)
        center = field - jnp.mean(field, -1, keepdims=True)
        unit = center * lax.rsqrt(jnp.mean(center * center, -1, keepdims=True) + norm_eps)
        gain_sum = gain_sum + jnp.sum(grad * unit, 0, keepdims=True)
        shift_sum = shift_sum + jnp.sum(grad, 0, keepdims=True)
        grad = grad.astype(low)
        for u in range(tile // half):
            to = table[spans + t * (tile // half) + u]
            dz, dy, _, _ = spot_of(table, spans, lax.div(to, 4), lax.rem(lax.div(to, 2), 2), 0, 0)
            out_ref[lax.rem(to, 2), dy, dz] = grad[u * half : (u + 1) * half]
    row = lax.broadcasted_iota(jnp.int32, (8, width), 0)
    sums = jnp.where(row == 0, gain_sum, jnp.where(row == 1, shift_sum, other_sums[...]))
    n_ctx = spans // 2
    cols = width // n_ctx
    here = table[2 * spans + 4]
    small = lax.broadcasted_iota(jnp.int32, (8, cols), 0)
    bias = jnp.where(small == 4, mixed_sums[:, :cols], jnp.where(small == 5, mixed_sums[:, 2 * cols :], 0.0))
    for c in range(n_ctx):
        block = sums[:, c * cols : (c + 1) * cols] + jnp.where(here == c, bias, 0.0)
        for f in range(4):
            send_ref[c * 4 + f] = block


def gather_grad_kernel(table, ff_ref, own_out, other_out, small_ref, square_ref, up_ref, out_ref, vec_ref):
    f32 = jnp.float32
    _, _, rows, ff = up_ref.shape
    n_ctx = small_ref.shape[0] // 4
    at = 4 * n_ctx + 5
    for r in range(8):
        _, dy, dx, dc = spot_of(table, 2 * n_ctx, 0, r // 4, (r // 2) % 2, r % 2)
        up_ref[dc, dx * 2 + dy] = ff_ref[r * rows : (r + 1) * rows, :]
    out = own_out[...].astype(f32)
    for k in range(other_out.shape[0]):
        out = out + other_out[k].astype(f32)
    out_ref[...] = out
    small = jnp.sum(small_ref[...], 0)
    mine = table[at + 2] * 2 + table[at + 3]
    picked = jnp.zeros((8, rows), f32)
    for f in range(4):
        picked = picked + jnp.where(mine == f, small[:, f * rows : (f + 1) * rows], 0.0)
    vec_ref[...] = picked
    n_ff = ff_ref.shape[0] - 16
    total = jnp.sum(jnp.square(ff_ref[:n_ff, :].astype(f32)), 0, keepdims=True)
    own = rows * 4
    bias = ff_ref[n_ff:, :own].astype(f32)[0:1]
    squared = jnp.sum(total, keepdims=True) + jnp.sum(jnp.square(bias), keepdims=True)
    squared = squared + jnp.sum(jnp.square(picked), keepdims=True) + jnp.sum(jnp.square(out), keepdims=True)
    square_ref[...] = jnp.broadcast_to(squared, square_ref.shape)


def qkv_square_kernel(qkv_ref, square_ref, out_ref):
    squared = jnp.sum(jnp.square(qkv_ref[...].astype(jnp.float32)), 0)
    out_ref[...] = square_ref[...] + jnp.sum(squared, keepdims=True)


def adam_kernel(*refs):
    f32 = jnp.float32
    table, squares, qkv_ref, out_ref, up_ref, ff_ref, vec_ref = refs[:7]
    masters, firsts, seconds = refs[7:13], refs[13:19], refs[19:25]
    norm_ref, results = refs[25], refs[26:]
    norm = jnp.sqrt(jnp.sum(jnp.sum(squares[...], 0, keepdims=True)[:, 0:1], keepdims=True))
    norm_ref[...] = norm
    clip = jnp.minimum(1.0, max_norm / (norm + 1e-06))
    n_ctx, rows, wide = qkv_ref.shape
    cols = wide // 3
    width = n_ctx * cols
    ff = up_ref.shape[4]
    n_line = n_ctx // 2
    at = 4 * n_ctx + 5
    own = ff // n_line
    n_ff = 8 * rows

    def put(item, spot, grad):
        new = adamw(masters[item][spot], grad, firsts[item][spot], seconds[item][spot], clip)
        for k, value in enumerate((grad,) + new):
            results[4 * item + k][spot] = value

    for c in range(n_ctx):
        for k in range(3):
            spot = (slice(None), slice(k * width + c * cols, k * width + (c + 1) * cols))
            put(0, spot, qkv_ref[c, :, k * cols : (k + 1) * cols].astype(f32))
    put(1, (slice(None), slice(None)), out_ref[...])
    for y in range(2):
        for x in range(2):
            for c in range(2):
                first = lax.rem(table[at + 1] + y, 2) * 4 + lax.rem(table[at + 2] + x, 2) * 2 + lax.rem(table[at + 3] + c, 2)
                for k in range(n_line):
                    spot = (slice(None), pl.ds(pl.multiple_of((k * 8 + first) * own, own), own))
                    put(2, spot, up_ref[y, x, c, :, k * own : (k + 1) * own].astype(f32))
    for h in range(width // ff):
        spot = (slice(None), slice(h * ff, (h + 1) * ff))
        put(3, spot, ff_ref[n_ff + h * own : n_ff + (h + 1) * own, :].astype(f32))
    n_down = n_ff + width // ff * own
    put(4, (slice(None), slice(None)), ff_ref[n_down:, :own].astype(f32)[0:1])
    put(5, (slice(None), slice(None)), vec_ref[...])


in_smem = pl.BlockSpec(memory_space=pltpu.SMEM)
in_vmem = pl.BlockSpec(memory_space=pltpu.VMEM)


def call(kernel, n_scalar, args, shapes, scratch=(), cost=1):
    return pl.pallas_call(
        kernel,
        out_shape=[jax.ShapeDtypeStruct(s, d) for s, d in shapes],
        in_specs=[in_smem] * n_scalar + [in_vmem] * (len(args) - n_scalar),
        out_specs=[in_vmem] * len(shapes),
        scratch_shapes=[pltpu.VMEM(s, d) for s, d in scratch],
        compiler_params=pltpu.CompilerParams(vmem_limit_bytes=48 * 1024 * 1024),
        cost_estimate=pl.CostEstimate(flops=cost, bytes_accessed=cost, transcendentals=0),
    )(*args)


def attend_forward(table, slopes, blocks, pieces, start, cols):
    tokens, width = blocks[0].shape
    n_blocks = sum([1 if b.ndim == 2 else b.shape[0] for b in blocks])
    seq = tokens * n_blocks
    f32, low = jnp.float32, jnp.bfloat16
    shapes = [
        ((seq, cols), low), ((cols, seq), f32), ((seq, 3 * cols), low), ((8, seq), f32),
        ((seq, width), low), ((seq, width), low), ((width, 3 * cols), low), ((8, width), f32),
    ]
    args = [table, slopes] + list(blocks) + list(pieces) + [start]
    return call(functools.partial(forward_kernel, len(blocks)), 2, args, shapes, [((width, 128), low)])


def local_split(
    inputs, out_grad, segments, pairs,
    w_qkv, w_out, w_up, w_down, up_bias, vectors,
    first_qkv, first_out, first_up, first_down, first_bias, first_vectors,
    second_qkv, second_out, second_up, second_down, second_bias, second_vectors,
):
    low = jnp.bfloat16
    f32 = jnp.float32
    nz = lax.axis_size("z")
    n_ctx = 2 * nz
    every = ("z", "y", "x", "c")
    ctx = ("z", "y")
    plane = ("y", "x", "c")
    zi, yi, xi, ci = (lax.axis_index(a) for a in every)
    ctx_i = zi * 2 + yi
    tokens, width = inputs.shape[1:]
    half = tokens // 2
    seq_len = tokens * n_ctx
    heads_own = HEADS // n_ctx
    cols = heads_own * HD
    rows = w_qkv.shape[0]
    ff_own = w_down.shape[0]
    ff = nz * ff_own
    n_half = width // ff
    field_low = inputs[0]
    field = field_low.astype(f32)
    cot_low = out_grad[0]

    line = [shift(field_low, "z", nz, k) for k in range(1, nz)]
    own_two = exchange(jnp.stack([field_low, cot_low]), "y")
    shapes = [((n_ctx, rows, 3 * cols + 128), low), ((8, rows, ff), low), ((n_half, ff_own, ff), low), ((rows, width), low)]
    packed = [pairs, w_qkv, vectors, segments, up_bias.reshape(1, ff_own), w_up, w_down, w_out]
    first_send, up_send, down_part, out_low = call(pack_kernel, 1, packed, shapes)
    first_got = swap(first_send, ctx)
    first_got, own_two, up_send, out_low, *line = gate(first_got, own_two, up_send, out_low, *line)
    pair_own, cot_y = own_two[0], own_two[1]

    pair_line = exchange(jnp.stack(line), "y")
    first_x = exchange(first_got, "x")
    up_part = swap(up_send, plane).reshape(8 * rows, ff)
    cot_two = jnp.stack([cot_low, cot_y])
    cot_x = exchange(cot_two, "x")
    out_line = [shift(out_low, "z", nz, k) for k in range(1, nz)]
    seg_all = first_got[:, 0:2, 3 * cols + 64 :].reshape(seq_len).astype(jnp.int32)
    bias_all = first_got[:, 2:4, 3 * cols + 64 :].reshape(nz, 2, ff_own)
    up_low = lax.dynamic_index_in_dim(bias_all, yi, 1, keepdims=False).reshape(1, ff).astype(f32)
    pair_all = first_got[:, 4, 3 * cols + 64].astype(jnp.int32)
    start = jnp.sum((seg_all[:, None] < seg_all[None, :]).astype(jnp.int32), 0, keepdims=True)
    slot_block = jnp.stack([pair_all, 2 * n_ctx - 1 - pair_all], 1)
    near = [((zi + k) % nz) * 2 + yi for k in range(nz)]
    near = jnp.stack(near + [((zi + k) % nz) * 2 + 1 - yi for k in range(nz)])
    ids = jnp.arange(n_ctx)
    near_block = jnp.sum(jnp.where((near[:, None] == ids[None, :])[:, :, None], slot_block[None], 0), 1)
    spans = jnp.arange(2 * n_ctx)
    block_slot = jnp.sum(jnp.where(slot_block.reshape(1, -1) == spans[:, None], spans[None, :], 0), 1)
    piece_f = jnp.stack([xi * 2 + ci, (1 - xi) * 2 + ci, xi * 2 + 1 - ci, (1 - xi) * 2 + 1 - ci])
    here = jnp.stack([ctx_i, zi, yi, xi, ci])
    table = jnp.concatenate([near_block.reshape(-1), block_slot, piece_f, here]).astype(jnp.int32)
    head_ids = (ctx_i * heads_own + jnp.arange(heads_own)).astype(f32)
    slopes = jnp.exp2(-8.0 * (head_ids + 1.0) / HEADS)
    first_x, cot_x, table, start, up_part, pair_line, *out_line = gate(
        first_x, cot_x, table, start, up_part, pair_line, *out_line
    )
    ff_all = lax.all_gather(jnp.concatenate([up_part, down_part.reshape(n_half * ff_own, ff)], 0), "z", axis=0)

    first_two = jnp.stack([first_got, first_x])
    pieces = (first_got, first_x, exchange(first_two, "c"))
    out_z = jnp.stack([out_low] + out_line)
    out_y = exchange(out_z, "y")
    blocks = [field_low] + line + [pair_own, pair_line]
    attended, att_t, qkv_low, lse, normed_one, seq_rows, qkv_w, vec = attend_forward(
        table, slopes, blocks, pieces, start, cols
    )
    cot_own = jnp.concatenate([cot_two, cot_x], 0)
    cot_other = exchange(cot_own, "c")
    attended, out_y, cot_other = gate(attended.reshape(n_ctx, tokens, cols), out_y, cot_other)

    attended_low = swap(attended, ctx)
    out_zy = jnp.stack([out_z, out_y])
    out_x = exchange(out_zy, "x")
    attended_low, out_x = gate(attended_low, out_x)
    out_own = jnp.concatenate([out_zy, out_x], 0)
    shapes = [((tokens, width), f32), ((tokens, width), low), ((width, width), low)]
    resid, mlp_low, out_w = call(
        project_kernel, 1, [table, attended_low, out_own, exchange(out_own, "c"), field_low, vec], shapes
    )

    mlp_y = exchange(mlp_low, "y")
    mlp_x = exchange(mlp_low, "x")
    mlp_c = exchange(mlp_low, "c")
    mlp_y, mlp_x, mlp_c = gate(mlp_y, mlp_x, mlp_c)
    mlp_d0 = exchange(mlp_x[:half], "y")
    mlp_d1 = exchange(mlp_y[half:], "x")
    mlp_cyx = exchange(jnp.stack([mlp_y, mlp_x]), "c")
    mlp_cd = exchange(jnp.stack([mlp_d0, mlp_d1]), "c")
    four = ((4, tokens, width), low)
    shapes = [four, four, ((8 * tokens, ff), low), ((8 * tokens, ff), low), ((8 * tokens, width), low)]
    scratch = [((ff, width), low), ((width, ff), low)]
    norm_keep, norm_give, hidden, grad_pre, mlp_in = call(
        feed_kernel,
        0,
        [mlp_low, mlp_y, mlp_x, mlp_d0, mlp_d1, mlp_c, mlp_cyx, mlp_cd, cot_own, cot_other, ff_all, up_low],
        shapes,
        scratch,
    )

    norm_c = add_low(norm_keep, exchange(norm_give, "c"))
    norm_d0 = exchange(norm_c[3, :half], "y")
    norm_d1 = exchange(norm_c[3, half:], "x")
    norm_y = exchange(jnp.concatenate([norm_c[1, :half], add_low(norm_c[1, half:], norm_d1)], 0), "y")
    norm_x = exchange(jnp.concatenate([add_low(norm_c[2, :half], norm_d0), norm_c[2, half:]], 0), "x")
    n_ff = 8 * rows + n_half * ff_own
    shapes = [((nz, n_ff + 16, ff), low), four, four]
    ff_terms, result_keep, result_give = call(
        feed_grad_kernel, 0, [mlp_in, grad_pre, hidden, cot_own, cot_other, ff_all], shapes, [((ff, width), low)]
    )
    ff_sum = lax.psum_scatter(ff_terms, "z", scatter_dimension=0, tiled=True)[0]
    shapes = [((tokens, width), f32), ((tokens, width), low), ((n_ctx, tokens, cols), low), ((8, width), f32)]
    grad_resid, resid_low, back_low, resid_sums = call(
        norm_back_kernel, 0, [norm_c[0], norm_x, norm_y, resid, cot_low, vec, out_w], shapes
    )
    back_low, resid_low, result_give = gate(back_low, resid_low, result_give)

    back_all = swap(back_low, ctx)
    out_terms = call(
        out_grad_kernel, 1, [table, attended_low, resid_low], [((2, 2, 2, nz, rows, width), low)]
    )[0]
    out_c = add_low(out_terms[0], exchange(out_terms[1], "c"))
    result_c = add_low(result_keep, exchange(result_give, "c"))
    back_all, out_c, result_c = gate(back_all, out_c, result_c)

    out_x_got = exchange(out_c[1], "x")
    shapes = [((seq_len, 3 * cols), low), ((8, 3 * cols), f32), ((2, 2, n_ctx, rows, 3 * cols), low)]
    scratch = [((seq_len, cols), low), ((seq_len, cols), f32), ((seq_len, cols), f32)]
    grad_mixed, mixed_sum, qkv_terms = call(
        backward_kernel,
        2,
        [table, slopes, back_all.reshape(seq_len, cols), qkv_low, att_t, lse, start, normed_one],
        shapes,
        scratch,
    )

    qkv_c = add_low(qkv_terms[0], exchange(qkv_terms[1], "c"))
    qkv_c, out_x_got, mixed_late = gate(qkv_c, out_x_got, grad_mixed)
    qkv_x = add_low(qkv_c[0], exchange(qkv_c[1], "x"))
    out_two = add_low(out_c[0], out_x_got)
    out_y_got = exchange(out_two[1], "y")
    shapes = [((2, 2, nz, half, width), low), ((4 * n_ctx, 8, cols), f32)]
    normed_grad, small_send = call(
        first_grad_kernel, 1, [table, mixed_late, qkv_w, seq_rows, mixed_sum, resid_sums], shapes
    )
    small_got = swap(small_send, every)
    qkv_x, small_got, out_y_got = gate(qkv_x, small_got, out_y_got)
    in_y = [exchange(normed_grad[u, 1], "y") for u in range(2)]

    qkv_got = swap(qkv_x, ctx)
    out_last = add_low(out_two[0], out_y_got)
    out_moved = jnp.stack([shift(out_last[k], "z", nz, -k) for k in range(1, nz)])
    in_z = [add_low(normed_grad[0, 0], in_y[0])]
    moved = [shift(in_z[0][k], "z", nz, -k) for k in range(1, nz)]
    shapes = [((8, 128), f32), ((2, 4, rows, ff), low), ((rows, width), f32), ((8, rows), f32)]
    squared, up_own, grad_out_own, grad_vec_own = call(
        gather_grad_kernel, 1, [table, ff_sum, out_last[0], out_moved, small_got], shapes
    )
    up_c = jnp.stack([up_own[0], exchange(up_own[1], "c")])
    squared = call(qkv_square_kernel, 0, [qkv_got, squared], [((8, 128), f32)])[0]

    squares = swap(jnp.broadcast_to(squared[:1], (4 * n_ctx, 128)), every)
    in_z = in_z + [add_low(normed_grad[1, 0], in_y[1])]
    moved = moved + [shift(in_z[1][k], "z", nz, -k) for k in range(1, nz)]
    up_x = jnp.stack([up_c[:, :2], exchange(up_c[:, 2:], "x")])
    up_y = jnp.stack([up_x[:, :, 0], exchange(up_x[:, :, 1], "y")])
    masters = [w_qkv, w_out, w_up, w_down, up_bias.reshape(1, ff_own), vectors]
    firsts = [first_qkv, first_out, first_up, first_down, first_bias.reshape(1, ff_own), first_vectors]
    seconds = [second_qkv, second_out, second_up, second_down, second_bias.reshape(1, ff_own), second_vectors]
    shapes = [((1, 1), f32)]
    for item in masters:
        shapes = shapes + [(item.shape, f32)] * 4
    grads = [table, squares, qkv_got, grad_out_own, up_y, ff_sum, grad_vec_own]
    grad_norm, *results = call(adam_kernel, 1, grads + masters + firsts + seconds, shapes)
    for k in range(16, 20):
        results[k] = results[k].reshape(ff_own)

    result_x = exchange(after(result_c[2:], qkv_c), "x")
    result_y = exchange(add_low(result_c[1], result_x[1]), "y")
    result = resid + result_c[0].astype(f32) + result_x[0].astype(f32) + result_y.astype(f32) + vec[7]
    own_grads = []
    moved = gate(*moved, squares)[:-1]
    for u in range(2):
        total = in_z[u][0].astype(f32)
        for other in moved[u * (nz - 1) : (u + 1) * (nz - 1)]:
            total = total + other.astype(f32)
        own_grads = own_grads + [total]
    norm_one_back = jax.vjp(lambda v: layer_norm(v, vec[0], vec[1]), field)[1]
    in_grad = grad_resid + norm_one_back(jnp.concatenate(own_grads, 0))[0]
    return (result.astype(low)[None], in_grad[None], grad_norm[0, 0], *results)


def solution(mesh):
    n_ctx = mesh.shape["ctx"]
    if HEADS % n_ctx == 0 and n_ctx % 2 == 0 and mesh.shape["fsdp"] == 4:
        body = local_split
        ctx, fsdp = ("z", "y"), ("x", "c")
        mesh = Mesh(mesh.devices.reshape(n_ctx // 2, 2, 2, 2), ctx + fsdp)
    else:
        body = local
        ctx, fsdp = ("ctx",), ("fsdp",)
    rows = P(fsdp, ctx, None)
    flat = P(fsdp, ctx)
    mat = P(ctx + fsdp, None)
    vec = P(ctx + fsdp)
    wide = P(None, ctx + fsdp)
    group = (mat, mat, mat, mat, vec, wide)
    outs = ()
    for spec in group:
        outs = outs + (spec,) * 4
    return jax.shard_map(
        body,
        mesh=mesh,
        in_specs=(rows, rows, flat, flat) + group * 3,
        out_specs=(rows, rows, P()) + outs,
        check_vma=False,
    )
```

```python
import functools
import math

import jax
import jax.numpy as jnp
from jax import lax
from jax.experimental import pallas as pl
from jax.experimental.pallas import tpu as pltpu
from jax.sharding import Mesh
from jax.sharding import PartitionSpec as P

HEADS = 16
HD = 64


norm_eps = 1e-05
beta_one = 0.9
beta_two = 0.95
adam_eps = 1e-08
learn_rate = 0.02
weight_decay = 0.1
adam_step = 10
max_norm = 1.0
masked = -1e30
group_heads = 2


def layer_norm(field, gain, shift):
    center = field - jnp.mean(field, -1, keepdims=True)
    spread = jnp.mean(center * center, -1, keepdims=True)
    return center * lax.rsqrt(spread + norm_eps) * gain + shift


def gelu_exact(field):
    return jax.nn.gelu(field, approximate=False)


def contract(left, right, left_dim, right_dim):
    return lax.dot_general(
        left, right, (((left_dim,), (right_dim,)), ((), ())), preferred_element_type=jnp.float32
    )


def place(pair_ids, block, n_ctx):
    blocks = jnp.stack([pair_ids, 2 * n_ctx - 1 - pair_ids], 1).reshape(-1)
    offsets = jnp.arange(block, dtype=jnp.int32)
    return (blocks[:, None] * block + offsets[None, :]).reshape(-1)


def pick(array, first):
    return lax.dynamic_slice_in_dim(array, first, group_heads, 1)


def adamw(weight, grad, first, second, clip):
    clipped = grad * clip
    first_new = beta_one * first + (1.0 - beta_one) * clipped
    second_new = beta_two * second + (1.0 - beta_two) * clipped * clipped
    first_hat = first_new / (1.0 - beta_one**adam_step)
    second_hat = second_new / (1.0 - beta_two**adam_step)
    update = -learn_rate * (first_hat / (jnp.sqrt(second_hat) + adam_eps) + weight_decay * weight)
    return (update, first_new, second_new)


def local(
    inputs,
    out_grad,
    segments,
    pairs,
    w_qkv,
    w_out,
    w_up,
    w_down,
    up_bias,
    vectors,
    first_qkv,
    first_out,
    first_up,
    first_down,
    first_bias,
    first_vectors,
    second_qkv,
    second_out,
    second_up,
    second_down,
    second_bias,
    second_vectors,
):
    low_type = jnp.bfloat16
    n_ctx = lax.axis_size("ctx")
    field = inputs[0].astype(jnp.float32)
    tokens = field.shape[0]
    block = tokens // 2
    width = field.shape[1]
    seq_len = tokens * n_ctx
    scale = HD ** (-0.5)
    groups = HEADS // group_heads
    slope = 2.0 ** (-8.0 * (jnp.arange(HEADS, dtype=jnp.float32) + 1.0) / HEADS)
    qkv_w, out_w, vec_low = (
        lax.all_gather(w_qkv.astype(low_type), ("ctx", "fsdp"), axis=0, tiled=True),
        lax.all_gather(w_out.astype(low_type), ("ctx", "fsdp"), axis=0, tiled=True),
        lax.all_gather(vectors.astype(low_type), ("ctx", "fsdp"), axis=1, tiled=True),
    )
    vec = vec_low.astype(jnp.float32)
    gain_one, shift_one, gain_two, shift_two = (vec[0], vec[1], vec[2], vec[3])
    bias_query, bias_value, bias_out, bias_down = (vec[4], vec[5], vec[6], vec[7])
    normed_one = layer_norm(field, gain_one, shift_one)
    attn_in = normed_one.astype(low_type)
    mixed = jnp.dot(attn_in, qkv_w, preferred_element_type=jnp.float32)
    query = (mixed[:, :width] + bias_query).astype(low_type)
    keys = mixed[:, width : 2 * width].astype(low_type)
    values = (mixed[:, 2 * width :] + bias_value).astype(low_type)
    pair_ids = pairs[0]
    kv_all, pair_all, seg_all = (
        lax.all_gather(jnp.concatenate([keys, values], 1), "ctx", axis=0, tiled=True),
        lax.all_gather(pair_ids, "ctx", axis=0, tiled=True),
        lax.all_gather(segments[0], "ctx", axis=0, tiled=True),
    )
    pos_query = place(pair_ids, block, n_ctx)
    pos_key = place(pair_all, block, n_ctx)
    seg_query = jnp.take(seg_all, pos_query)
    seg_key = jnp.take(seg_all, pos_key)
    relative = (pos_key[None, :] - pos_query[:, None]).astype(jnp.float32)
    allowed = (seg_query[:, None] == seg_key[None, :]) & (pos_key[None, :] <= pos_query[:, None])
    query_heads = query.reshape(tokens, HEADS, HD)
    key_heads = kv_all[:, :width].reshape(seq_len, HEADS, HD)
    value_heads = kv_all[:, width:].reshape(seq_len, HEADS, HD)

    def scores_of(query_part, key_part, first, offsets, visible):
        slopes = lax.dynamic_slice_in_dim(slope, first, group_heads, 0)
        raw = (
            jnp.einsum("rhe,khe->hrk", query_part, key_part, preferred_element_type=jnp.float32)
            * scale
        )
        raw = raw + slopes[:, None, None] * offsets[None]
        return jnp.where(visible[None], raw, masked)

    def forward_group(index, carry):
        attended, log_total = carry
        first = index * group_heads
        scores = scores_of(
            pick(query_heads, first), pick(key_heads, first), first, relative, allowed
        )
        top = jnp.max(scores, -1, keepdims=True)
        expo = jnp.exp(scores - top)
        total = jnp.sum(expo, -1, keepdims=True)
        chance_low = (expo / total).astype(low_type)
        part_out = jnp.einsum(
            "hrk,khe->rhe", chance_low, pick(value_heads, first), preferred_element_type=jnp.float32
        )
        attended = lax.dynamic_update_slice_in_dim(attended, part_out, first, 1)
        log_total = lax.dynamic_update_slice_in_dim(
            log_total, (top + jnp.log(total))[:, :, 0].T, first, 1
        )
        return (attended, log_total)

    attended, log_total = lax.fori_loop(
        0,
        groups,
        forward_group,
        (jnp.zeros((tokens, HEADS, HD), jnp.float32), jnp.zeros((tokens, HEADS), jnp.float32)),
    )
    attended_low = attended.reshape(tokens, width).astype(low_type)
    resid = field + jnp.dot(attended_low, out_w, preferred_element_type=jnp.float32) + bias_out
    normed_two = layer_norm(resid, gain_two, shift_two)
    mlp_in = normed_two.astype(low_type)
    up_w, down_w, up_low = (
        lax.all_gather(w_up.astype(low_type), ("ctx", "fsdp"), axis=0, tiled=True),
        lax.all_gather(w_down.astype(low_type), ("ctx", "fsdp"), axis=0, tiled=True),
        lax.all_gather(up_bias.astype(low_type), ("ctx", "fsdp"), axis=0, tiled=True),
    )
    pre = jnp.dot(mlp_in, up_w, preferred_element_type=jnp.float32) + up_low.astype(jnp.float32)
    hidden = gelu_exact(pre).astype(low_type)
    result = resid + jnp.dot(hidden, down_w, preferred_element_type=jnp.float32) + bias_down
    cotangent_low = out_grad[0]
    cotangent = cotangent_low.astype(jnp.float32)
    up_back, down_back = (
        lax.all_gather(w_up.astype(low_type), ("ctx", "fsdp"), axis=0, tiled=True),
        lax.all_gather(w_down.astype(low_type), ("ctx", "fsdp"), axis=0, tiled=True),
    )
    grad_down_term = contract(hidden, cotangent_low, 0, 0)
    grad_bias_down = jnp.sum(cotangent, 0)
    grad_hidden = contract(cotangent_low, down_back, 1, 1)
    gelu_back = jax.vjp(gelu_exact, pre)[1]
    grad_pre = gelu_back(grad_hidden)[0].astype(low_type)
    grad_up_bias = jnp.sum(grad_pre.astype(jnp.float32), 0)
    grad_up_term = contract(mlp_in, grad_pre, 0, 0)
    grad_normed_two = contract(grad_pre, up_back, 1, 1)
    norm_two_back = jax.vjp(layer_norm, resid, gain_two, shift_two)[1]
    grad_resid_norm, grad_gain_two, grad_shift_two = norm_two_back(grad_normed_two)
    grad_resid = cotangent + grad_resid_norm
    grad_up_own, grad_down_own, grad_bias_own = (
        lax.psum_scatter(grad_up_term, ("ctx", "fsdp"), scatter_dimension=0, tiled=True),
        lax.psum_scatter(grad_down_term, ("ctx", "fsdp"), scatter_dimension=0, tiled=True),
        lax.psum_scatter(grad_up_bias, ("ctx", "fsdp"), scatter_dimension=0, tiled=True),
    )
    qkv_back, out_back = (
        lax.all_gather(w_qkv.astype(low_type), ("ctx", "fsdp"), axis=0, tiled=True),
        lax.all_gather(w_out.astype(low_type), ("ctx", "fsdp"), axis=0, tiled=True),
    )
    grad_bias_out = jnp.sum(grad_resid, 0)
    resid_low = grad_resid.astype(low_type)
    grad_out_term = contract(attended_low, resid_low, 0, 0)
    back_low = contract(resid_low, out_back, 1, 1).astype(low_type)
    back_heads = back_low.reshape(tokens, HEADS, HD)

    def backward_group(index, carry):
        grad_query, grad_key, grad_value = carry
        first = index * group_heads
        query_part = pick(query_heads, first)
        key_part = pick(key_heads, first)
        value_part = pick(value_heads, first)
        back_part = pick(back_heads, first)
        scores = scores_of(query_part, key_part, first, relative, allowed)
        logsum = lax.dynamic_slice_in_dim(log_total, first, group_heads, 1).T
        chance = jnp.exp(scores - logsum[:, :, None])
        pushed = jnp.einsum(
            "rhe,khe->hrk", back_part, value_part, preferred_element_type=jnp.float32
        )
        centre = jnp.sum(chance * pushed, -1, keepdims=True)
        dscore = (chance * (pushed - centre)).astype(low_type)
        chance_low = chance.astype(low_type)
        part_query = (
            jnp.einsum("hrk,khe->rhe", dscore, key_part, preferred_element_type=jnp.float32) * scale
        )
        part_key = (
            jnp.einsum("hrk,rhe->khe", dscore, query_part, preferred_element_type=jnp.float32)
            * scale
        )
        part_value = jnp.einsum(
            "hrk,rhe->khe", chance_low, back_part, preferred_element_type=jnp.float32
        )
        grad_query = lax.dynamic_update_slice_in_dim(grad_query, part_query, first, 1)
        grad_key = lax.dynamic_update_slice_in_dim(grad_key, part_key, first, 1)
        grad_value = lax.dynamic_update_slice_in_dim(grad_value, part_value, first, 1)
        return (grad_query, grad_key, grad_value)

    zero_keys = jnp.zeros((seq_len, HEADS, HD), jnp.float32)
    grad_query, grad_key, grad_value = lax.fori_loop(
        0,
        groups,
        backward_group,
        (jnp.zeros((tokens, HEADS, HD), jnp.float32), zero_keys, zero_keys),
    )
    own_key, own_value = (
        lax.psum_scatter(
            grad_key.reshape(seq_len, width).astype(jnp.bfloat16),
            "ctx",
            scatter_dimension=0,
            tiled=True,
        ).astype(jnp.float32),
        lax.psum_scatter(
            grad_value.reshape(seq_len, width).astype(jnp.bfloat16),
            "ctx",
            scatter_dimension=0,
            tiled=True,
        ).astype(jnp.float32),
    )
    grad_query_low = grad_query.reshape(tokens, width).astype(low_type)
    grad_key_low = own_key.astype(low_type)
    grad_value_low = own_value.astype(low_type)
    grad_mixed = jnp.concatenate([grad_query_low, grad_key_low, grad_value_low], 1)
    grad_bias_query = jnp.sum(grad_query_low.astype(jnp.float32), 0)
    grad_bias_value = jnp.sum(grad_value_low.astype(jnp.float32), 0)
    grad_qkv_term = contract(attn_in, grad_mixed, 0, 0)
    grad_normed_one = contract(grad_mixed, qkv_back, 1, 1)
    norm_one_back = jax.vjp(layer_norm, field, gain_one, shift_one)[1]
    grad_field_norm, grad_gain_one, grad_shift_one = norm_one_back(grad_normed_one)
    in_grad = grad_resid + grad_field_norm
    grad_vec_term = jnp.stack(
        [
            grad_gain_one,
            grad_shift_one,
            grad_gain_two,
            grad_shift_two,
            grad_bias_query,
            grad_bias_value,
            grad_bias_out,
            grad_bias_down,
        ],
        0,
    )
    grad_qkv_own, grad_out_own, grad_vec_own = (
        lax.psum_scatter(grad_qkv_term, ("ctx", "fsdp"), scatter_dimension=0, tiled=True),
        lax.psum_scatter(grad_out_term, ("ctx", "fsdp"), scatter_dimension=0, tiled=True),
        lax.psum_scatter(grad_vec_term, ("ctx", "fsdp"), scatter_dimension=1, tiled=True),
    )
    grads = (grad_qkv_own, grad_out_own, grad_up_own, grad_down_own, grad_bias_own, grad_vec_own)
    local_squares = sum([jnp.sum(item * item) for item in grads])
    grad_norm = jnp.sqrt(lax.psum(local_squares, ("ctx", "fsdp")))
    clip = jnp.minimum(1.0, max_norm / (grad_norm + 1e-06))
    masters = (w_qkv, w_out, w_up, w_down, up_bias, vectors)
    firsts = (first_qkv, first_out, first_up, first_down, first_bias, first_vectors)
    seconds = (second_qkv, second_out, second_up, second_down, second_bias, second_vectors)
    results = []
    for weight, grad, first, second in zip(masters, grads, firsts, seconds):
        update, first_new, second_new = adamw(weight, grad, first, second, clip)
        results = results + [grad, update, first_new, second_new]
    return (
        result.astype(low_type)[None],
        in_grad[None],
        grad_norm,
        results[0],
        results[1],
        results[2],
        results[3],
        results[4],
        results[5],
        results[6],
        results[7],
        results[8],
        results[9],
        results[10],
        results[11],
        results[12],
        results[13],
        results[14],
        results[15],
        results[16],
        results[17],
        results[18],
        results[19],
        results[20],
        results[21],
        results[22],
        results[23],
    )


def exchange(v, axis):
    return lax.ppermute(v, axis, [(0, 1), (1, 0)])


def shift(v, axis, n_line, k):
    return lax.ppermute(v, axis, [(i, (i - k) % n_line) for i in range(n_line)])


def swap(v, axes):
    return lax.all_to_all(v, axes, 0, 0, tiled=True)


def gate(*values):
    return lax.optimization_barrier(values)


def after(v, *others):
    return lax.optimization_barrier((v,) + others)[0]


def order_two(own, other, axis, dim):
    first = lax.axis_index(axis) == 0
    return jnp.stack([jnp.where(first, own, other), jnp.where(first, other, own)], dim)


def split_two(part, axis, dim):
    me = lax.axis_index(axis)
    keep = lax.dynamic_index_in_dim(part, me, dim, keepdims=False)
    return keep, lax.dynamic_index_in_dim(part, 1 - me, dim, keepdims=False)


def add_low(keep, got):
    return (keep.astype(jnp.float32) + got.astype(jnp.float32)).astype(jnp.bfloat16)


def line_gives(part, axis, n_line):
    me = lax.axis_index(axis)
    blocks = [lax.dynamic_index_in_dim(part, (me + k) % n_line, 0, keepdims=False) for k in range(n_line)]
    return blocks[0], [shift(blocks[k], axis, n_line, -k) for k in range(1, n_line)]


def line_order(parts, axis):
    n_line = len(parts)
    first = (n_line - lax.axis_index(axis)) % n_line
    return lax.dynamic_slice_in_dim(jnp.concatenate([jnp.stack(parts)] * 2, 0), first, n_line, 0)


def lanes_of(head, shape):
    return lax.broadcasted_iota(jnp.int32, shape, 1) // HD == head


def head_parts(query, keys, slope, head):
    seq = keys.shape[0]
    lane = lax.broadcasted_iota(jnp.int32, keys.shape, 1)
    own = lane // HD == head
    spot = lane - (1 - head) * HD
    bias = lax.broadcasted_iota(jnp.int32, (seq, 1), 0).astype(jnp.float32) * (slope * HD**0.5)
    high = bias.astype(jnp.bfloat16)
    rest = bias - high.astype(jnp.float32)
    middle = rest.astype(jnp.bfloat16)
    small = (rest - middle.astype(jnp.float32)).astype(jnp.bfloat16)
    zero = jnp.zeros_like(keys)
    extra = jnp.where(spot == 0, high, jnp.where(spot == 1, middle, jnp.where(spot == 2, small, zero)))
    ones = jnp.where((spot >= 0) & (spot <= 2), jnp.ones_like(keys), zero)
    return jnp.where(own, query, ones), jnp.where(own, keys, extra)


def visible(start, tile, at, size):
    key = lax.broadcasted_iota(jnp.int32, (size, tile), 0)
    seen = key >= start
    return seen & (key <= lax.broadcasted_iota(jnp.int32, (size, tile), 1) + at)


def forward_kernel(n_refs, meta, slopes, *refs):
    pieces = refs[n_refs : n_refs + 4]
    start_ref = refs[n_refs + 4]
    att_ref, att_t, qkv_ref, lse_ref, normed, x_ref, w_ref, vec_ref, extra = refs[n_refs + 5 :]
    n_line = (n_refs - 3) // 2 + 1
    own, pair, pair_line = refs[0], refs[1], refs[2]
    line, rest = refs[3 : 2 + n_line], refs[2 + n_line : 1 + 2 * n_line]
    n_blocks = 2 * n_line
    cut = line[0].shape[1]

    def block_part(b, span):
        z, other = b % n_line, b // n_line
        if z == 0:
            return (pair if other else own)[span, :]
        first = pair_line[z - 1, span, :] if other else line[z - 1][span, :]
        return jnp.concatenate([first, rest[z - 1][other, span, :]], 1)

    f32, low = jnp.float32, jnp.bfloat16
    n_ctx, rows, _ = pieces[0].shape
    tokens, width = own.shape
    half = tokens // 2
    seq = tokens * n_blocks
    cols = qkv_ref.shape[1] // 3
    spans = 2 * n_blocks
    for c in range(n_ctx):
        for p in range(4):
            piece = pieces[p][c]
            to = pl.ds(pl.multiple_of(c * 4 * rows + meta[2 * spans + p] * rows, rows), rows)
            w_ref[to, :] = piece[:, : 3 * cols]
            extra[to, :] = piece[:, 3 * cols :]
    pick_rows = (
        lax.broadcasted_iota(jnp.int32, (8, 128), 0) == lax.broadcasted_iota(jnp.int32, (8, 128), 1)
    ).astype(low)
    vec = contract(pick_rows, extra[...], 1, 1)
    vec_ref[...] = vec
    gain, move = vec[0:1], vec[1:2]
    for j in range(spans):
        part = block_part(j // 2, slice((j % 2) * half, (j % 2 + 1) * half))
        to = pl.ds(pl.multiple_of(meta[j] * half, half), half)
        x_ref[to, :] = part
        normed[to, :] = layer_norm(part.astype(f32), gain, move).astype(low)
    at = pl.ds(pl.multiple_of(meta[2 * spans + 4] * cols, cols), cols)
    bias_q, bias_v = vec_ref[4:5, at], vec_ref[5:6, at]
    tile = min(256, seq)
    for t in range(seq // tile):
        span = pl.ds(t * tile, tile)
        mixed = jnp.dot(normed[span, :], w_ref[...], preferred_element_type=f32)
        qkv_ref[span, :cols] = (mixed[:, :cols] + bias_q).astype(low)
        qkv_ref[span, cols : 2 * cols] = mixed[:, cols : 2 * cols].astype(low)
        qkv_ref[span, 2 * cols :] = (mixed[:, 2 * cols :] + bias_v).astype(low)
    factor = HD**-0.5 * 1.4426950408889634
    query, keys, values = qkv_ref[:, :cols], qkv_ref[:, cols : 2 * cols], qkv_ref[:, 2 * cols :]
    lse_ref[...] = jnp.zeros_like(lse_ref)
    for h in range(cols // HD):
        q_h, k_h = head_parts(query, keys, slopes[h], h)
        v_h = jnp.where(lanes_of(h, values.shape), values, jnp.zeros_like(values))
        for t in range(seq // tile):
            size = (t + 1) * tile
            span = slice(t * tile, (t + 1) * tile)
            score = contract(k_h[:size], q_h[span], 1, 1) * factor
            score = jnp.where(visible(start_ref[:, span], tile, t * tile, size), score, masked)
            top = jnp.max(score, 0, keepdims=True)
            expo = jnp.exp2(score - top)
            total = jnp.sum(expo, 0, keepdims=True)
            lse_ref[h : h + 1, span] = top + jnp.log2(total)
            part = contract(v_h[:size], expo.astype(low), 0, 0) / total
            att_t[:, span] = part if h == 0 else att_t[:, span] + part
    for t in range(seq // tile):
        span = slice(t * tile, (t + 1) * tile)
        x_tile = att_t[:, span].T.astype(low)
        for u in range(tile // half):
            b = t * (tile // half) + u
            to = meta[spans + b]
            att_ref[pl.ds(pl.multiple_of(to * half, half), half), :] = x_tile[u * half : (u + 1) * half]


def pack_kernel(pairs, w_qkv, vectors, segments, up_bias, w_up, w_down, w_out, first_ref, up_ref, down_ref, out_ref):
    low, f32 = jnp.bfloat16, jnp.float32
    n_ctx, rows, wide = first_ref.shape
    cols = (wide - 128) // 3
    width = n_ctx * cols
    row = lax.broadcasted_iota(jnp.int32, (rows, 128), 0)
    lane = lax.broadcasted_iota(jnp.int32, (rows, 128), 1)
    one_hot = lax.broadcasted_iota(jnp.int32, (8, 128), 0) == lax.broadcasted_iota(jnp.int32, (8, 128), 1)
    columns = contract(vectors[...].astype(low), one_hot.astype(low), 0, 0)
    seg, bias = segments[...].astype(f32), up_bias[...]
    lines = [pltpu.roll(seg, 64, 1), seg, pltpu.roll(bias, 64, 1), bias]
    extra = jnp.where(lane < 8, columns, 0.0)
    for k in range(4):
        extra = jnp.where((row == k) & (lane >= 64), lines[k], extra)
    extra = jnp.where((row == 4) & (lane >= 64), pairs[0, 0].astype(f32), extra).astype(low)
    for c in range(n_ctx):
        for k in range(3):
            first_ref[c, :, k * cols : (k + 1) * cols] = w_qkv[:, k * width + c * cols : k * width + (c + 1) * cols].astype(low)
        first_ref[c, :, 3 * cols :] = extra
    n_plane, _, ff = up_ref.shape
    own = ff // (n_ctx // 2)
    for r in range(n_plane):
        for k in range(n_ctx // 2):
            up_ref[r, :, k * own : (k + 1) * own] = w_up[:, (k * n_plane + r) * own : (k * n_plane + r + 1) * own].astype(low)
    for k in range(down_ref.shape[0]):
        down_ref[k] = w_down[:, k * ff : (k + 1) * ff].astype(low)
    wide_out = out_ref.shape[1]
    for k in range(out_ref.shape[0] // rows):
        out_ref[k * rows : (k + 1) * rows, :] = w_out[:, k * wide_out : (k + 1) * wide_out].astype(low)


def project_kernel(table, att, own_ref, x_ref, c_ref, cx_ref, field, vec, resid_ref, mlp_ref, w_ref):
    low, f32 = jnp.bfloat16, jnp.float32
    n_ctx, tokens, cols = att.shape
    n_line = own_ref.shape[1]
    rows = w_ref.shape[0] // (8 * n_line)
    wide = own_ref.shape[3]
    at = 4 * n_ctx + 5
    zi, yi, xi, ci = (table[at + k] for k in range(4))
    for q, ref in enumerate((own_ref, x_ref, c_ref, cx_ref)):
        for p in range(2):
            for k in range(n_line):
                z = lax.rem(zi + k, n_line)
                y = lax.rem(yi + p, 2)
                x = lax.rem(xi + q % 2, 2)
                to = ((z * 2 + y) * 4 + x * 2 + lax.rem(ci + q // 2, 2)) * rows
                for part in range(tokens // rows):
                    spot = (pl.ds(pl.multiple_of(to, rows), rows), slice(part * wide, (part + 1) * wide))
                    w_ref[spot] = ref[p, k, part * rows : (part + 1) * rows, :]
    heads = jnp.concatenate([att[c] for c in range(n_ctx)], 1)
    moved = jnp.dot(heads, w_ref[...], preferred_element_type=f32)
    resid = field[...].astype(f32) + moved + vec[6:7]
    resid_ref[...] = resid
    mlp_ref[...] = layer_norm(resid, vec[2:3], vec[3:4]).astype(low)


def down_of(ff_all, down):
    n_line, own = ff_all.shape[0], down.shape[0] // ff_all.shape[0]
    ff = down.shape[0]
    up_rows = ff_all.shape[1] - down.shape[1] * own // ff
    for k in range(n_line):
        for h in range(down.shape[1] // ff):
            down[k * own : (k + 1) * own, h * ff : (h + 1) * ff] = ff_all[k, up_rows + h * own : up_rows + (h + 1) * own, :]


def feed_kernel(*refs):
    low, f32 = jnp.bfloat16, jnp.float32
    m_own, m_y, m_x, m_d0, m_d1, m_c, m_cyx, m_cd = refs[:8]
    cots, ff_all, bias = refs[8:12], refs[12], refs[13]
    keep_ref, give_ref, hidden_ref, pre_ref, mlp_ref, down, up = refs[14:]
    tokens, width = m_own.shape
    half = tokens // 2
    ff = hidden_ref.shape[1]
    n_line = ff_all.shape[0]
    up_rows = width // n_line
    for k in range(n_line):
        up[k * up_rows : (k + 1) * up_rows, :] = ff_all[k, :up_rows, :]
    down_of(ff_all, down)
    blocks = (m_own[...], m_y[...], m_x[...], None, m_c[...], m_cyx[0], m_cyx[1])
    for b, block in enumerate(blocks):
        if block is not None:
            mlp_ref[b * tokens : (b + 1) * tokens, :] = block
    mlp_ref[3 * tokens : 3 * tokens + half, :] = m_d0[...]
    mlp_ref[3 * tokens + half : 4 * tokens, :] = m_d1[...]
    mlp_ref[7 * tokens : 7 * tokens + half, :] = m_cd[0]
    mlp_ref[7 * tokens + half : 8 * tokens, :] = m_cd[1]
    for t in range(4):
        span = slice(2 * t * tokens, 2 * (t + 1) * tokens)
        pre = jnp.dot(mlp_ref[span, :], up[...], preferred_element_type=f32) + bias[...]
        cdf = 0.5 * (1.0 + lax.erf(pre * 0.7071067811865476))
        pdf = jnp.exp(-0.5 * pre * pre) * 0.3989422804014327
        hidden_ref[span, :] = (pre * cdf).astype(low)
        cot = cots[t][...].reshape(2 * tokens, width)
        grad = (contract(cot, down[...], 1, 1) * (cdf + pre * pdf)).astype(low)
        pre_ref[span, :] = grad
        part = contract(grad, up[...], 1, 1).astype(low).reshape(2, tokens, width)
        to = keep_ref if t < 2 else give_ref
        to[2 * (t % 2) : 2 * (t % 2) + 2] = part


def feed_grad_kernel(mlp_ref, pre_ref, hidden_ref, cot_0, cot_1, cot_2, cot_3, terms_ref):
    low, f32 = jnp.bfloat16, jnp.float32
    seq, width = mlp_ref.shape
    ff = pre_ref.shape[1]
    n_line = terms_ref.shape[0]
    own, up_rows = ff // n_line, width // n_line
    n_half = width // ff
    for k in range(n_line):
        up = contract(mlp_ref[:, k * up_rows : (k + 1) * up_rows], pre_ref[...], 0, 0)
        terms_ref[k, :up_rows, :] = up.astype(low)
        for h in range(n_half):
            part = slice(k * own, (k + 1) * own)
            cut = slice(h * ff, (h + 1) * ff)
            cot = [ref[:, :, cut].reshape(seq // 4, ff) for ref in (cot_0, cot_1, cot_2, cot_3)]
            total = contract(hidden_ref[:, part], jnp.concatenate(cot, 0), 0, 0)
            terms_ref[k, up_rows + h * own : up_rows + (h + 1) * own, :] = total.astype(low)
    sums = jnp.sum(pre_ref[...].astype(f32), 0, keepdims=True)
    pad = terms_ref.shape[1] - up_rows - n_half * own
    for k in range(n_line):
        line = jnp.concatenate([sums[:, k * own : (k + 1) * own], jnp.zeros((1, ff - own), f32)], 1)
        terms_ref[k, up_rows + n_half * own :, :] = jnp.broadcast_to(line, (pad, ff)).astype(low)


def result_kernel(hidden_ref, ff_all, keep_ref, give_ref, down):
    down_of(ff_all, down)
    tokens = keep_ref.shape[1]
    for t in range(4):
        span = slice(2 * t * tokens, 2 * (t + 1) * tokens)
        part = jnp.dot(hidden_ref[span, :], down[...], preferred_element_type=jnp.float32)
        to = keep_ref if t < 2 else give_ref
        to[2 * (t % 2) : 2 * (t % 2) + 2] = part.astype(jnp.bfloat16).reshape(2, tokens, down.shape[1])


def norm_back_kernel(
    table, own, got_x, got_y, resid_ref, cot_ref, vec, w_ref, att, grad_ref, back_ref, sums_ref, keep_ref, give_ref, terms
):
    low, f32 = jnp.bfloat16, jnp.float32
    grad = own[...].astype(f32) + got_x[...].astype(f32) + got_y[...].astype(f32)
    resid = resid_ref[...]
    center = resid - jnp.mean(resid, -1, keepdims=True)
    sharp = lax.rsqrt(jnp.mean(center * center, -1, keepdims=True) + norm_eps)
    unit = center * sharp
    scaled = grad * vec[2:3]
    inner = scaled - jnp.mean(scaled, -1, keepdims=True) - unit * jnp.mean(scaled * unit, -1, keepdims=True)
    cot = cot_ref[...].astype(f32)
    total = cot + inner * sharp
    grad_ref[...] = total
    rounded = total.astype(low)
    back = contract(rounded, w_ref[...], 1, 1).astype(low)
    n_ctx, _, cols = back_ref.shape
    for c in range(n_ctx):
        back_ref[c] = back[:, c * cols : (c + 1) * cols]
    row = lax.broadcasted_iota(jnp.int32, sums_ref.shape, 0)
    sums = jnp.where(row == 2, jnp.sum(grad * unit, 0, keepdims=True), 0.0)
    sums = jnp.where(row == 3, jnp.sum(grad, 0, keepdims=True), sums)
    sums = jnp.where(row == 6, jnp.sum(total, 0, keepdims=True), sums)
    sums_ref[...] = jnp.where(row == 7, jnp.sum(cot, 0, keepdims=True), sums)
    for c in range(n_ctx):
        terms[c * cols : (c + 1) * cols, :] = contract(att[c], rounded, 0, 0).astype(low)
    n_line, rows = keep_ref.shape[2:4]
    at = 4 * n_ctx + 5
    for which, ref in enumerate((keep_ref, give_ref)):
        for q in range(4 * n_line):
            x, y, z = q // (2 * n_line), q // n_line % 2, q % n_line
            chip = (lax.rem(table[at] + z, n_line) * 2 + lax.rem(table[at + 1] + y, 2)) * 4
            to = (chip + lax.rem(table[at + 2] + x, 2) * 2 + lax.rem(table[at + 3] + which, 2)) * rows
            ref[x, y, z] = terms[pl.ds(pl.multiple_of(to, rows), rows), :]


def backward_kernel(
    table, slopes, back_ref, qkv_ref, att_t, lse_ref, start_ref, normed, w_ref, x_ref, sums_ref,
    keep_ref, give_ref, keep_a, give_a, keep_b, give_b, mixed_ref, back, d_key, d_value, moved, made,
):
    f32, low = jnp.float32, jnp.bfloat16
    seq, cols = back_ref.shape
    n_ctx, rows = keep_ref.shape[1:3]
    width = w_ref.shape[0]
    spans = 2 * n_ctx
    half = seq // spans
    for b in range(spans):
        back[b * half : (b + 1) * half, :] = back_ref[pl.ds(pl.multiple_of(table[spans + b] * half, half), half), :]
    factor = HD**-0.5 * 1.4426950408889634
    query, keys, values = qkv_ref[:, :cols], qkv_ref[:, cols : 2 * cols], qkv_ref[:, 2 * cols :]
    grads = back[...]
    product = att_t[...] * grads.astype(f32).T
    tile = min(256, seq)
    d_query = [None] * (seq // tile)
    for h in range(cols // HD):
        q_h, k_h = head_parts(query, keys, slopes[h], h)
        own = lanes_of(h, values.shape)
        zero = jnp.zeros_like(values)
        v_h, g_h = jnp.where(own, values, zero), jnp.where(own, grads, zero)
        qq_h, kk_h = jnp.where(own, query, zero), jnp.where(own, keys, zero)
        delta = jnp.sum(product[h * HD : (h + 1) * HD], 0, keepdims=True)
        for t in reversed(range(seq // tile)):
            size = (t + 1) * tile
            span = slice(t * tile, (t + 1) * tile)
            score = contract(k_h[:size], q_h[span], 1, 1) * factor
            score = jnp.where(visible(start_ref[:, span], tile, t * tile, size), score, masked)
            chance = jnp.exp2(score - lse_ref[h : h + 1, span])
            pushed = contract(v_h[:size], g_h[span], 1, 1)
            dscore = (chance * (pushed - delta[:, span])).astype(low)
            part_v = jnp.dot(chance.astype(low), g_h[span], preferred_element_type=f32)
            part_k = jnp.dot(dscore, qq_h[span], preferred_element_type=f32)
            if h == 0 and t == seq // tile - 1:
                d_value[...] = part_v
                d_key[...] = part_k
            else:
                d_value[:size, :] += part_v
                d_key[:size, :] += part_k
            part_q = contract(kk_h[:size], dscore, 0, 0)
            d_query[t] = part_q if h == 0 else d_query[t] + part_q
    scale = HD**-0.5
    for t in range(seq // tile):
        mixed_ref[t * tile : (t + 1) * tile, :cols] = (d_query[t] * scale).T.astype(low)
    mixed_ref[:, cols : 2 * cols] = (d_key[...] * scale).astype(low)
    mixed_ref[:, 2 * cols :] = d_value[...].astype(low)
    mixed = mixed_ref[...]
    mixed_sums = jnp.sum(mixed.astype(f32), 0, keepdims=True)
    gain_sum = jnp.zeros((1, width), f32)
    shift_sum = jnp.zeros((1, width), f32)
    for t in range(seq // tile):
        grad = contract(mixed_ref[t * tile : (t + 1) * tile, :], w_ref[...], 1, 1)
        field = x_ref[t * tile : (t + 1) * tile, :].astype(f32)
        center = field - jnp.mean(field, -1, keepdims=True)
        unit = center * lax.rsqrt(jnp.mean(center * center, -1, keepdims=True) + norm_eps)
        gain_sum = gain_sum + jnp.sum(grad * unit, 0, keepdims=True)
        shift_sum = shift_sum + jnp.sum(grad, 0, keepdims=True)
        moved[t * tile : (t + 1) * tile, :] = grad.astype(low)
    n_line = spans // 4
    cut = keep_a.shape[2]
    for y, (ref_a, ref_b) in enumerate(((keep_a, keep_b), (give_a, give_b))):
        for z in range(n_line):
            for u in range(2):
                part = pl.ds(pl.multiple_of(table[(y * n_line + z) * 2 + u] * half, half), half)
                to = slice(u * half, (u + 1) * half)
                ref_a[z, to, :] = moved[part, :cut]
                ref_b[z, to, :] = moved[part, cut:]
    row = lax.broadcasted_iota(jnp.int32, (8, width), 0)
    sums = jnp.where(row == 0, gain_sum, jnp.where(row == 1, shift_sum, sums_ref[...]))
    here = table[2 * spans + 4]
    small = lax.broadcasted_iota(jnp.int32, (8, cols), 0)
    bias = jnp.where(small == 4, mixed_sums[:, :cols], jnp.where(small == 5, mixed_sums[:, 2 * cols :], 0.0))
    terms = contract(mixed, normed[...], 0, 0)
    blank = jnp.zeros((rows - 8, cols), f32)
    for c in range(n_ctx):
        part = terms[:, c * 4 * rows : (c + 1) * 4 * rows].T.astype(low)
        block = sums[:, c * cols : (c + 1) * cols] + jnp.where(here == c, bias, 0.0)
        block = jnp.concatenate([block, blank], 0).astype(low)
        for f in range(4):
            made[(c * 4 + f) * rows : (c * 4 + f + 1) * rows, : 3 * cols] = part[f * rows : (f + 1) * rows]
            made[(c * 4 + f) * rows : (c * 4 + f + 1) * rows, 3 * cols :] = block
    at = 2 * spans + 5
    for which, ref in enumerate((keep_ref, give_ref)):
        for x in range(2):
            f = lax.rem(table[at + 2] + x, 2) * 2 + lax.rem(table[at + 3] + which, 2)
            for c in range(n_ctx):
                ref[x, c] = made[pl.ds(pl.multiple_of((c * 4 + f) * rows, rows), rows), :]


def square_kernel(table, qkv_ref, ff_ref, own_out, *refs):
    f32 = jnp.float32
    others, (square_ref, out_ref, vec_ref) = refs[:-3], refs[-3:]
    n_ctx, rows, wide = qkv_ref.shape
    cols = wide // 4
    at = 4 * n_ctx + 5
    out = own_out[...].astype(f32)
    for other in others:
        out = out + other[...].astype(f32)
    out_ref[...] = out
    small = jnp.sum(qkv_ref[:, :, 3 * cols :].astype(f32), 0)[:8]
    mine = table[at + 2] * 2 + table[at + 3]
    picked = jnp.zeros((8, rows), f32)
    for f in range(4):
        picked = picked + jnp.where(mine == f, small[:, f * rows : (f + 1) * rows], 0.0)
    vec_ref[...] = picked
    n_ff = ff_ref.shape[0] - 16
    bias = ff_ref[n_ff:, : 4 * rows].astype(f32)[0:1]
    squared = jnp.sum(jnp.square(bias), keepdims=True) + jnp.sum(jnp.square(picked), keepdims=True)
    squared = squared + jnp.sum(jnp.sum(jnp.square(ff_ref[:n_ff, :].astype(f32)), 0, keepdims=True), keepdims=True)
    squared = squared + jnp.sum(jnp.sum(jnp.square(out), 0, keepdims=True), keepdims=True)
    qkv = jnp.sum(jnp.square(qkv_ref[:, :, : 3 * cols].astype(f32)), 0)
    squared = squared + jnp.sum(jnp.sum(qkv, 0, keepdims=True), keepdims=True)
    square_ref[...] = jnp.broadcast_to(squared, square_ref.shape)


def clip_of(squares):
    norm = jnp.sqrt(jnp.sum(jnp.sum(squares[...], 0, keepdims=True)[:, 0:1], keepdims=True))
    return norm, jnp.minimum(1.0, max_norm / (norm + 1e-06))


def adam_put(refs, spot, grad, clip):
    weight, first, second = refs[:3]
    new = adamw(weight[spot], grad, first[spot], second[spot], clip)
    for ref, value in zip(refs[3:], (grad,) + new):
        ref[spot] = value


def adam_kernel(*refs):
    f32 = jnp.float32
    squares, qkv_ref, out_ref, ff_ref, vec_ref = refs[:5]
    items = [[refs[5 + 5 * m + n] for m in range(3)] + list(refs[21 + 4 * n : 25 + 4 * n]) for n in range(5)]
    norm, clip = clip_of(squares)
    refs[20][...] = norm
    n_ctx, rows, wide = qkv_ref.shape
    cols = wide // 4
    width = n_ctx * cols
    ff = ff_ref.shape[1]
    own = 4 * rows
    n_ff = 8 * rows
    whole = (slice(None), slice(None))
    for c in range(n_ctx):
        for k in range(3):
            spot = (slice(None), slice(k * width + c * cols, k * width + (c + 1) * cols))
            adam_put(items[0], spot, qkv_ref[c, :, k * cols : (k + 1) * cols].astype(f32), clip)
    adam_put(items[1], whole, out_ref[...], clip)
    for h in range(width // ff):
        spot = (slice(None), slice(h * ff, (h + 1) * ff))
        adam_put(items[2], spot, ff_ref[n_ff + h * own : n_ff + (h + 1) * own, :].astype(f32), clip)
    n_down = n_ff + width // ff * own
    adam_put(items[3], whole, ff_ref[n_down:, :own].astype(f32)[0:1], clip)
    adam_put(items[4], whole, vec_ref[...], clip)


def adam_up_kernel(squares, up_ref, *refs):
    _, clip = clip_of(squares)
    n_plane, rows, ff = up_ref.shape
    own = 4 * rows
    for r in range(n_plane):
        for k in range(ff // own):
            spot = (slice(None), slice((k * n_plane + r) * own, (k * n_plane + r + 1) * own))
            adam_put(refs, spot, up_ref[r, :, k * own : (k + 1) * own].astype(jnp.float32), clip)


in_smem = pl.BlockSpec(memory_space=pltpu.SMEM)
in_vmem = pl.BlockSpec(memory_space=pltpu.VMEM)


def call(kernel, n_scalar, args, shapes, scratch=(), cost=1, limit=48):
    return pl.pallas_call(
        kernel,
        out_shape=[jax.ShapeDtypeStruct(s, d) for s, d in shapes],
        in_specs=[in_smem] * n_scalar + [in_vmem] * (len(args) - n_scalar),
        out_specs=[in_vmem] * len(shapes),
        scratch_shapes=[pltpu.VMEM(s, d) for s, d in scratch],
        compiler_params=pltpu.CompilerParams(vmem_limit_bytes=limit * 1024 * 1024),
        cost_estimate=pl.CostEstimate(flops=cost, bytes_accessed=cost, transcendentals=0),
    )(*args)


def attend_forward(table, slopes, blocks, pieces, start, cols):
    tokens, width = blocks[0].shape
    seq = tokens * (len(blocks) - 1)
    f32, low = jnp.float32, jnp.bfloat16
    shapes = [
        ((seq, cols), low), ((cols, seq), f32), ((seq, 3 * cols), low), ((8, seq), f32),
        ((seq, width), low), ((seq, width), low), ((width, 3 * cols), low), ((8, width), f32),
    ]
    args = [table, slopes] + list(blocks) + list(pieces) + [start]
    return call(functools.partial(forward_kernel, len(blocks)), 2, args, shapes, [((width, 128), low)], 9000000000, 60)


def local_split(
    inputs, out_grad, segments, pairs,
    w_qkv, w_out, w_up, w_down, up_bias, vectors,
    first_qkv, first_out, first_up, first_down, first_bias, first_vectors,
    second_qkv, second_out, second_up, second_down, second_bias, second_vectors,
):
    low = jnp.bfloat16
    f32 = jnp.float32
    nz = lax.axis_size("z")
    n_ctx = 2 * nz
    every = ("z", "y", "x", "c")
    ctx = ("z", "y")
    plane = ("y", "x", "c")
    zi, yi, xi, ci = (lax.axis_index(a) for a in every)
    ctx_i = zi * 2 + yi
    tokens, width = inputs.shape[1:]
    half = tokens // 2
    seq_len = tokens * n_ctx
    heads_own = HEADS // n_ctx
    cols = heads_own * HD
    rows = w_qkv.shape[0]
    ff_own = w_down.shape[0]
    ff = nz * ff_own
    n_half = width // ff
    field_low = inputs[0]
    field = field_low.astype(f32)
    cot_low = out_grad[0]

    cut = width - width // 4
    field_cut = field_low[:, :cut]
    line = [shift(field_cut, "z", nz, k) for k in range(1, nz)]
    own_two = exchange(jnp.stack([field_low, cot_low]), "y")
    shapes = [((n_ctx, rows, 3 * cols + 128), low), ((8, rows, ff), low), ((n_half, ff_own, ff), low), ((tokens, width // 4), low)]
    packed = [pairs, w_qkv, vectors, segments, up_bias.reshape(1, ff_own), w_up, w_down, w_out]
    first_send, up_send, down_part, out_low = call(pack_kernel, 1, packed, shapes, limit=60)
    first_got = swap(first_send, ctx)
    up_part = swap(after(up_send, first_got), plane).reshape(8 * rows, ff)
    ff_send = jnp.concatenate([up_part, down_part.reshape(n_half * ff_own, ff)], 0)
    ff_send, first_got, own_two, out_low, *line = gate(ff_send, first_got, own_two, out_low, *line)
    pair_own, cot_y = own_two[0], own_two[1]

    ff_all = lax.all_gather(ff_send, "z", axis=0)
    pair_line = exchange(jnp.stack(line), "y")
    rest_own = jnp.stack([field_low[:, cut:], pair_own[:, cut:], out_low])
    rest = [shift(rest_own, "z", nz, k) for k in range(1, nz)]
    first_x = exchange(first_got, "x")
    first_c = exchange(first_got, "c")
    first_cx = exchange(first_x, "c")
    cot_two = jnp.stack([cot_low, cot_y])
    cot_x = exchange(cot_two, "x")
    seg_all = first_got[:, 0:2, 3 * cols + 64 :].reshape(seq_len).astype(jnp.int32)
    bias_all = first_got[:, 2:4, 3 * cols + 64 :].reshape(nz, 2, ff_own)
    up_low = lax.dynamic_index_in_dim(bias_all, yi, 1, keepdims=False).reshape(1, ff).astype(f32)
    pair_all = first_got[:, 4, 3 * cols + 64].astype(jnp.int32)
    start = jnp.sum((seg_all[:, None] < seg_all[None, :]).astype(jnp.int32), 0, keepdims=True)
    slot_block = jnp.stack([pair_all, 2 * n_ctx - 1 - pair_all], 1)
    near = [((zi + k) % nz) * 2 + yi for k in range(nz)]
    near = jnp.stack(near + [((zi + k) % nz) * 2 + 1 - yi for k in range(nz)])
    ids = jnp.arange(n_ctx)
    near_block = jnp.sum(jnp.where((near[:, None] == ids[None, :])[:, :, None], slot_block[None], 0), 1)
    spans = jnp.arange(2 * n_ctx)
    block_slot = jnp.sum(jnp.where(slot_block.reshape(1, -1) == spans[:, None], spans[None, :], 0), 1)
    piece_f = jnp.stack([xi * 2 + ci, (1 - xi) * 2 + ci, xi * 2 + 1 - ci, (1 - xi) * 2 + 1 - ci])
    here = jnp.stack([ctx_i, zi, yi, xi, ci])
    table = jnp.concatenate([near_block.reshape(-1), block_slot, piece_f, here]).astype(jnp.int32)
    head_ids = (ctx_i * heads_own + jnp.arange(heads_own)).astype(f32)
    slopes = jnp.exp2(-8.0 * (head_ids + 1.0) / HEADS)
    out_z = jnp.stack([out_low] + [v[2] for v in rest])
    first_x, first_c, first_cx, cot_x, table, start, pair_line, slopes, out_z, *rest = gate(
        first_x, first_c, first_cx, cot_x, table, start, pair_line, slopes, out_z, *rest
    )

    out_y = exchange(out_z, "y")
    cot_c = exchange(cot_two, "c")
    pieces = (first_got, first_x, first_c, first_cx)
    blocks = [field_low, pair_own, pair_line] + line + rest
    attended, att_t, qkv_low, lse, normed_one, seq_rows, qkv_w, vec = attend_forward(
        table, slopes, blocks, pieces, start, cols
    )
    attended, out_y, cot_c = gate(attended.reshape(n_ctx, tokens, cols), out_y, cot_c)

    attended_low = swap(attended, ctx)
    out_zy = jnp.stack([out_z, out_y])
    out_x = exchange(out_zy, "x")
    out_c_two = exchange(out_zy, "c")
    cot_cx = exchange(cot_x, "c")
    attended_low, out_x, out_c_two, cot_cx = gate(attended_low, out_x, out_c_two, cot_cx)
    cots = [cot_two, cot_x, cot_c, cot_cx]
    shapes = [((tokens, width), f32), ((tokens, width), low), ((width, width), low)]
    parts = [table, attended_low, out_zy, out_x, out_c_two, exchange(out_x, "c"), field_low, vec]
    resid, mlp_low, out_w = call(project_kernel, 1, parts, shapes)

    mlp_y = exchange(mlp_low, "y")
    mlp_x = exchange(mlp_low, "x")
    mlp_c = exchange(mlp_low, "c")
    mlp_y, mlp_x, mlp_c = gate(mlp_y, mlp_x, mlp_c)
    mlp_d0 = exchange(mlp_x[:half], "y")
    mlp_d1 = exchange(mlp_y[half:], "x")
    mlp_cyx = exchange(jnp.stack([mlp_y, mlp_x]), "c")
    mlp_cd = exchange(jnp.stack([mlp_d0, mlp_d1]), "c")
    four = ((4, tokens, width), low)
    shapes = [four, four, ((8 * tokens, ff), low), ((8 * tokens, ff), low), ((8 * tokens, width), low)]
    scratch = [((ff, width), low), ((width, ff), low)]
    norm_keep, norm_give, hidden, grad_pre, mlp_in = call(
        feed_kernel,
        0,
        [mlp_low, mlp_y, mlp_x, mlp_d0, mlp_d1, mlp_c, mlp_cyx, mlp_cd] + cots + [ff_all, up_low],
        shapes,
        scratch,
        limit=60,
    )

    n_ff = 8 * rows + n_half * ff_own
    ff_terms = call(
        feed_grad_kernel, 0, [mlp_in, grad_pre, hidden] + cots, [((nz, n_ff + 16, ff), low)], (), 1, 60
    )[0]
    norm_c_got = exchange(norm_give, "c")
    norm_c_got, ff_terms = gate(norm_c_got, ff_terms)
    ff_sum = lax.psum_scatter(ff_terms, "z", scatter_dimension=0, tiled=True)[0]

    norm_d0 = exchange(add_low(norm_keep[3, :half], norm_c_got[3, :half]), "y")
    norm_d1 = exchange(add_low(norm_keep[3, half:], norm_c_got[3, half:]), "x")
    norm_own, norm_y, norm_x = (add_low(norm_keep[k], norm_c_got[k]) for k in range(3))
    norm_d0, norm_d1, norm_own, norm_y, norm_x = gate(norm_d0, norm_d1, norm_own, norm_y, norm_x)
    norm_y = exchange(jnp.concatenate([norm_y[:half], add_low(norm_y[half:], norm_d1)], 0), "y")
    norm_x = exchange(jnp.concatenate([add_low(norm_x[:half], norm_d0), norm_x[half:]], 0), "x")
    result_keep, result_give = call(
        result_kernel, 0, [after(hidden, norm_d0), ff_all], [four, four], [((ff, width), low)]
    )
    norm_x, norm_y, result_keep, result_give = gate(norm_x, norm_y, result_keep, result_give)
    shapes = [((tokens, width), f32), ((n_ctx, tokens, cols), low), ((8, width), f32)]
    shapes = shapes + [((2, 2, nz, rows, width), low)] * 2
    grad_resid, back_low, resid_sums, out_keep, out_give = call(
        norm_back_kernel,
        1,
        [table, norm_own, norm_x, norm_y, resid, cot_low, vec, out_w, attended_low],
        shapes,
        [((width, width), low)],
    )

    back_all = swap(back_low, ctx)
    out_c_got = exchange(out_give, "c")
    result_c_got = exchange(result_give, "c")
    back_all, out_c_got, result_c_got = gate(back_all, out_c_got, result_c_got)

    out_x_got = exchange(add_low(out_keep[1], out_c_got[1]), "x")
    shapes = [((2, n_ctx, rows, 4 * cols), low)] * 2
    part = width // 2
    shapes = shapes + [((nz, tokens, part), low)] * 2 + [((nz, tokens, width - part), low)] * 2
    scratch = [((seq_len, 3 * cols), low), ((seq_len, cols), low), ((seq_len, cols), f32), ((seq_len, cols), f32)]
    scratch = scratch + [((seq_len, width), low), ((width, 4 * cols), low)]
    back_all = back_all.reshape(seq_len, cols)
    made = call(
        backward_kernel,
        2,
        [table, slopes, back_all, qkv_low, att_t, lse, start, normed_one, qkv_w, seq_rows, resid_sums],
        shapes,
        scratch,
        9000000000,
        60,
    )
    *made, out_x_got = gate(*made, out_x_got)
    qkv_keep, qkv_give = made[:2]
    in_keep, in_give = made[2::2], made[3::2]

    qkv_c_got = exchange(qkv_give, "c")
    qkv_c = add_low(qkv_keep[0], qkv_c_got[0])
    qkv_x_got = exchange(add_low(qkv_keep[1], qkv_c_got[1]), "x")
    out_c = add_low(out_keep[0], out_c_got[0])
    out_two = add_low(out_c[0], out_x_got[0])
    out_y_got = exchange(add_low(out_c[1], out_x_got[1]), "y")
    in_a = exchange(after(in_give[0], qkv_c), "y")
    result_send = add_low(result_keep[2:], result_c_got[2:])
    result_x = exchange(after(result_send, qkv_c), "x")
    qkv_x_got, qkv_c, out_y_got, result_send = gate(qkv_x_got, qkv_c, out_y_got, result_send)
    qkv_x = add_low(qkv_c, qkv_x_got)

    qkv_got = swap(qkv_x, ctx)
    out_own = add_low(out_two[0], out_y_got[0])
    out_moved = [shift(add_low(out_two[k], out_y_got[k]), "z", nz, -k) for k in range(1, nz)]
    in_b = exchange(after(in_give[1], qkv_c), "y")
    in_a = after(in_a, qkv_x)
    in_za = [shift(add_low(in_keep[0][k], in_a[k]), "z", nz, -k) for k in range(1, nz)]
    up_send = after(ff_sum, qkv_x)[: 8 * rows].reshape(8, rows, ff)
    result_x = after(result_x, qkv_x)
    result_c = add_low(result_keep[:2], result_c_got[:2])
    result_y = exchange(add_low(result_c[1], result_x[1]), "y")
    qkv_got, in_b, up_send, *gated = gate(qkv_got, in_b, up_send, *out_moved, out_own)
    out_moved = gated[: nz - 1]
    shapes = [((8, 128), f32), ((rows, width), f32), ((8, rows), f32)]
    squared, grad_out_own, grad_vec_own = call(
        square_kernel, 1, [table, qkv_got, ff_sum, out_own, *out_moved], shapes
    )

    squares = swap(jnp.broadcast_to(squared[:1], (4 * n_ctx, 128)), every)
    in_zb = [shift(add_low(in_keep[1][k], in_b[k]), "z", nz, -k) for k in range(1, nz)]
    result_y = after(result_y, squared)
    result = resid + result_c[0].astype(f32) + result_x[0].astype(f32) + result_y.astype(f32) + vec[7]
    result, squares = gate(result.astype(low), squares)
    up_got = swap(after(up_send, squares), plane)
    masters = [w_qkv, w_out, w_down, up_bias.reshape(1, ff_own), vectors]
    firsts = [first_qkv, first_out, first_down, first_bias.reshape(1, ff_own), first_vectors]
    seconds = [second_qkv, second_out, second_down, second_bias.reshape(1, ff_own), second_vectors]
    shapes = [((1, 1), f32)]
    for item in masters:
        shapes = shapes + [(item.shape, f32)] * 4
    grads = [squares, qkv_got, grad_out_own, ff_sum, grad_vec_own]
    grad_norm, *results = call(adam_kernel, 0, grads + masters + firsts + seconds, shapes, limit=60)
    for k in range(12, 16):
        results[k] = results[k].reshape(ff_own)
    ups = call(adam_up_kernel, 0, [squares, up_got, w_up, first_up, second_up], [(w_up.shape, f32)] * 4, limit=60)
    results = results[:8] + list(ups) + results[8:]

    *late, _ = gate(*in_za, *in_zb, grad_norm)
    sum_a = in_keep[0][0].astype(f32) + in_a[0].astype(f32)
    sum_b = in_keep[1][0].astype(f32) + in_b[0].astype(f32)
    for k in range(nz - 1):
        sum_a = sum_a + late[k].astype(f32)
        sum_b = sum_b + late[nz - 1 + k].astype(f32)
    own_grads = jnp.concatenate([sum_a, sum_b], 1)
    norm_one_back = jax.vjp(lambda v: layer_norm(v, vec[0], vec[1]), field)[1]
    in_grad = grad_resid + norm_one_back(own_grads)[0]
    return (result[None], in_grad[None], grad_norm[0, 0], *results)


def solution(mesh):
    n_ctx = mesh.shape["ctx"]
    if HEADS % n_ctx == 0 and n_ctx % 2 == 0 and mesh.shape["fsdp"] == 4:
        body = local_split
        ctx, fsdp = ("z", "y"), ("x", "c")
        mesh = Mesh(mesh.devices.reshape(n_ctx // 2, 2, 2, 2), ctx + fsdp)
    else:
        body = local
        ctx, fsdp = ("ctx",), ("fsdp",)
    rows = P(fsdp, ctx, None)
    flat = P(fsdp, ctx)
    mat = P(ctx + fsdp, None)
    vec = P(ctx + fsdp)
    wide = P(None, ctx + fsdp)
    group = (mat, mat, mat, mat, vec, wide)
    outs = ()
    for spec in group:
        outs = outs + (spec,) * 4
    return jax.shard_map(
        body,
        mesh=mesh,
        in_specs=(rows, rows, flat, flat) + group * 3,
        out_specs=(rows, rows, P()) + outs,
        check_vma=False,
    )
```

```python
import functools
import math

import jax
import jax.numpy as jnp
from jax import lax
from jax.experimental import pallas as pl
from jax.experimental.pallas import tpu as pltpu
from jax.sharding import Mesh
from jax.sharding import PartitionSpec as P

HEADS = 16
HD = 64


norm_eps = 1e-05
beta_one = 0.9
beta_two = 0.95
adam_eps = 1e-08
learn_rate = 0.02
weight_decay = 0.1
adam_step = 10
max_norm = 1.0
masked = -1e30
group_heads = 2


def layer_norm(field, gain, shift):
    center = field - jnp.mean(field, -1, keepdims=True)
    spread = jnp.mean(center * center, -1, keepdims=True)
    return center * lax.rsqrt(spread + norm_eps) * gain + shift


def gelu_exact(field):
    return jax.nn.gelu(field, approximate=False)


def contract(left, right, left_dim, right_dim):
    return lax.dot_general(
        left, right, (((left_dim,), (right_dim,)), ((), ())), preferred_element_type=jnp.float32
    )


def place(pair_ids, block, n_ctx):
    blocks = jnp.stack([pair_ids, 2 * n_ctx - 1 - pair_ids], 1).reshape(-1)
    offsets = jnp.arange(block, dtype=jnp.int32)
    return (blocks[:, None] * block + offsets[None, :]).reshape(-1)


def pick(array, first):
    return lax.dynamic_slice_in_dim(array, first, group_heads, 1)


def adamw(weight, grad, first, second, clip):
    clipped = grad * clip
    first_new = beta_one * first + (1.0 - beta_one) * clipped
    second_new = beta_two * second + (1.0 - beta_two) * clipped * clipped
    first_hat = first_new / (1.0 - beta_one**adam_step)
    second_hat = second_new / (1.0 - beta_two**adam_step)
    update = -learn_rate * (first_hat / (jnp.sqrt(second_hat) + adam_eps) + weight_decay * weight)
    return (update, first_new, second_new)


def local(
    inputs,
    out_grad,
    segments,
    pairs,
    w_qkv,
    w_out,
    w_up,
    w_down,
    up_bias,
    vectors,
    first_qkv,
    first_out,
    first_up,
    first_down,
    first_bias,
    first_vectors,
    second_qkv,
    second_out,
    second_up,
    second_down,
    second_bias,
    second_vectors,
):
    low_type = jnp.bfloat16
    n_ctx = lax.axis_size("ctx")
    field = inputs[0].astype(jnp.float32)
    tokens = field.shape[0]
    block = tokens // 2
    width = field.shape[1]
    seq_len = tokens * n_ctx
    scale = HD ** (-0.5)
    groups = HEADS // group_heads
    slope = 2.0 ** (-8.0 * (jnp.arange(HEADS, dtype=jnp.float32) + 1.0) / HEADS)
    qkv_w, out_w, vec_low = (
        lax.all_gather(w_qkv.astype(low_type), ("ctx", "fsdp"), axis=0, tiled=True),
        lax.all_gather(w_out.astype(low_type), ("ctx", "fsdp"), axis=0, tiled=True),
        lax.all_gather(vectors.astype(low_type), ("ctx", "fsdp"), axis=1, tiled=True),
    )
    vec = vec_low.astype(jnp.float32)
    gain_one, shift_one, gain_two, shift_two = (vec[0], vec[1], vec[2], vec[3])
    bias_query, bias_value, bias_out, bias_down = (vec[4], vec[5], vec[6], vec[7])
    normed_one = layer_norm(field, gain_one, shift_one)
    attn_in = normed_one.astype(low_type)
    mixed = jnp.dot(attn_in, qkv_w, preferred_element_type=jnp.float32)
    query = (mixed[:, :width] + bias_query).astype(low_type)
    keys = mixed[:, width : 2 * width].astype(low_type)
    values = (mixed[:, 2 * width :] + bias_value).astype(low_type)
    pair_ids = pairs[0]
    kv_all, pair_all, seg_all = (
        lax.all_gather(jnp.concatenate([keys, values], 1), "ctx", axis=0, tiled=True),
        lax.all_gather(pair_ids, "ctx", axis=0, tiled=True),
        lax.all_gather(segments[0], "ctx", axis=0, tiled=True),
    )
    pos_query = place(pair_ids, block, n_ctx)
    pos_key = place(pair_all, block, n_ctx)
    seg_query = jnp.take(seg_all, pos_query)
    seg_key = jnp.take(seg_all, pos_key)
    relative = (pos_key[None, :] - pos_query[:, None]).astype(jnp.float32)
    allowed = (seg_query[:, None] == seg_key[None, :]) & (pos_key[None, :] <= pos_query[:, None])
    query_heads = query.reshape(tokens, HEADS, HD)
    key_heads = kv_all[:, :width].reshape(seq_len, HEADS, HD)
    value_heads = kv_all[:, width:].reshape(seq_len, HEADS, HD)

    def scores_of(query_part, key_part, first, offsets, visible):
        slopes = lax.dynamic_slice_in_dim(slope, first, group_heads, 0)
        raw = (
            jnp.einsum("rhe,khe->hrk", query_part, key_part, preferred_element_type=jnp.float32)
            * scale
        )
        raw = raw + slopes[:, None, None] * offsets[None]
        return jnp.where(visible[None], raw, masked)

    def forward_group(index, carry):
        attended, log_total = carry
        first = index * group_heads
        scores = scores_of(
            pick(query_heads, first), pick(key_heads, first), first, relative, allowed
        )
        top = jnp.max(scores, -1, keepdims=True)
        expo = jnp.exp(scores - top)
        total = jnp.sum(expo, -1, keepdims=True)
        chance_low = (expo / total).astype(low_type)
        part_out = jnp.einsum(
            "hrk,khe->rhe", chance_low, pick(value_heads, first), preferred_element_type=jnp.float32
        )
        attended = lax.dynamic_update_slice_in_dim(attended, part_out, first, 1)
        log_total = lax.dynamic_update_slice_in_dim(
            log_total, (top + jnp.log(total))[:, :, 0].T, first, 1
        )
        return (attended, log_total)

    attended, log_total = lax.fori_loop(
        0,
        groups,
        forward_group,
        (jnp.zeros((tokens, HEADS, HD), jnp.float32), jnp.zeros((tokens, HEADS), jnp.float32)),
    )
    attended_low = attended.reshape(tokens, width).astype(low_type)
    resid = field + jnp.dot(attended_low, out_w, preferred_element_type=jnp.float32) + bias_out
    normed_two = layer_norm(resid, gain_two, shift_two)
    mlp_in = normed_two.astype(low_type)
    up_w, down_w, up_low = (
        lax.all_gather(w_up.astype(low_type), ("ctx", "fsdp"), axis=0, tiled=True),
        lax.all_gather(w_down.astype(low_type), ("ctx", "fsdp"), axis=0, tiled=True),
        lax.all_gather(up_bias.astype(low_type), ("ctx", "fsdp"), axis=0, tiled=True),
    )
    pre = jnp.dot(mlp_in, up_w, preferred_element_type=jnp.float32) + up_low.astype(jnp.float32)
    hidden = gelu_exact(pre).astype(low_type)
    result = resid + jnp.dot(hidden, down_w, preferred_element_type=jnp.float32) + bias_down
    cotangent_low = out_grad[0]
    cotangent = cotangent_low.astype(jnp.float32)
    up_back, down_back = (
        lax.all_gather(w_up.astype(low_type), ("ctx", "fsdp"), axis=0, tiled=True),
        lax.all_gather(w_down.astype(low_type), ("ctx", "fsdp"), axis=0, tiled=True),
    )
    grad_down_term = contract(hidden, cotangent_low, 0, 0)
    grad_bias_down = jnp.sum(cotangent, 0)
    grad_hidden = contract(cotangent_low, down_back, 1, 1)
    gelu_back = jax.vjp(gelu_exact, pre)[1]
    grad_pre = gelu_back(grad_hidden)[0].astype(low_type)
    grad_up_bias = jnp.sum(grad_pre.astype(jnp.float32), 0)
    grad_up_term = contract(mlp_in, grad_pre, 0, 0)
    grad_normed_two = contract(grad_pre, up_back, 1, 1)
    norm_two_back = jax.vjp(layer_norm, resid, gain_two, shift_two)[1]
    grad_resid_norm, grad_gain_two, grad_shift_two = norm_two_back(grad_normed_two)
    grad_resid = cotangent + grad_resid_norm
    grad_up_own, grad_down_own, grad_bias_own = (
        lax.psum_scatter(grad_up_term, ("ctx", "fsdp"), scatter_dimension=0, tiled=True),
        lax.psum_scatter(grad_down_term, ("ctx", "fsdp"), scatter_dimension=0, tiled=True),
        lax.psum_scatter(grad_up_bias, ("ctx", "fsdp"), scatter_dimension=0, tiled=True),
    )
    qkv_back, out_back = (
        lax.all_gather(w_qkv.astype(low_type), ("ctx", "fsdp"), axis=0, tiled=True),
        lax.all_gather(w_out.astype(low_type), ("ctx", "fsdp"), axis=0, tiled=True),
    )
    grad_bias_out = jnp.sum(grad_resid, 0)
    resid_low = grad_resid.astype(low_type)
    grad_out_term = contract(attended_low, resid_low, 0, 0)
    back_low = contract(resid_low, out_back, 1, 1).astype(low_type)
    back_heads = back_low.reshape(tokens, HEADS, HD)

    def backward_group(index, carry):
        grad_query, grad_key, grad_value = carry
        first = index * group_heads
        query_part = pick(query_heads, first)
        key_part = pick(key_heads, first)
        value_part = pick(value_heads, first)
        back_part = pick(back_heads, first)
        scores = scores_of(query_part, key_part, first, relative, allowed)
        logsum = lax.dynamic_slice_in_dim(log_total, first, group_heads, 1).T
        chance = jnp.exp(scores - logsum[:, :, None])
        pushed = jnp.einsum(
            "rhe,khe->hrk", back_part, value_part, preferred_element_type=jnp.float32
        )
        centre = jnp.sum(chance * pushed, -1, keepdims=True)
        dscore = (chance * (pushed - centre)).astype(low_type)
        chance_low = chance.astype(low_type)
        part_query = (
            jnp.einsum("hrk,khe->rhe", dscore, key_part, preferred_element_type=jnp.float32) * scale
        )
        part_key = (
            jnp.einsum("hrk,rhe->khe", dscore, query_part, preferred_element_type=jnp.float32)
            * scale
        )
        part_value = jnp.einsum(
            "hrk,rhe->khe", chance_low, back_part, preferred_element_type=jnp.float32
        )
        grad_query = lax.dynamic_update_slice_in_dim(grad_query, part_query, first, 1)
        grad_key = lax.dynamic_update_slice_in_dim(grad_key, part_key, first, 1)
        grad_value = lax.dynamic_update_slice_in_dim(grad_value, part_value, first, 1)
        return (grad_query, grad_key, grad_value)

    zero_keys = jnp.zeros((seq_len, HEADS, HD), jnp.float32)
    grad_query, grad_key, grad_value = lax.fori_loop(
        0,
        groups,
        backward_group,
        (jnp.zeros((tokens, HEADS, HD), jnp.float32), zero_keys, zero_keys),
    )
    own_key, own_value = (
        lax.psum_scatter(
            grad_key.reshape(seq_len, width).astype(jnp.bfloat16),
            "ctx",
            scatter_dimension=0,
            tiled=True,
        ).astype(jnp.float32),
        lax.psum_scatter(
            grad_value.reshape(seq_len, width).astype(jnp.bfloat16),
            "ctx",
            scatter_dimension=0,
            tiled=True,
        ).astype(jnp.float32),
    )
    grad_query_low = grad_query.reshape(tokens, width).astype(low_type)
    grad_key_low = own_key.astype(low_type)
    grad_value_low = own_value.astype(low_type)
    grad_mixed = jnp.concatenate([grad_query_low, grad_key_low, grad_value_low], 1)
    grad_bias_query = jnp.sum(grad_query_low.astype(jnp.float32), 0)
    grad_bias_value = jnp.sum(grad_value_low.astype(jnp.float32), 0)
    grad_qkv_term = contract(attn_in, grad_mixed, 0, 0)
    grad_normed_one = contract(grad_mixed, qkv_back, 1, 1)
    norm_one_back = jax.vjp(layer_norm, field, gain_one, shift_one)[1]
    grad_field_norm, grad_gain_one, grad_shift_one = norm_one_back(grad_normed_one)
    in_grad = grad_resid + grad_field_norm
    grad_vec_term = jnp.stack(
        [
            grad_gain_one,
            grad_shift_one,
            grad_gain_two,
            grad_shift_two,
            grad_bias_query,
            grad_bias_value,
            grad_bias_out,
            grad_bias_down,
        ],
        0,
    )
    grad_qkv_own, grad_out_own, grad_vec_own = (
        lax.psum_scatter(grad_qkv_term, ("ctx", "fsdp"), scatter_dimension=0, tiled=True),
        lax.psum_scatter(grad_out_term, ("ctx", "fsdp"), scatter_dimension=0, tiled=True),
        lax.psum_scatter(grad_vec_term, ("ctx", "fsdp"), scatter_dimension=1, tiled=True),
    )
    grads = (grad_qkv_own, grad_out_own, grad_up_own, grad_down_own, grad_bias_own, grad_vec_own)
    local_squares = sum([jnp.sum(item * item) for item in grads])
    grad_norm = jnp.sqrt(lax.psum(local_squares, ("ctx", "fsdp")))
    clip = jnp.minimum(1.0, max_norm / (grad_norm + 1e-06))
    masters = (w_qkv, w_out, w_up, w_down, up_bias, vectors)
    firsts = (first_qkv, first_out, first_up, first_down, first_bias, first_vectors)
    seconds = (second_qkv, second_out, second_up, second_down, second_bias, second_vectors)
    results = []
    for weight, grad, first, second in zip(masters, grads, firsts, seconds):
        update, first_new, second_new = adamw(weight, grad, first, second, clip)
        results = results + [grad, update, first_new, second_new]
    return (
        result.astype(low_type)[None],
        in_grad[None],
        grad_norm,
        results[0],
        results[1],
        results[2],
        results[3],
        results[4],
        results[5],
        results[6],
        results[7],
        results[8],
        results[9],
        results[10],
        results[11],
        results[12],
        results[13],
        results[14],
        results[15],
        results[16],
        results[17],
        results[18],
        results[19],
        results[20],
        results[21],
        results[22],
        results[23],
    )


def exchange(v, axis):
    return lax.ppermute(v, axis, [(0, 1), (1, 0)])


def shift(v, axis, n_line, k):
    return lax.ppermute(v, axis, [(i, (i - k) % n_line) for i in range(n_line)])


def swap(v, axes):
    return lax.all_to_all(v, axes, 0, 0, tiled=True)


def gate(*values):
    return lax.optimization_barrier(values)


def after(v, *others):
    return lax.optimization_barrier((v,) + others)[0]


def order_two(own, other, axis, dim):
    first = lax.axis_index(axis) == 0
    return jnp.stack([jnp.where(first, own, other), jnp.where(first, other, own)], dim)


def split_two(part, axis, dim):
    me = lax.axis_index(axis)
    keep = lax.dynamic_index_in_dim(part, me, dim, keepdims=False)
    return keep, lax.dynamic_index_in_dim(part, 1 - me, dim, keepdims=False)


def add_low(keep, got):
    return (keep.astype(jnp.float32) + got.astype(jnp.float32)).astype(jnp.bfloat16)


def line_gives(part, axis, n_line):
    me = lax.axis_index(axis)
    blocks = [lax.dynamic_index_in_dim(part, (me + k) % n_line, 0, keepdims=False) for k in range(n_line)]
    return blocks[0], [shift(blocks[k], axis, n_line, -k) for k in range(1, n_line)]


def line_order(parts, axis):
    n_line = len(parts)
    first = (n_line - lax.axis_index(axis)) % n_line
    return lax.dynamic_slice_in_dim(jnp.concatenate([jnp.stack(parts)] * 2, 0), first, n_line, 0)


def lanes_of(head, shape):
    return lax.broadcasted_iota(jnp.int32, shape, 1) // HD == head


def head_parts(query, keys, slope, head):
    seq = keys.shape[0]
    lane = lax.broadcasted_iota(jnp.int32, keys.shape, 1)
    own = lane // HD == head
    spot = lane - (1 - head) * HD
    bias = lax.broadcasted_iota(jnp.int32, (seq, 1), 0).astype(jnp.float32) * (slope * HD**0.5)
    high = bias.astype(jnp.bfloat16)
    rest = bias - high.astype(jnp.float32)
    middle = rest.astype(jnp.bfloat16)
    small = (rest - middle.astype(jnp.float32)).astype(jnp.bfloat16)
    zero = jnp.zeros_like(keys)
    extra = jnp.where(spot == 0, high, jnp.where(spot == 1, middle, jnp.where(spot == 2, small, zero)))
    ones = jnp.where((spot >= 0) & (spot <= 2), jnp.ones_like(keys), zero)
    return jnp.where(own, query, ones), jnp.where(own, keys, extra)


def visible(start, tile, at, size):
    key = lax.broadcasted_iota(jnp.int32, (size, tile), 0)
    seen = key >= start
    return seen & (key <= lax.broadcasted_iota(jnp.int32, (size, tile), 1) + at)


def forward_kernel(n_refs, meta, slopes, *refs):
    pieces = refs[n_refs : n_refs + 4]
    start_ref = refs[n_refs + 4]
    att_ref, att_t, qkv_ref, lse_ref, normed, x_ref, w_ref, vec_ref, extra = refs[n_refs + 5 :]
    n_line = (n_refs - 3) // 2 + 1
    own, pair, pair_line = refs[0], refs[1], refs[2]
    line, rest = refs[3 : 2 + n_line], refs[2 + n_line : 1 + 2 * n_line]
    n_blocks = 2 * n_line
    cut = line[0].shape[1]

    def block_part(b, span):
        z, other = b % n_line, b // n_line
        if z == 0:
            return (pair if other else own)[span, :]
        first = pair_line[z - 1, span, :] if other else line[z - 1][span, :]
        return jnp.concatenate([first, rest[z - 1][other, span, :]], 1)

    f32, low = jnp.float32, jnp.bfloat16
    n_ctx, rows, _ = pieces[0].shape
    tokens, width = own.shape
    half = tokens // 2
    seq = tokens * n_blocks
    cols = qkv_ref.shape[1] // 3
    spans = 2 * n_blocks
    for c in range(n_ctx):
        for p in range(4):
            piece = pieces[p][c]
            to = pl.ds(pl.multiple_of(c * 4 * rows + meta[2 * spans + p] * rows, rows), rows)
            w_ref[to, :] = piece[:, : 3 * cols]
            extra[to, :] = piece[:, 3 * cols :]
    pick_rows = (
        lax.broadcasted_iota(jnp.int32, (8, 128), 0) == lax.broadcasted_iota(jnp.int32, (8, 128), 1)
    ).astype(low)
    vec = contract(pick_rows, extra[...], 1, 1)
    vec_ref[...] = vec
    gain, move = vec[0:1], vec[1:2]
    for j in range(spans):
        part = block_part(j // 2, slice((j % 2) * half, (j % 2 + 1) * half))
        to = pl.ds(pl.multiple_of(meta[j] * half, half), half)
        x_ref[to, :] = part
        normed[to, :] = layer_norm(part.astype(f32), gain, move).astype(low)
    at = pl.ds(pl.multiple_of(meta[2 * spans + 4] * cols, cols), cols)
    bias_q, bias_v = vec_ref[4:5, at], vec_ref[5:6, at]
    tile = min(256, seq)
    for t in range(seq // tile):
        span = pl.ds(t * tile, tile)
        mixed = jnp.dot(normed[span, :], w_ref[...], preferred_element_type=f32)
        qkv_ref[span, :cols] = (mixed[:, :cols] + bias_q).astype(low)
        qkv_ref[span, cols : 2 * cols] = mixed[:, cols : 2 * cols].astype(low)
        qkv_ref[span, 2 * cols :] = (mixed[:, 2 * cols :] + bias_v).astype(low)
    factor = HD**-0.5 * 1.4426950408889634
    query, keys, values = qkv_ref[:, :cols], qkv_ref[:, cols : 2 * cols], qkv_ref[:, 2 * cols :]
    lse_ref[...] = jnp.zeros_like(lse_ref)
    for h in range(cols // HD):
        q_h, k_h = head_parts(query, keys, slopes[h], h)
        v_h = jnp.where(lanes_of(h, values.shape), values, jnp.zeros_like(values))
        for t in range(seq // tile):
            size = (t + 1) * tile
            span = slice(t * tile, (t + 1) * tile)
            score = contract(k_h[:size], q_h[span], 1, 1) * factor
            score = jnp.where(visible(start_ref[:, span], tile, t * tile, size), score, masked)
            top = jnp.max(score, 0, keepdims=True)
            expo = jnp.exp2(score - top)
            total = jnp.sum(expo, 0, keepdims=True)
            lse_ref[h : h + 1, span] = top + jnp.log2(total)
            part = contract(v_h[:size], expo.astype(low), 0, 0) / total
            att_t[:, span] = part if h == 0 else att_t[:, span] + part
    for t in range(seq // tile):
        span = slice(t * tile, (t + 1) * tile)
        x_tile = att_t[:, span].T.astype(low)
        for u in range(tile // half):
            b = t * (tile // half) + u
            to = meta[spans + b]
            att_ref[pl.ds(pl.multiple_of(to * half, half), half), :] = x_tile[u * half : (u + 1) * half]


def pack_kernel(pairs, w_qkv, vectors, segments, up_bias, w_up, w_down, w_out, first_ref, up_ref, down_ref, out_ref):
    low, f32 = jnp.bfloat16, jnp.float32
    n_ctx, rows, wide = first_ref.shape
    cols = (wide - 128) // 3
    width = n_ctx * cols
    row = lax.broadcasted_iota(jnp.int32, (rows, 128), 0)
    lane = lax.broadcasted_iota(jnp.int32, (rows, 128), 1)
    one_hot = lax.broadcasted_iota(jnp.int32, (8, 128), 0) == lax.broadcasted_iota(jnp.int32, (8, 128), 1)
    columns = contract(vectors[...].astype(low), one_hot.astype(low), 0, 0)
    seg, bias = segments[...].astype(f32), up_bias[...]
    lines = [pltpu.roll(seg, 64, 1), seg, pltpu.roll(bias, 64, 1), bias]
    extra = jnp.where(lane < 8, columns, 0.0)
    for k in range(4):
        extra = jnp.where((row == k) & (lane >= 64), lines[k], extra)
    extra = jnp.where((row == 4) & (lane >= 64), pairs[0, 0].astype(f32), extra).astype(low)
    for c in range(n_ctx):
        for k in range(3):
            first_ref[c, :, k * cols : (k + 1) * cols] = w_qkv[:, k * width + c * cols : k * width + (c + 1) * cols].astype(low)
        first_ref[c, :, 3 * cols :] = extra
    n_plane, _, ff = up_ref.shape
    own = ff // (n_ctx // 2)
    for r in range(n_plane):
        for k in range(n_ctx // 2):
            up_ref[r, :, k * own : (k + 1) * own] = w_up[:, (k * n_plane + r) * own : (k * n_plane + r + 1) * own].astype(low)
    for k in range(down_ref.shape[0]):
        down_ref[k] = w_down[:, k * ff : (k + 1) * ff].astype(low)
    wide_out = out_ref.shape[1]
    for k in range(out_ref.shape[0] // rows):
        out_ref[k * rows : (k + 1) * rows, :] = w_out[:, k * wide_out : (k + 1) * wide_out].astype(low)


def project_kernel(table, att, own_ref, x_ref, c_ref, cx_ref, field, vec, resid_ref, mlp_ref, w_ref):
    low, f32 = jnp.bfloat16, jnp.float32
    n_ctx, tokens, cols = att.shape
    n_line = own_ref.shape[1]
    rows = w_ref.shape[0] // (8 * n_line)
    wide = own_ref.shape[3]
    at = 4 * n_ctx + 5
    zi, yi, xi, ci = (table[at + k] for k in range(4))
    for q, ref in enumerate((own_ref, x_ref, c_ref, cx_ref)):
        for p in range(2):
            for k in range(n_line):
                z = lax.rem(zi + k, n_line)
                y = lax.rem(yi + p, 2)
                x = lax.rem(xi + q % 2, 2)
                to = ((z * 2 + y) * 4 + x * 2 + lax.rem(ci + q // 2, 2)) * rows
                for part in range(tokens // rows):
                    spot = (pl.ds(pl.multiple_of(to, rows), rows), slice(part * wide, (part + 1) * wide))
                    w_ref[spot] = ref[p, k, part * rows : (part + 1) * rows, :]
    heads = jnp.concatenate([att[c] for c in range(n_ctx)], 1)
    moved = jnp.dot(heads, w_ref[...], preferred_element_type=f32)
    resid = field[...].astype(f32) + moved + vec[6:7]
    resid_ref[...] = resid
    mlp_ref[...] = layer_norm(resid, vec[2:3], vec[3:4]).astype(low)


def both_down(parts, down):
    ff = down.shape[0] // 2
    n_line = parts[0].shape[0]
    own = ff // n_line
    n_half = down.shape[1] // ff
    up_rows = parts[0].shape[1] - n_half * own
    for c, part in enumerate(parts):
        for k in range(n_line):
            for h in range(n_half):
                rows = slice(up_rows + h * own, up_rows + (h + 1) * own)
                down[c * ff + k * own : c * ff + (k + 1) * own, h * ff : (h + 1) * ff] = part[k, rows, :]


def feed_kernel(
    m_own, m_y, m_x, m_d0, m_d1, cot_0, cot_1, ff_own, ff_other, bias_own, bias_other,
    norm_own, norm_y, norm_x, norm_d, hidden_ref, pre_ref, mlp_ref, down, up,
):
    low, f32 = jnp.bfloat16, jnp.float32
    tokens, width = m_own.shape
    half = tokens // 2
    n_line, _, ff = ff_own.shape
    up_rows = width // n_line
    for c, part in enumerate((ff_own, ff_other)):
        for k in range(n_line):
            up[k * up_rows : (k + 1) * up_rows, c * ff : (c + 1) * ff] = part[k, :up_rows, :]
    both_down((ff_own, ff_other), down)
    bias = jnp.concatenate([bias_own[...], bias_other[...]], 1)
    for n, block in enumerate((m_own, m_y, m_x)):
        mlp_ref[n * tokens : (n + 1) * tokens, :] = block[...]
    mlp_ref[3 * tokens : 3 * tokens + half, :] = m_d0[...]
    mlp_ref[3 * tokens + half :, :] = m_d1[...]
    for t in range(2):
        span = slice(2 * t * tokens, 2 * (t + 1) * tokens)
        cot = (cot_0, cot_1)[t][...].reshape(2 * tokens, width)
        grads = []
        for c in range(2):
            cut = slice(c * ff, (c + 1) * ff)
            pre = jnp.dot(mlp_ref[span, :], up[:, cut], preferred_element_type=f32) + bias[:, cut]
            cdf = 0.5 * (1.0 + lax.erf(pre * 0.7071067811865476))
            pdf = jnp.exp(-0.5 * pre * pre) * 0.3989422804014327
            hidden_ref[span, cut] = (pre * cdf).astype(low)
            grad = (contract(cot, down[cut, :], 1, 1) * (cdf + pre * pdf)).astype(low)
            pre_ref[span, cut] = grad
            grads = grads + [grad]
        part = contract(jnp.concatenate(grads, 1), up[...], 1, 1).astype(low)
        first, second = ((norm_own, norm_y), (norm_x, norm_d))[t]
        first[...] = part[:tokens]
        second[...] = part[tokens:]


def feed_grad_kernel(mlp_ref, pre_ref, hidden_ref, cot_0, cot_1, keep_ref, give_ref):
    low, f32 = jnp.bfloat16, jnp.float32
    seq, width = mlp_ref.shape
    n_line, _, ff = keep_ref.shape
    own, up_rows, n_half = ff // n_line, width // n_line, width // ff
    cot = jnp.concatenate([ref[...].reshape(seq // 2, width) for ref in (cot_0, cot_1)], 0)
    for c, ref in enumerate((keep_ref, give_ref)):
        cut = slice(c * ff, (c + 1) * ff)
        down = contract(hidden_ref[:, cut], cot, 0, 0).astype(low)
        sums = jnp.sum(pre_ref[:, cut].astype(f32), 0, keepdims=True)
        pad = ref.shape[1] - up_rows - n_half * own
        up = contract(mlp_ref[...], pre_ref[:, cut], 0, 0).astype(low)
        for k in range(n_line):
            ref[k, :up_rows, :] = up[k * up_rows : (k + 1) * up_rows]
            for h in range(n_half):
                part = down[k * own : (k + 1) * own, h * ff : (h + 1) * ff]
                ref[k, up_rows + h * own : up_rows + (h + 1) * own, :] = part
            line = jnp.concatenate([sums[:, k * own : (k + 1) * own], jnp.zeros((1, ff - own), f32)], 1)
            ref[k, up_rows + n_half * own :, :] = jnp.broadcast_to(line, (pad, ff)).astype(low)


def result_kernel(hidden_ref, ff_own, ff_other, keep_ref, give_ref, down):
    both_down((ff_own, ff_other), down)
    half = hidden_ref.shape[0] // 2
    for t, ref in enumerate((keep_ref, give_ref)):
        part = jnp.dot(hidden_ref[t * half : (t + 1) * half, :], down[...], preferred_element_type=jnp.float32)
        ref[...] = part.astype(jnp.bfloat16).reshape(ref.shape)


def norm_back_kernel(
    table, own, got_x, got_y, resid_ref, cot_ref, vec, w_ref, att, grad_ref, back_ref, sums_ref, keep_ref, give_ref, terms
):
    low, f32 = jnp.bfloat16, jnp.float32
    grad = own[...].astype(f32) + got_x[...].astype(f32) + got_y[...].astype(f32)
    resid = resid_ref[...]
    center = resid - jnp.mean(resid, -1, keepdims=True)
    sharp = lax.rsqrt(jnp.mean(center * center, -1, keepdims=True) + norm_eps)
    unit = center * sharp
    scaled = grad * vec[2:3]
    inner = scaled - jnp.mean(scaled, -1, keepdims=True) - unit * jnp.mean(scaled * unit, -1, keepdims=True)
    cot = cot_ref[...].astype(f32)
    total = cot + inner * sharp
    grad_ref[...] = total
    rounded = total.astype(low)
    back = contract(rounded, w_ref[...], 1, 1).astype(low)
    n_ctx, _, cols = back_ref.shape
    for c in range(n_ctx):
        back_ref[c] = back[:, c * cols : (c + 1) * cols]
    row = lax.broadcasted_iota(jnp.int32, sums_ref.shape, 0)
    sums = jnp.where(row == 2, jnp.sum(grad * unit, 0, keepdims=True), 0.0)
    sums = jnp.where(row == 3, jnp.sum(grad, 0, keepdims=True), sums)
    sums = jnp.where(row == 6, jnp.sum(total, 0, keepdims=True), sums)
    sums_ref[...] = jnp.where(row == 7, jnp.sum(cot, 0, keepdims=True), sums)
    for c in range(n_ctx):
        terms[c * cols : (c + 1) * cols, :] = contract(att[c], rounded, 0, 0).astype(low)
    n_line, rows = keep_ref.shape[2:4]
    at = 4 * n_ctx + 5
    for which, ref in enumerate((keep_ref, give_ref)):
        for q in range(4 * n_line):
            x, y, z = q // (2 * n_line), q // n_line % 2, q % n_line
            chip = (lax.rem(table[at] + z, n_line) * 2 + lax.rem(table[at + 1] + y, 2)) * 4
            to = (chip + lax.rem(table[at + 2] + x, 2) * 2 + lax.rem(table[at + 3] + which, 2)) * rows
            ref[x, y, z] = terms[pl.ds(pl.multiple_of(to, rows), rows), :]


def backward_kernel(
    table, slopes, back_ref, qkv_ref, att_t, lse_ref, start_ref, normed, w_ref, x_ref, sums_ref,
    keep_ref, give_ref, in_keep, in_give, mixed_ref, back, d_key, d_value, moved, made,
):
    f32, low = jnp.float32, jnp.bfloat16
    seq, cols = back_ref.shape
    n_ctx, rows = keep_ref.shape[1:3]
    width = w_ref.shape[0]
    spans = 2 * n_ctx
    half = seq // spans
    for b in range(spans):
        back[b * half : (b + 1) * half, :] = back_ref[pl.ds(pl.multiple_of(table[spans + b] * half, half), half), :]
    factor = HD**-0.5 * 1.4426950408889634
    query, keys, values = qkv_ref[:, :cols], qkv_ref[:, cols : 2 * cols], qkv_ref[:, 2 * cols :]
    grads = back[...]
    product = att_t[...] * grads.astype(f32).T
    tile = min(256, seq)
    d_query = [None] * (seq // tile)
    for h in range(cols // HD):
        q_h, k_h = head_parts(query, keys, slopes[h], h)
        own = lanes_of(h, values.shape)
        zero = jnp.zeros_like(values)
        v_h, g_h = jnp.where(own, values, zero), jnp.where(own, grads, zero)
        qq_h, kk_h = jnp.where(own, query, zero), jnp.where(own, keys, zero)
        delta = jnp.sum(product[h * HD : (h + 1) * HD], 0, keepdims=True)
        for t in reversed(range(seq // tile)):
            size = (t + 1) * tile
            span = slice(t * tile, (t + 1) * tile)
            score = contract(k_h[:size], q_h[span], 1, 1) * factor
            score = jnp.where(visible(start_ref[:, span], tile, t * tile, size), score, masked)
            chance = jnp.exp2(score - lse_ref[h : h + 1, span])
            pushed = contract(v_h[:size], g_h[span], 1, 1)
            dscore = (chance * (pushed - delta[:, span])).astype(low)
            part_v = jnp.dot(chance.astype(low), g_h[span], preferred_element_type=f32)
            part_k = jnp.dot(dscore, qq_h[span], preferred_element_type=f32)
            if h == 0 and t == seq // tile - 1:
                d_value[...] = part_v
                d_key[...] = part_k
            else:
                d_value[:size, :] += part_v
                d_key[:size, :] += part_k
            part_q = contract(kk_h[:size], dscore, 0, 0)
            d_query[t] = part_q if h == 0 else d_query[t] + part_q
    scale = HD**-0.5
    for t in range(seq // tile):
        mixed_ref[t * tile : (t + 1) * tile, :cols] = (d_query[t] * scale).T.astype(low)
    mixed_ref[:, cols : 2 * cols] = (d_key[...] * scale).astype(low)
    mixed_ref[:, 2 * cols :] = d_value[...].astype(low)
    mixed = mixed_ref[...]
    mixed_sums = jnp.sum(mixed.astype(f32), 0, keepdims=True)
    gain_sum = jnp.zeros((1, width), f32)
    shift_sum = jnp.zeros((1, width), f32)
    for t in range(seq // tile):
        grad = contract(mixed_ref[t * tile : (t + 1) * tile, :], w_ref[...], 1, 1)
        field = x_ref[t * tile : (t + 1) * tile, :].astype(f32)
        center = field - jnp.mean(field, -1, keepdims=True)
        unit = center * lax.rsqrt(jnp.mean(center * center, -1, keepdims=True) + norm_eps)
        gain_sum = gain_sum + jnp.sum(grad * unit, 0, keepdims=True)
        shift_sum = shift_sum + jnp.sum(grad, 0, keepdims=True)
        moved[t * tile : (t + 1) * tile, :] = grad.astype(low)
    n_line = spans // 4
    for y, ref in enumerate((in_keep, in_give)):
        for z in range(n_line):
            for u in range(2):
                part = pl.ds(pl.multiple_of(table[(y * n_line + z) * 2 + u] * half, half), half)
                ref[z, u * half : (u + 1) * half, :] = moved[part, :]
    row = lax.broadcasted_iota(jnp.int32, (8, width), 0)
    sums = jnp.where(row == 0, gain_sum, jnp.where(row == 1, shift_sum, sums_ref[...]))
    here = table[2 * spans + 4]
    small = lax.broadcasted_iota(jnp.int32, (8, cols), 0)
    bias = jnp.where(small == 4, mixed_sums[:, :cols], jnp.where(small == 5, mixed_sums[:, 2 * cols :], 0.0))
    terms = contract(mixed, normed[...], 0, 0)
    blank = jnp.zeros((rows - 8, cols), f32)
    for c in range(n_ctx):
        part = terms[:, c * 4 * rows : (c + 1) * 4 * rows].T.astype(low)
        block = sums[:, c * cols : (c + 1) * cols] + jnp.where(here == c, bias, 0.0)
        block = jnp.concatenate([block, blank], 0).astype(low)
        for f in range(4):
            made[(c * 4 + f) * rows : (c * 4 + f + 1) * rows, : 3 * cols] = part[f * rows : (f + 1) * rows]
            made[(c * 4 + f) * rows : (c * 4 + f + 1) * rows, 3 * cols :] = block
    at = 2 * spans + 5
    for which, ref in enumerate((keep_ref, give_ref)):
        for x in range(2):
            f = lax.rem(table[at + 2] + x, 2) * 2 + lax.rem(table[at + 3] + which, 2)
            for c in range(n_ctx):
                ref[x, c] = made[pl.ds(pl.multiple_of((c * 4 + f) * rows, rows), rows), :]


def square_kernel(table, qkv_ref, ff_ref, own_out, *refs):
    f32 = jnp.float32
    others, (square_ref, out_ref, vec_ref) = refs[:-3], refs[-3:]
    n_ctx, rows, wide = qkv_ref.shape
    cols = wide // 4
    at = 4 * n_ctx + 5
    out = own_out[...].astype(f32)
    for other in others:
        out = out + other[...].astype(f32)
    out_ref[...] = out
    small = jnp.sum(qkv_ref[:, :, 3 * cols :].astype(f32), 0)[:8]
    mine = table[at + 2] * 2 + table[at + 3]
    picked = jnp.zeros((8, rows), f32)
    for f in range(4):
        picked = picked + jnp.where(mine == f, small[:, f * rows : (f + 1) * rows], 0.0)
    vec_ref[...] = picked
    n_ff = ff_ref.shape[0] - 16
    bias = ff_ref[n_ff:, : 4 * rows].astype(f32)[0:1]
    squared = jnp.sum(jnp.square(bias), keepdims=True) + jnp.sum(jnp.square(picked), keepdims=True)
    squared = squared + jnp.sum(jnp.sum(jnp.square(ff_ref[:n_ff, :].astype(f32)), 0, keepdims=True), keepdims=True)
    squared = squared + jnp.sum(jnp.sum(jnp.square(out), 0, keepdims=True), keepdims=True)
    qkv = jnp.sum(jnp.square(qkv_ref[:, :, : 3 * cols].astype(f32)), 0)
    squared = squared + jnp.sum(jnp.sum(qkv, 0, keepdims=True), keepdims=True)
    square_ref[...] = jnp.broadcast_to(squared.reshape(1, 1, 1), square_ref.shape)


def clip_of(squares):
    norm = jnp.sqrt(jnp.sum(squares[...], 0)[:, 0:1])
    return norm, jnp.minimum(1.0, max_norm / (norm + 1e-06))


def adam_put(refs, spot, grad, clip):
    weight, first, second = refs[:3]
    new = adamw(weight[spot], grad, first[spot], second[spot], clip)
    for ref, value in zip(refs[3:], (grad,) + new):
        ref[spot] = value


def adam_kernel(*refs):
    f32 = jnp.float32
    squares, qkv_ref, out_ref, ff_ref, vec_ref = refs[:5]
    items = [[refs[5 + 5 * m + n] for m in range(3)] + list(refs[21 + 4 * n : 25 + 4 * n]) for n in range(5)]
    norm, clip = clip_of(squares)
    refs[20][...] = norm
    n_ctx, rows, wide = qkv_ref.shape
    cols = wide // 4
    width = n_ctx * cols
    ff = ff_ref.shape[1]
    own = 4 * rows
    n_ff = 8 * rows
    whole = (slice(None), slice(None))
    for c in range(n_ctx):
        for k in range(3):
            spot = (slice(None), slice(k * width + c * cols, k * width + (c + 1) * cols))
            adam_put(items[0], spot, qkv_ref[c, :, k * cols : (k + 1) * cols].astype(f32), clip)
    adam_put(items[1], whole, out_ref[...], clip)
    for h in range(width // ff):
        spot = (slice(None), slice(h * ff, (h + 1) * ff))
        adam_put(items[2], spot, ff_ref[n_ff + h * own : n_ff + (h + 1) * own, :].astype(f32), clip)
    n_down = n_ff + width // ff * own
    adam_put(items[3], whole, ff_ref[n_down:, :own].astype(f32)[0:1], clip)
    adam_put(items[4], whole, vec_ref[...], clip)


def adam_up_kernel(squares, up_ref, *refs):
    _, clip = clip_of(squares)
    n_plane, rows, ff = up_ref.shape
    own = 4 * rows
    for r in range(n_plane):
        for k in range(ff // own):
            spot = (slice(None), slice((k * n_plane + r) * own, (k * n_plane + r + 1) * own))
            adam_put(refs, spot, up_ref[r, :, k * own : (k + 1) * own].astype(jnp.float32), clip)


in_smem = pl.BlockSpec(memory_space=pltpu.SMEM)
in_vmem = pl.BlockSpec(memory_space=pltpu.VMEM)


def call(kernel, n_scalar, args, shapes, scratch=(), cost=1, limit=60):
    return pl.pallas_call(
        kernel,
        out_shape=[jax.ShapeDtypeStruct(s, d) for s, d in shapes],
        in_specs=[in_smem] * n_scalar + [in_vmem] * (len(args) - n_scalar),
        out_specs=[in_vmem] * len(shapes),
        scratch_shapes=[pltpu.VMEM(s, d) for s, d in scratch],
        compiler_params=pltpu.CompilerParams(vmem_limit_bytes=limit * 1024 * 1024),
        cost_estimate=pl.CostEstimate(flops=cost, bytes_accessed=cost, transcendentals=0),
    )(*args)


def attend_forward(table, slopes, blocks, pieces, start, cols):
    tokens, width = blocks[0].shape
    seq = tokens * (len(blocks) - 1)
    f32, low = jnp.float32, jnp.bfloat16
    shapes = [
        ((seq, cols), low), ((cols, seq), f32), ((seq, 3 * cols), low), ((8, seq), f32),
        ((seq, width), low), ((seq, width), low), ((width, 3 * cols), low), ((8, width), f32),
    ]
    args = [table, slopes] + list(blocks) + list(pieces) + [start]
    return call(functools.partial(forward_kernel, len(blocks)), 2, args, shapes, [((width, 128), low)], 9000000000, 60)


def local_split(
    inputs, out_grad, segments, pairs,
    w_qkv, w_out, w_up, w_down, up_bias, vectors,
    first_qkv, first_out, first_up, first_down, first_bias, first_vectors,
    second_qkv, second_out, second_up, second_down, second_bias, second_vectors,
):
    low = jnp.bfloat16
    f32 = jnp.float32
    nz = lax.axis_size("z")
    n_ctx = 2 * nz
    every = ("z", "y", "x", "c")
    ctx = ("z", "y")
    plane = ("y", "x", "c")
    zi, yi, xi, ci = (lax.axis_index(a) for a in every)
    ctx_i = zi * 2 + yi
    tokens, width = inputs.shape[1:]
    half = tokens // 2
    seq_len = tokens * n_ctx
    heads_own = HEADS // n_ctx
    cols = heads_own * HD
    rows = w_qkv.shape[0]
    ff_own = w_down.shape[0]
    ff = nz * ff_own
    n_half = width // ff
    field_low = inputs[0]
    field = field_low.astype(f32)
    cot_low = out_grad[0]

    cut = width - width // 4
    field_cut = field_low[:, :cut]
    line = [shift(field_cut, "z", nz, k) for k in range(1, nz)]
    own_two = exchange(jnp.stack([field_low, cot_low]), "y")
    shapes = [((n_ctx, rows, 3 * cols + 128), low), ((8, rows, ff), low), ((n_half, ff_own, ff), low), ((tokens, width // 4), low)]
    packed = [pairs, w_qkv, vectors, segments, up_bias.reshape(1, ff_own), w_up, w_down, w_out]
    first_send, up_send, down_part, out_low = call(pack_kernel, 1, packed, shapes, limit=60)
    first_got = swap(first_send, ctx)
    up_part = swap(after(up_send, first_got), plane).reshape(8 * rows, ff)
    ff_send = jnp.concatenate([up_part, down_part.reshape(n_half * ff_own, ff)], 0)
    ff_send, first_got, own_two, out_low, *line = gate(ff_send, first_got, own_two, out_low, *line)
    pair_own, cot_y = own_two[0], own_two[1]

    ff_all = lax.all_gather(ff_send, "z", axis=0)
    pair_line = exchange(jnp.stack(line), "y")
    rest_own = jnp.stack([field_low[:, cut:], pair_own[:, cut:], out_low])
    rest = [shift(rest_own, "z", nz, k) for k in range(1, nz)]
    first_x = exchange(first_got, "x")
    first_c = exchange(first_got, "c")
    first_cx = exchange(first_x, "c")
    cot_two = jnp.stack([cot_low, cot_y])
    cot_x = exchange(cot_two, "x")
    seg_all = first_got[:, 0:2, 3 * cols + 64 :].reshape(seq_len).astype(jnp.int32)
    up_low = []
    for got in (first_got, first_c):
        bias_all = got[:, 2:4, 3 * cols + 64 :].reshape(nz, 2, ff_own)
        bias_all = lax.dynamic_index_in_dim(bias_all, yi, 1, keepdims=False)
        up_low = up_low + [bias_all.reshape(1, ff).astype(f32)]
    pair_all = first_got[:, 4, 3 * cols + 64].astype(jnp.int32)
    start = jnp.sum((seg_all[:, None] < seg_all[None, :]).astype(jnp.int32), 0, keepdims=True)
    slot_block = jnp.stack([pair_all, 2 * n_ctx - 1 - pair_all], 1)
    near = [((zi + k) % nz) * 2 + yi for k in range(nz)]
    near = jnp.stack(near + [((zi + k) % nz) * 2 + 1 - yi for k in range(nz)])
    ids = jnp.arange(n_ctx)
    near_block = jnp.sum(jnp.where((near[:, None] == ids[None, :])[:, :, None], slot_block[None], 0), 1)
    spans = jnp.arange(2 * n_ctx)
    block_slot = jnp.sum(jnp.where(slot_block.reshape(1, -1) == spans[:, None], spans[None, :], 0), 1)
    piece_f = jnp.stack([xi * 2 + ci, (1 - xi) * 2 + ci, xi * 2 + 1 - ci, (1 - xi) * 2 + 1 - ci])
    here = jnp.stack([ctx_i, zi, yi, xi, ci])
    table = jnp.concatenate([near_block.reshape(-1), block_slot, piece_f, here]).astype(jnp.int32)
    head_ids = (ctx_i * heads_own + jnp.arange(heads_own)).astype(f32)
    slopes = jnp.exp2(-8.0 * (head_ids + 1.0) / HEADS)
    out_z = jnp.stack([out_low] + [v[2] for v in rest])
    first_x, first_c, first_cx, cot_x, table, start, pair_line, slopes, out_z, *rest = gate(
        first_x, first_c, first_cx, cot_x, table, start, pair_line, slopes, out_z, *rest
    )

    out_y = exchange(out_z, "y")
    pieces = (first_got, first_x, first_c, first_cx)
    blocks = [field_low, pair_own, pair_line] + line + rest
    attended, att_t, qkv_low, lse, normed_one, seq_rows, qkv_w, vec = attend_forward(
        table, slopes, blocks, pieces, start, cols
    )
    attended, out_y = gate(attended.reshape(n_ctx, tokens, cols), out_y)

    attended_low = swap(attended, ctx)
    out_zy = jnp.stack([out_z, out_y])
    out_x = exchange(out_zy, "x")
    out_c_two = exchange(out_zy, "c")
    attended_low, out_x, out_c_two = gate(attended_low, out_x, out_c_two)
    cots = [cot_two, cot_x]
    shapes = [((tokens, width), f32), ((tokens, width), low), ((width, width), low)]
    parts = [table, attended_low, out_zy, out_x, out_c_two, exchange(out_x, "c"), field_low, vec]
    resid, mlp_low, out_w = call(project_kernel, 1, parts, shapes)

    mlp_y = exchange(mlp_low, "y")
    mlp_x = exchange(mlp_low, "x")
    mlp_y, mlp_x = gate(mlp_y, mlp_x)
    mlp_d0 = exchange(mlp_x[:half], "y")
    mlp_d1 = exchange(mlp_y[half:], "x")
    ff_other = exchange(after(ff_all, mlp_low), "c")
    mlp_d0, mlp_d1, ff_other = gate(mlp_d0, mlp_d1, ff_other)
    four = 4 * tokens
    one = ((tokens, width), low)
    shapes = [one] * 4 + [((four, 2 * ff), low)] * 2 + [((four, width), low)]
    scratch = [((2 * ff, width), low), ((width, 2 * ff), low)]
    rows_in = [mlp_low, mlp_y, mlp_x, mlp_d0, mlp_d1] + cots + [ff_all, ff_other] + up_low
    norm_own, norm_y, norm_x, norm_d, hidden, grad_pre, mlp_in = call(
        feed_kernel, 0, rows_in, shapes, scratch, limit=60
    )

    norm_d0 = exchange(norm_d[:half], "y")
    norm_d1 = exchange(norm_d[half:], "x")
    n_ff = 8 * rows + n_half * ff_own
    ff_keep, ff_give = call(
        feed_grad_kernel, 0, [mlp_in, grad_pre, hidden] + cots, [((nz, n_ff + 16, ff), low)] * 2, (), 1, 60
    )
    norm_d0, norm_d1, ff_give = gate(norm_d0, norm_d1, ff_give)
    norm_y = jnp.concatenate([norm_y[:half], add_low(norm_y[half:], norm_d1)], 0)
    norm_x = jnp.concatenate([add_low(norm_x[:half], norm_d0), norm_x[half:]], 0)
    norm_y, norm_x, ff_keep = gate(norm_y, norm_x, ff_keep)
    norm_y, norm_x = exchange(norm_y, "y"), exchange(norm_x, "x")
    ff_terms = add_low(ff_keep, exchange(ff_give, "c"))
    ff_sum = lax.psum_scatter(ff_terms, "z", scatter_dimension=0, tiled=True)[0]
    norm_x, norm_y, ff_terms = gate(norm_x, norm_y, ff_terms)
    shapes = [((tokens, width), f32), ((n_ctx, tokens, cols), low), ((8, width), f32)]
    shapes = shapes + [((2, 2, nz, rows, width), low)] * 2
    grad_resid, back_low, resid_sums, out_keep, out_give = call(
        norm_back_kernel,
        1,
        [table, norm_own, norm_x, norm_y, resid, cot_low, vec, out_w, attended_low],
        shapes,
        [((width, width), low)],
    )

    back_all = swap(back_low, ctx)
    out_c_got = exchange(out_give, "c")
    result_keep, result_give = call(
        result_kernel,
        0,
        [after(hidden, back_low), ff_all, ff_other],
        [((2, tokens, width), low)] * 2,
        [((2 * ff, width), low)],
    )
    back_all, out_c_got, result_keep, result_give = gate(back_all, out_c_got, result_keep, result_give)

    out_x_got = exchange(add_low(out_keep[1], out_c_got[1]), "x")
    shapes = [((2, n_ctx, rows, 4 * cols), low)] * 2
    shapes = shapes + [((nz, tokens, width), low)] * 2
    scratch = [((seq_len, 3 * cols), low), ((seq_len, cols), low), ((seq_len, cols), f32), ((seq_len, cols), f32)]
    scratch = scratch + [((seq_len, width), low), ((width, 4 * cols), low)]
    back_all = back_all.reshape(seq_len, cols)
    made = call(
        backward_kernel,
        2,
        [table, slopes, back_all, qkv_low, att_t, lse, start, normed_one, qkv_w, seq_rows, resid_sums],
        shapes,
        scratch,
        9000000000,
        60,
    )
    *made, out_x_got = gate(*made, out_x_got)
    qkv_keep, qkv_give, in_keep, in_give = made

    qkv_c_got = exchange(qkv_give, "c")
    qkv_c = add_low(qkv_keep[0], qkv_c_got[0])
    qkv_x_got = exchange(add_low(qkv_keep[1], qkv_c_got[1]), "x")
    out_c = add_low(out_keep[0], out_c_got[0])
    out_two = add_low(out_c[0], out_x_got[0])
    out_y_got = exchange(add_low(out_c[1], out_x_got[1]), "y")
    in_got = exchange(after(in_give, qkv_c), "y")
    result_x = exchange(after(result_give, qkv_c), "x")
    qkv_x_got, qkv_c, out_y_got = gate(qkv_x_got, qkv_c, out_y_got)
    qkv_x = add_low(qkv_c, qkv_x_got)

    qkv_got = swap(qkv_x, ctx)
    out_y_got = after(out_y_got, qkv_x)
    out_own = add_low(out_two[0], out_y_got[0])
    out_moved = [shift(add_low(out_two[k], out_y_got[k]), "z", nz, -k) for k in range(1, nz)]
    up_send = after(ff_sum, qkv_x)[: 8 * rows].reshape(8, rows, ff)
    result_x = after(result_x, qkv_x)
    result_y = exchange(add_low(result_keep[1], result_x[1]), "y")
    qkv_got, in_got, up_send, *out_moved = gate(qkv_got, in_got, up_send, *out_moved)
    shapes = [((4 * n_ctx, 1, 128), f32), ((rows, width), f32), ((8, rows), f32)]
    squared, grad_out_own, grad_vec_own = call(
        square_kernel, 1, [table, qkv_got, ff_sum, out_own, *out_moved], shapes, limit=48
    )

    squares = swap(squared, every)
    in_z = [shift(add_low(in_keep[k], in_got[k]), "z", nz, -k) for k in range(1, nz)]
    up_got = swap(after(up_send, squares), plane)
    masters = [w_qkv, w_out, w_down, up_bias.reshape(1, ff_own), vectors]
    firsts = [first_qkv, first_out, first_down, first_bias.reshape(1, ff_own), first_vectors]
    seconds = [second_qkv, second_out, second_down, second_bias.reshape(1, ff_own), second_vectors]
    shapes = [((1, 1), f32)]
    for item in masters:
        shapes = shapes + [(item.shape, f32)] * 4
    grads = [squares, qkv_got, grad_out_own, ff_sum, grad_vec_own]
    grad_norm, *results = call(adam_kernel, 0, grads + masters + firsts + seconds, shapes, limit=60)
    for k in range(12, 16):
        results[k] = results[k].reshape(ff_own)
    ups = call(adam_up_kernel, 0, [squares, up_got, w_up, first_up, second_up], [(w_up.shape, f32)] * 4, limit=60)
    results = results[:8] + list(ups) + results[8:]

    result_y = after(result_y, squares)
    result = (resid + result_keep[0].astype(f32) + result_x[0].astype(f32) + result_y.astype(f32) + vec[7]).astype(low)
    own_grads = in_keep[0].astype(f32) + in_got[0].astype(f32)
    for other in gate(*in_z, grad_norm)[:-1]:
        own_grads = own_grads + other.astype(f32)
    norm_one_back = jax.vjp(lambda v: layer_norm(v, vec[0], vec[1]), field)[1]
    in_grad = grad_resid + norm_one_back(own_grads)[0]
    return (result[None], in_grad[None], grad_norm[0, 0], *results)


def solution(mesh):
    n_ctx = mesh.shape["ctx"]
    if HEADS % n_ctx == 0 and n_ctx % 2 == 0 and mesh.shape["fsdp"] == 4:
        body = local_split
        ctx, fsdp = ("z", "y"), ("x", "c")
        mesh = Mesh(mesh.devices.reshape(n_ctx // 2, 2, 2, 2), ctx + fsdp)
    else:
        body = local
        ctx, fsdp = ("ctx",), ("fsdp",)
    rows = P(fsdp, ctx, None)
    flat = P(fsdp, ctx)
    mat = P(ctx + fsdp, None)
    vec = P(ctx + fsdp)
    wide = P(None, ctx + fsdp)
    group = (mat, mat, mat, mat, vec, wide)
    outs = ()
    for spec in group:
        outs = outs + (spec,) * 4
    return jax.shard_map(
        body,
        mesh=mesh,
        in_specs=(rows, rows, flat, flat) + group * 3,
        out_specs=(rows, rows, P()) + outs,
        check_vma=False,
    )
```

```python
import functools
import math

import jax
import jax.numpy as jnp
from jax import lax
from jax.experimental import pallas as pl
from jax.experimental.pallas import tpu as pltpu
from jax.sharding import Mesh
from jax.sharding import PartitionSpec as P

HEADS = 16
HD = 64


norm_eps = 1e-05
beta_one = 0.9
beta_two = 0.95
adam_eps = 1e-08
learn_rate = 0.02
weight_decay = 0.1
adam_step = 10
max_norm = 1.0
masked = -1e30
group_heads = 2


def layer_norm(field, gain, shift):
    center = field - jnp.mean(field, -1, keepdims=True)
    spread = jnp.mean(center * center, -1, keepdims=True)
    return center * lax.rsqrt(spread + norm_eps) * gain + shift


def gelu_exact(field):
    return jax.nn.gelu(field, approximate=False)


def contract(left, right, left_dim, right_dim):
    return lax.dot_general(
        left, right, (((left_dim,), (right_dim,)), ((), ())), preferred_element_type=jnp.float32
    )


def place(pair_ids, block, n_ctx):
    blocks = jnp.stack([pair_ids, 2 * n_ctx - 1 - pair_ids], 1).reshape(-1)
    offsets = jnp.arange(block, dtype=jnp.int32)
    return (blocks[:, None] * block + offsets[None, :]).reshape(-1)


def pick(array, first):
    return lax.dynamic_slice_in_dim(array, first, group_heads, 1)


def adamw(weight, grad, first, second, clip):
    clipped = grad * clip
    first_new = beta_one * first + (1.0 - beta_one) * clipped
    second_new = beta_two * second + (1.0 - beta_two) * clipped * clipped
    first_hat = first_new / (1.0 - beta_one**adam_step)
    second_hat = second_new / (1.0 - beta_two**adam_step)
    update = -learn_rate * (first_hat / (jnp.sqrt(second_hat) + adam_eps) + weight_decay * weight)
    return (update, first_new, second_new)


def local(
    inputs,
    out_grad,
    segments,
    pairs,
    w_qkv,
    w_out,
    w_up,
    w_down,
    up_bias,
    vectors,
    first_qkv,
    first_out,
    first_up,
    first_down,
    first_bias,
    first_vectors,
    second_qkv,
    second_out,
    second_up,
    second_down,
    second_bias,
    second_vectors,
):
    low_type = jnp.bfloat16
    n_ctx = lax.axis_size("ctx")
    field = inputs[0].astype(jnp.float32)
    tokens = field.shape[0]
    block = tokens // 2
    width = field.shape[1]
    seq_len = tokens * n_ctx
    scale = HD ** (-0.5)
    groups = HEADS // group_heads
    slope = 2.0 ** (-8.0 * (jnp.arange(HEADS, dtype=jnp.float32) + 1.0) / HEADS)
    qkv_w, out_w, vec_low = (
        lax.all_gather(w_qkv.astype(low_type), ("ctx", "fsdp"), axis=0, tiled=True),
        lax.all_gather(w_out.astype(low_type), ("ctx", "fsdp"), axis=0, tiled=True),
        lax.all_gather(vectors.astype(low_type), ("ctx", "fsdp"), axis=1, tiled=True),
    )
    vec = vec_low.astype(jnp.float32)
    gain_one, shift_one, gain_two, shift_two = (vec[0], vec[1], vec[2], vec[3])
    bias_query, bias_value, bias_out, bias_down = (vec[4], vec[5], vec[6], vec[7])
    normed_one = layer_norm(field, gain_one, shift_one)
    attn_in = normed_one.astype(low_type)
    mixed = jnp.dot(attn_in, qkv_w, preferred_element_type=jnp.float32)
    query = (mixed[:, :width] + bias_query).astype(low_type)
    keys = mixed[:, width : 2 * width].astype(low_type)
    values = (mixed[:, 2 * width :] + bias_value).astype(low_type)
    pair_ids = pairs[0]
    kv_all, pair_all, seg_all = (
        lax.all_gather(jnp.concatenate([keys, values], 1), "ctx", axis=0, tiled=True),
        lax.all_gather(pair_ids, "ctx", axis=0, tiled=True),
        lax.all_gather(segments[0], "ctx", axis=0, tiled=True),
    )
    pos_query = place(pair_ids, block, n_ctx)
    pos_key = place(pair_all, block, n_ctx)
    seg_query = jnp.take(seg_all, pos_query)
    seg_key = jnp.take(seg_all, pos_key)
    relative = (pos_key[None, :] - pos_query[:, None]).astype(jnp.float32)
    allowed = (seg_query[:, None] == seg_key[None, :]) & (pos_key[None, :] <= pos_query[:, None])
    query_heads = query.reshape(tokens, HEADS, HD)
    key_heads = kv_all[:, :width].reshape(seq_len, HEADS, HD)
    value_heads = kv_all[:, width:].reshape(seq_len, HEADS, HD)

    def scores_of(query_part, key_part, first, offsets, visible):
        slopes = lax.dynamic_slice_in_dim(slope, first, group_heads, 0)
        raw = (
            jnp.einsum("rhe,khe->hrk", query_part, key_part, preferred_element_type=jnp.float32)
            * scale
        )
        raw = raw + slopes[:, None, None] * offsets[None]
        return jnp.where(visible[None], raw, masked)

    def forward_group(index, carry):
        attended, log_total = carry
        first = index * group_heads
        scores = scores_of(
            pick(query_heads, first), pick(key_heads, first), first, relative, allowed
        )
        top = jnp.max(scores, -1, keepdims=True)
        expo = jnp.exp(scores - top)
        total = jnp.sum(expo, -1, keepdims=True)
        chance_low = (expo / total).astype(low_type)
        part_out = jnp.einsum(
            "hrk,khe->rhe", chance_low, pick(value_heads, first), preferred_element_type=jnp.float32
        )
        attended = lax.dynamic_update_slice_in_dim(attended, part_out, first, 1)
        log_total = lax.dynamic_update_slice_in_dim(
            log_total, (top + jnp.log(total))[:, :, 0].T, first, 1
        )
        return (attended, log_total)

    attended, log_total = lax.fori_loop(
        0,
        groups,
        forward_group,
        (jnp.zeros((tokens, HEADS, HD), jnp.float32), jnp.zeros((tokens, HEADS), jnp.float32)),
    )
    attended_low = attended.reshape(tokens, width).astype(low_type)
    resid = field + jnp.dot(attended_low, out_w, preferred_element_type=jnp.float32) + bias_out
    normed_two = layer_norm(resid, gain_two, shift_two)
    mlp_in = normed_two.astype(low_type)
    up_w, down_w, up_low = (
        lax.all_gather(w_up.astype(low_type), ("ctx", "fsdp"), axis=0, tiled=True),
        lax.all_gather(w_down.astype(low_type), ("ctx", "fsdp"), axis=0, tiled=True),
        lax.all_gather(up_bias.astype(low_type), ("ctx", "fsdp"), axis=0, tiled=True),
    )
    pre = jnp.dot(mlp_in, up_w, preferred_element_type=jnp.float32) + up_low.astype(jnp.float32)
    hidden = gelu_exact(pre).astype(low_type)
    result = resid + jnp.dot(hidden, down_w, preferred_element_type=jnp.float32) + bias_down
    cotangent_low = out_grad[0]
    cotangent = cotangent_low.astype(jnp.float32)
    up_back, down_back = (
        lax.all_gather(w_up.astype(low_type), ("ctx", "fsdp"), axis=0, tiled=True),
        lax.all_gather(w_down.astype(low_type), ("ctx", "fsdp"), axis=0, tiled=True),
    )
    grad_down_term = contract(hidden, cotangent_low, 0, 0)
    grad_bias_down = jnp.sum(cotangent, 0)
    grad_hidden = contract(cotangent_low, down_back, 1, 1)
    gelu_back = jax.vjp(gelu_exact, pre)[1]
    grad_pre = gelu_back(grad_hidden)[0].astype(low_type)
    grad_up_bias = jnp.sum(grad_pre.astype(jnp.float32), 0)
    grad_up_term = contract(mlp_in, grad_pre, 0, 0)
    grad_normed_two = contract(grad_pre, up_back, 1, 1)
    norm_two_back = jax.vjp(layer_norm, resid, gain_two, shift_two)[1]
    grad_resid_norm, grad_gain_two, grad_shift_two = norm_two_back(grad_normed_two)
    grad_resid = cotangent + grad_resid_norm
    grad_up_own, grad_down_own, grad_bias_own = (
        lax.psum_scatter(grad_up_term, ("ctx", "fsdp"), scatter_dimension=0, tiled=True),
        lax.psum_scatter(grad_down_term, ("ctx", "fsdp"), scatter_dimension=0, tiled=True),
        lax.psum_scatter(grad_up_bias, ("ctx", "fsdp"), scatter_dimension=0, tiled=True),
    )
    qkv_back, out_back = (
        lax.all_gather(w_qkv.astype(low_type), ("ctx", "fsdp"), axis=0, tiled=True),
        lax.all_gather(w_out.astype(low_type), ("ctx", "fsdp"), axis=0, tiled=True),
    )
    grad_bias_out = jnp.sum(grad_resid, 0)
    resid_low = grad_resid.astype(low_type)
    grad_out_term = contract(attended_low, resid_low, 0, 0)
    back_low = contract(resid_low, out_back, 1, 1).astype(low_type)
    back_heads = back_low.reshape(tokens, HEADS, HD)

    def backward_group(index, carry):
        grad_query, grad_key, grad_value = carry
        first = index * group_heads
        query_part = pick(query_heads, first)
        key_part = pick(key_heads, first)
        value_part = pick(value_heads, first)
        back_part = pick(back_heads, first)
        scores = scores_of(query_part, key_part, first, relative, allowed)
        logsum = lax.dynamic_slice_in_dim(log_total, first, group_heads, 1).T
        chance = jnp.exp(scores - logsum[:, :, None])
        pushed = jnp.einsum(
            "rhe,khe->hrk", back_part, value_part, preferred_element_type=jnp.float32
        )
        centre = jnp.sum(chance * pushed, -1, keepdims=True)
        dscore = (chance * (pushed - centre)).astype(low_type)
        chance_low = chance.astype(low_type)
        part_query = (
            jnp.einsum("hrk,khe->rhe", dscore, key_part, preferred_element_type=jnp.float32) * scale
        )
        part_key = (
            jnp.einsum("hrk,rhe->khe", dscore, query_part, preferred_element_type=jnp.float32)
            * scale
        )
        part_value = jnp.einsum(
            "hrk,rhe->khe", chance_low, back_part, preferred_element_type=jnp.float32
        )
        grad_query = lax.dynamic_update_slice_in_dim(grad_query, part_query, first, 1)
        grad_key = lax.dynamic_update_slice_in_dim(grad_key, part_key, first, 1)
        grad_value = lax.dynamic_update_slice_in_dim(grad_value, part_value, first, 1)
        return (grad_query, grad_key, grad_value)

    zero_keys = jnp.zeros((seq_len, HEADS, HD), jnp.float32)
    grad_query, grad_key, grad_value = lax.fori_loop(
        0,
        groups,
        backward_group,
        (jnp.zeros((tokens, HEADS, HD), jnp.float32), zero_keys, zero_keys),
    )
    own_key, own_value = (
        lax.psum_scatter(
            grad_key.reshape(seq_len, width).astype(jnp.bfloat16),
            "ctx",
            scatter_dimension=0,
            tiled=True,
        ).astype(jnp.float32),
        lax.psum_scatter(
            grad_value.reshape(seq_len, width).astype(jnp.bfloat16),
            "ctx",
            scatter_dimension=0,
            tiled=True,
        ).astype(jnp.float32),
    )
    grad_query_low = grad_query.reshape(tokens, width).astype(low_type)
    grad_key_low = own_key.astype(low_type)
    grad_value_low = own_value.astype(low_type)
    grad_mixed = jnp.concatenate([grad_query_low, grad_key_low, grad_value_low], 1)
    grad_bias_query = jnp.sum(grad_query_low.astype(jnp.float32), 0)
    grad_bias_value = jnp.sum(grad_value_low.astype(jnp.float32), 0)
    grad_qkv_term = contract(attn_in, grad_mixed, 0, 0)
    grad_normed_one = contract(grad_mixed, qkv_back, 1, 1)
    norm_one_back = jax.vjp(layer_norm, field, gain_one, shift_one)[1]
    grad_field_norm, grad_gain_one, grad_shift_one = norm_one_back(grad_normed_one)
    in_grad = grad_resid + grad_field_norm
    grad_vec_term = jnp.stack(
        [
            grad_gain_one,
            grad_shift_one,
            grad_gain_two,
            grad_shift_two,
            grad_bias_query,
            grad_bias_value,
            grad_bias_out,
            grad_bias_down,
        ],
        0,
    )
    grad_qkv_own, grad_out_own, grad_vec_own = (
        lax.psum_scatter(grad_qkv_term, ("ctx", "fsdp"), scatter_dimension=0, tiled=True),
        lax.psum_scatter(grad_out_term, ("ctx", "fsdp"), scatter_dimension=0, tiled=True),
        lax.psum_scatter(grad_vec_term, ("ctx", "fsdp"), scatter_dimension=1, tiled=True),
    )
    grads = (grad_qkv_own, grad_out_own, grad_up_own, grad_down_own, grad_bias_own, grad_vec_own)
    local_squares = sum([jnp.sum(item * item) for item in grads])
    grad_norm = jnp.sqrt(lax.psum(local_squares, ("ctx", "fsdp")))
    clip = jnp.minimum(1.0, max_norm / (grad_norm + 1e-06))
    masters = (w_qkv, w_out, w_up, w_down, up_bias, vectors)
    firsts = (first_qkv, first_out, first_up, first_down, first_bias, first_vectors)
    seconds = (second_qkv, second_out, second_up, second_down, second_bias, second_vectors)
    results = []
    for weight, grad, first, second in zip(masters, grads, firsts, seconds):
        update, first_new, second_new = adamw(weight, grad, first, second, clip)
        results = results + [grad, update, first_new, second_new]
    return (
        result.astype(low_type)[None],
        in_grad[None],
        grad_norm,
        results[0],
        results[1],
        results[2],
        results[3],
        results[4],
        results[5],
        results[6],
        results[7],
        results[8],
        results[9],
        results[10],
        results[11],
        results[12],
        results[13],
        results[14],
        results[15],
        results[16],
        results[17],
        results[18],
        results[19],
        results[20],
        results[21],
        results[22],
        results[23],
    )


def exchange(v, axis):
    return lax.ppermute(v, axis, [(0, 1), (1, 0)])


def shift(v, axis, n_line, k):
    return lax.ppermute(v, axis, [(i, (i - k) % n_line) for i in range(n_line)])


def swap(v, axes):
    return lax.all_to_all(v, axes, 0, 0, tiled=True)


def gate(*values):
    return lax.optimization_barrier(values)


def after(v, *others):
    return lax.optimization_barrier((v,) + others)[0]


def order_two(own, other, axis, dim):
    first = lax.axis_index(axis) == 0
    return jnp.stack([jnp.where(first, own, other), jnp.where(first, other, own)], dim)


def split_two(part, axis, dim):
    me = lax.axis_index(axis)
    keep = lax.dynamic_index_in_dim(part, me, dim, keepdims=False)
    return keep, lax.dynamic_index_in_dim(part, 1 - me, dim, keepdims=False)


def add_low(keep, got):
    return (keep.astype(jnp.float32) + got.astype(jnp.float32)).astype(jnp.bfloat16)


def line_gives(part, axis, n_line):
    me = lax.axis_index(axis)
    blocks = [lax.dynamic_index_in_dim(part, (me + k) % n_line, 0, keepdims=False) for k in range(n_line)]
    return blocks[0], [shift(blocks[k], axis, n_line, -k) for k in range(1, n_line)]


def line_order(parts, axis):
    n_line = len(parts)
    first = (n_line - lax.axis_index(axis)) % n_line
    return lax.dynamic_slice_in_dim(jnp.concatenate([jnp.stack(parts)] * 2, 0), first, n_line, 0)


def lanes_of(head, shape):
    return lax.broadcasted_iota(jnp.int32, shape, 1) // HD == head


def head_parts(query, keys, slope, head):
    seq = keys.shape[0]
    lane = lax.broadcasted_iota(jnp.int32, keys.shape, 1)
    own = lane // HD == head
    spot = lane - (1 - head) * HD
    bias = lax.broadcasted_iota(jnp.int32, (seq, 1), 0).astype(jnp.float32) * (slope * HD**0.5)
    high = bias.astype(jnp.bfloat16)
    rest = bias - high.astype(jnp.float32)
    middle = rest.astype(jnp.bfloat16)
    small = (rest - middle.astype(jnp.float32)).astype(jnp.bfloat16)
    zero = jnp.zeros_like(keys)
    extra = jnp.where(spot == 0, high, jnp.where(spot == 1, middle, jnp.where(spot == 2, small, zero)))
    ones = jnp.where((spot >= 0) & (spot <= 2), jnp.ones_like(keys), zero)
    return jnp.where(own, query, ones), jnp.where(own, keys, extra)


def visible(start, tile, at, size):
    key = lax.broadcasted_iota(jnp.int32, (size, tile), 0)
    seen = key >= start
    return seen & (key <= lax.broadcasted_iota(jnp.int32, (size, tile), 1) + at)


def forward_kernel(n_refs, meta, slopes, *refs):
    pieces = refs[n_refs : n_refs + 4]
    start_ref = refs[n_refs + 4]
    att_ref, att_t, qkv_ref, lse_ref, normed, x_ref, w_ref, vec_ref, extra = refs[n_refs + 5 :]
    n_line = n_refs // 2
    own, pair, pair_line, line = refs[0], refs[1], refs[2 : 1 + n_line], refs[1 + n_line : n_refs]
    n_blocks = 2 * n_line

    def block_part(b, span):
        z, other = b % n_line, b // n_line
        if z == 0:
            return (pair if other else own)[span, :]
        return pair_line[z - 1][span, :] if other else line[z - 1][span, :]

    f32, low = jnp.float32, jnp.bfloat16
    n_ctx, rows, _ = pieces[0].shape
    tokens, width = own.shape
    half = tokens // 2
    seq = tokens * n_blocks
    cols = qkv_ref.shape[1] // 3
    spans = 2 * n_blocks
    for c in range(n_ctx):
        for p in range(4):
            piece = pieces[p][c]
            to = pl.ds(pl.multiple_of(c * 4 * rows + meta[2 * spans + p] * rows, rows), rows)
            w_ref[to, :] = piece[:, : 3 * cols]
            extra[to, :] = piece[:, 3 * cols :]
    pick_rows = (
        lax.broadcasted_iota(jnp.int32, (8, 128), 0) == lax.broadcasted_iota(jnp.int32, (8, 128), 1)
    ).astype(low)
    vec = contract(pick_rows, extra[...], 1, 1)
    vec_ref[...] = vec
    gain, move = vec[0:1], vec[1:2]
    for j in range(spans):
        part = block_part(j // 2, slice((j % 2) * half, (j % 2 + 1) * half))
        to = pl.ds(pl.multiple_of(meta[j] * half, half), half)
        x_ref[to, :] = part
        normed[to, :] = layer_norm(part.astype(f32), gain, move).astype(low)
    at = pl.ds(pl.multiple_of(meta[2 * spans + 4] * cols, cols), cols)
    bias_q, bias_v = vec_ref[4:5, at], vec_ref[5:6, at]
    tile = min(256, seq)
    for t in range(seq // tile):
        span = pl.ds(t * tile, tile)
        mixed = jnp.dot(normed[span, :], w_ref[...], preferred_element_type=f32)
        qkv_ref[span, :cols] = (mixed[:, :cols] + bias_q).astype(low)
        qkv_ref[span, cols : 2 * cols] = mixed[:, cols : 2 * cols].astype(low)
        qkv_ref[span, 2 * cols :] = (mixed[:, 2 * cols :] + bias_v).astype(low)
    factor = HD**-0.5 * 1.4426950408889634
    query, keys, values = qkv_ref[:, :cols], qkv_ref[:, cols : 2 * cols], qkv_ref[:, 2 * cols :]
    lse_ref[...] = jnp.zeros_like(lse_ref)
    for h in range(cols // HD):
        q_h, k_h = head_parts(query, keys, slopes[h], h)
        v_h = jnp.where(lanes_of(h, values.shape), values, jnp.zeros_like(values))
        for t in range(seq // tile):
            size = (t + 1) * tile
            span = slice(t * tile, (t + 1) * tile)
            score = contract(k_h[:size], q_h[span], 1, 1) * factor
            score = jnp.where(visible(start_ref[:, span], tile, t * tile, size), score, masked)
            top = jnp.max(score, 0, keepdims=True)
            expo = jnp.exp2(score - top)
            total = jnp.sum(expo, 0, keepdims=True)
            lse_ref[h : h + 1, span] = top + jnp.log2(total)
            part = contract(v_h[:size], expo.astype(low), 0, 0) / total
            att_t[:, span] = part if h == 0 else att_t[:, span] + part
    for t in range(seq // tile):
        span = slice(t * tile, (t + 1) * tile)
        x_tile = att_t[:, span].T.astype(low)
        for u in range(tile // half):
            b = t * (tile // half) + u
            to = meta[spans + b]
            att_ref[pl.ds(pl.multiple_of(to * half, half), half), :] = x_tile[u * half : (u + 1) * half]


def pack_kernel(pairs, w_qkv, vectors, segments, up_bias, w_up, w_down, w_out, first_ref, up_ref, down_ref, out_ref):
    low, f32 = jnp.bfloat16, jnp.float32
    n_ctx, rows, wide = first_ref.shape
    cols = (wide - 128) // 3
    width = n_ctx * cols
    row = lax.broadcasted_iota(jnp.int32, (rows, 128), 0)
    lane = lax.broadcasted_iota(jnp.int32, (rows, 128), 1)
    one_hot = lax.broadcasted_iota(jnp.int32, (8, 128), 0) == lax.broadcasted_iota(jnp.int32, (8, 128), 1)
    columns = contract(vectors[...].astype(low), one_hot.astype(low), 0, 0)
    seg, bias = segments[...].astype(f32), up_bias[...]
    lines = [pltpu.roll(seg, 64, 1), seg, pltpu.roll(bias, 64, 1), bias]
    extra = jnp.where(lane < 8, columns, 0.0)
    for k in range(4):
        extra = jnp.where((row == k) & (lane >= 64), lines[k], extra)
    extra = jnp.where((row == 4) & (lane >= 64), pairs[0, 0].astype(f32), extra).astype(low)
    for c in range(n_ctx):
        for k in range(3):
            first_ref[c, :, k * cols : (k + 1) * cols] = w_qkv[:, k * width + c * cols : k * width + (c + 1) * cols].astype(low)
        first_ref[c, :, 3 * cols :] = extra
    n_plane, _, ff = up_ref.shape
    own = ff // (n_ctx // 2)
    for r in range(n_plane):
        for k in range(n_ctx // 2):
            up_ref[r, :, k * own : (k + 1) * own] = w_up[:, (k * n_plane + r) * own : (k * n_plane + r + 1) * own].astype(low)
    for k in range(down_ref.shape[0]):
        down_ref[k] = w_down[:, k * ff : (k + 1) * ff].astype(low)
    wide_out = out_ref.shape[1]
    for k in range(out_ref.shape[0] // rows):
        out_ref[k * rows : (k + 1) * rows, :] = w_out[:, k * wide_out : (k + 1) * wide_out].astype(low)


def project_kernel(table, att, own_ref, x_ref, c_ref, cx_ref, field, vec, resid_ref, mlp_ref, w_ref):
    low, f32 = jnp.bfloat16, jnp.float32
    n_ctx, tokens, cols = att.shape
    n_line = own_ref.shape[1]
    rows = w_ref.shape[0] // (8 * n_line)
    wide = own_ref.shape[3]
    at = 4 * n_ctx + 5
    zi, yi, xi, ci = (table[at + k] for k in range(4))
    for q, ref in enumerate((own_ref, x_ref, c_ref, cx_ref)):
        for p in range(2):
            for k in range(n_line):
                z = lax.rem(zi + k, n_line)
                y = lax.rem(yi + p, 2)
                x = lax.rem(xi + q % 2, 2)
                to = ((z * 2 + y) * 4 + x * 2 + lax.rem(ci + q // 2, 2)) * rows
                for part in range(tokens // rows):
                    spot = (pl.ds(pl.multiple_of(to, rows), rows), slice(part * wide, (part + 1) * wide))
                    w_ref[spot] = ref[p, k, part * rows : (part + 1) * rows, :]
    heads = jnp.concatenate([att[c] for c in range(n_ctx)], 1)
    moved = jnp.dot(heads, w_ref[...], preferred_element_type=f32)
    resid = field[...].astype(f32) + moved + vec[6:7]
    resid_ref[...] = resid
    mlp_ref[...] = layer_norm(resid, vec[2:3], vec[3:4]).astype(low)


def both_down(parts, down):
    ff = down.shape[0] // 2
    n_line = parts[0].shape[0]
    own = ff // n_line
    n_half = down.shape[1] // ff
    up_rows = parts[0].shape[1] - n_half * own
    for c, part in enumerate(parts):
        for k in range(n_line):
            for h in range(n_half):
                rows = slice(up_rows + h * own, up_rows + (h + 1) * own)
                down[c * ff + k * own : c * ff + (k + 1) * own, h * ff : (h + 1) * ff] = part[k, rows, :]


def feed_kernel(
    m_own, m_y, m_x, m_d0, m_d1, cot_0, cot_1, ff_own, ff_other, bias_own, bias_other,
    norm_own, norm_y, norm_x, norm_d, hidden_ref, pre_ref, mlp_ref, down, up,
):
    low, f32 = jnp.bfloat16, jnp.float32
    tokens, width = m_own.shape
    half = tokens // 2
    n_line, _, ff = ff_own.shape
    up_rows = width // n_line
    for c, part in enumerate((ff_own, ff_other)):
        for k in range(n_line):
            up[k * up_rows : (k + 1) * up_rows, c * ff : (c + 1) * ff] = part[k, :up_rows, :]
    both_down((ff_own, ff_other), down)
    bias = jnp.concatenate([bias_own[...], bias_other[...]], 1)
    for n, block in enumerate((m_own, m_y, m_x)):
        mlp_ref[n * tokens : (n + 1) * tokens, :] = block[...]
    mlp_ref[3 * tokens : 3 * tokens + half, :] = m_d0[...]
    mlp_ref[3 * tokens + half :, :] = m_d1[...]
    for t in range(2):
        span = slice(2 * t * tokens, 2 * (t + 1) * tokens)
        cot = (cot_0, cot_1)[t][...].reshape(2 * tokens, width)
        grads = []
        for c in range(2):
            cut = slice(c * ff, (c + 1) * ff)
            pre = jnp.dot(mlp_ref[span, :], up[:, cut], preferred_element_type=f32) + bias[:, cut]
            cdf = 0.5 * (1.0 + lax.erf(pre * 0.7071067811865476))
            pdf = jnp.exp(-0.5 * pre * pre) * 0.3989422804014327
            hidden_ref[span, cut] = (pre * cdf).astype(low)
            grad = (contract(cot, down[cut, :], 1, 1) * (cdf + pre * pdf)).astype(low)
            pre_ref[span, cut] = grad
            grads = grads + [grad]
        part = contract(jnp.concatenate(grads, 1), up[...], 1, 1).astype(low)
        first, second = ((norm_own, norm_y), (norm_x, norm_d))[t]
        first[...] = part[:tokens]
        second[...] = part[tokens:]


def feed_grad_kernel(mlp_ref, pre_ref, hidden_ref, cot_0, cot_1, keep_ref, give_ref):
    low, f32 = jnp.bfloat16, jnp.float32
    seq, width = mlp_ref.shape
    n_line, _, ff = keep_ref.shape
    own, up_rows, n_half = ff // n_line, width // n_line, width // ff
    cot = jnp.concatenate([ref[...].reshape(seq // 2, width) for ref in (cot_0, cot_1)], 0)
    for c, ref in enumerate((keep_ref, give_ref)):
        cut = slice(c * ff, (c + 1) * ff)
        down = contract(hidden_ref[:, cut], cot, 0, 0).astype(low)
        sums = jnp.sum(pre_ref[:, cut].astype(f32), 0, keepdims=True)
        pad = ref.shape[1] - up_rows - n_half * own
        up = contract(mlp_ref[...], pre_ref[:, cut], 0, 0).astype(low)
        for k in range(n_line):
            ref[k, :up_rows, :] = up[k * up_rows : (k + 1) * up_rows]
            for h in range(n_half):
                part = down[k * own : (k + 1) * own, h * ff : (h + 1) * ff]
                ref[k, up_rows + h * own : up_rows + (h + 1) * own, :] = part
            line = jnp.concatenate([sums[:, k * own : (k + 1) * own], jnp.zeros((1, ff - own), f32)], 1)
            ref[k, up_rows + n_half * own :, :] = jnp.broadcast_to(line, (pad, ff)).astype(low)


def result_kernel(hidden_ref, ff_own, ff_other, keep_ref, give_ref, down):
    both_down((ff_own, ff_other), down)
    half = hidden_ref.shape[0] // 2
    for t, ref in enumerate((keep_ref, give_ref)):
        part = jnp.dot(hidden_ref[t * half : (t + 1) * half, :], down[...], preferred_element_type=jnp.float32)
        ref[...] = part.astype(jnp.bfloat16).reshape(ref.shape)


def norm_back_kernel(
    table, own, got_x, got_y, resid_ref, cot_ref, vec, w_ref, att, grad_ref, back_ref, sums_ref, keep_ref, give_ref, terms
):
    low, f32 = jnp.bfloat16, jnp.float32
    grad = own[...].astype(f32) + got_x[...].astype(f32) + got_y[...].astype(f32)
    resid = resid_ref[...]
    center = resid - jnp.mean(resid, -1, keepdims=True)
    sharp = lax.rsqrt(jnp.mean(center * center, -1, keepdims=True) + norm_eps)
    unit = center * sharp
    scaled = grad * vec[2:3]
    inner = scaled - jnp.mean(scaled, -1, keepdims=True) - unit * jnp.mean(scaled * unit, -1, keepdims=True)
    cot = cot_ref[...].astype(f32)
    total = cot + inner * sharp
    grad_ref[...] = total
    rounded = total.astype(low)
    back = contract(rounded, w_ref[...], 1, 1).astype(low)
    n_ctx, _, cols = back_ref.shape
    for c in range(n_ctx):
        back_ref[c] = back[:, c * cols : (c + 1) * cols]
    row = lax.broadcasted_iota(jnp.int32, sums_ref.shape, 0)
    sums = jnp.where(row == 2, jnp.sum(grad * unit, 0, keepdims=True), 0.0)
    sums = jnp.where(row == 3, jnp.sum(grad, 0, keepdims=True), sums)
    sums = jnp.where(row == 6, jnp.sum(total, 0, keepdims=True), sums)
    sums_ref[...] = jnp.where(row == 7, jnp.sum(cot, 0, keepdims=True), sums)
    for c in range(n_ctx):
        terms[c * cols : (c + 1) * cols, :] = contract(att[c], rounded, 0, 0).astype(low)
    n_line, rows = keep_ref.shape[2:4]
    at = 4 * n_ctx + 5
    for which, ref in enumerate((keep_ref, give_ref)):
        for q in range(4 * n_line):
            x, y, z = q // (2 * n_line), q // n_line % 2, q % n_line
            chip = (lax.rem(table[at] + z, n_line) * 2 + lax.rem(table[at + 1] + y, 2)) * 4
            to = (chip + lax.rem(table[at + 2] + x, 2) * 2 + lax.rem(table[at + 3] + which, 2)) * rows
            ref[x, y, z] = terms[pl.ds(pl.multiple_of(to, rows), rows), :]


def backward_kernel(
    table, slopes, back_ref, qkv_ref, att_t, lse_ref, start_ref, normed, w_ref, x_ref, sums_ref,
    keep_ref, give_ref, in_keep, in_give, mixed_ref, back, d_key, d_value, moved, made,
):
    f32, low = jnp.float32, jnp.bfloat16
    seq, cols = back_ref.shape
    n_ctx, rows = keep_ref.shape[1:3]
    width = w_ref.shape[0]
    spans = 2 * n_ctx
    half = seq // spans
    for b in range(spans):
        back[b * half : (b + 1) * half, :] = back_ref[pl.ds(pl.multiple_of(table[spans + b] * half, half), half), :]
    factor = HD**-0.5 * 1.4426950408889634
    query, keys, values = qkv_ref[:, :cols], qkv_ref[:, cols : 2 * cols], qkv_ref[:, 2 * cols :]
    grads = back[...]
    product = att_t[...] * grads.astype(f32).T
    tile = min(256, seq)
    d_query = [None] * (seq // tile)
    for h in range(cols // HD):
        q_h, k_h = head_parts(query, keys, slopes[h], h)
        own = lanes_of(h, values.shape)
        zero = jnp.zeros_like(values)
        v_h, g_h = jnp.where(own, values, zero), jnp.where(own, grads, zero)
        qq_h, kk_h = jnp.where(own, query, zero), jnp.where(own, keys, zero)
        delta = jnp.sum(product[h * HD : (h + 1) * HD], 0, keepdims=True)
        for t in reversed(range(seq // tile)):
            size = (t + 1) * tile
            span = slice(t * tile, (t + 1) * tile)
            score = contract(k_h[:size], q_h[span], 1, 1) * factor
            score = jnp.where(visible(start_ref[:, span], tile, t * tile, size), score, masked)
            chance = jnp.exp2(score - lse_ref[h : h + 1, span])
            pushed = contract(v_h[:size], g_h[span], 1, 1)
            dscore = (chance * (pushed - delta[:, span])).astype(low)
            part_v = jnp.dot(chance.astype(low), g_h[span], preferred_element_type=f32)
            part_k = jnp.dot(dscore, qq_h[span], preferred_element_type=f32)
            if h == 0 and t == seq // tile - 1:
                d_value[...] = part_v
                d_key[...] = part_k
            else:
                d_value[:size, :] += part_v
                d_key[:size, :] += part_k
            part_q = contract(kk_h[:size], dscore, 0, 0)
            d_query[t] = part_q if h == 0 else d_query[t] + part_q
    scale = HD**-0.5
    for t in range(seq // tile):
        mixed_ref[t * tile : (t + 1) * tile, :cols] = (d_query[t] * scale).T.astype(low)
    mixed_ref[:, cols : 2 * cols] = (d_key[...] * scale).astype(low)
    mixed_ref[:, 2 * cols :] = d_value[...].astype(low)
    mixed = mixed_ref[...]
    mixed_sums = jnp.sum(mixed.astype(f32), 0, keepdims=True)
    gain_sum = jnp.zeros((1, width), f32)
    shift_sum = jnp.zeros((1, width), f32)
    for t in range(seq // tile):
        grad = contract(mixed_ref[t * tile : (t + 1) * tile, :], w_ref[...], 1, 1)
        field = x_ref[t * tile : (t + 1) * tile, :].astype(f32)
        center = field - jnp.mean(field, -1, keepdims=True)
        unit = center * lax.rsqrt(jnp.mean(center * center, -1, keepdims=True) + norm_eps)
        gain_sum = gain_sum + jnp.sum(grad * unit, 0, keepdims=True)
        shift_sum = shift_sum + jnp.sum(grad, 0, keepdims=True)
        moved[t * tile : (t + 1) * tile, :] = grad.astype(low)
    n_line = spans // 4
    for y, ref in enumerate((in_keep, in_give)):
        for z in range(n_line):
            for u in range(2):
                part = pl.ds(pl.multiple_of(table[(y * n_line + z) * 2 + u] * half, half), half)
                ref[z, u * half : (u + 1) * half, :] = moved[part, :]
    row = lax.broadcasted_iota(jnp.int32, (8, width), 0)
    sums = jnp.where(row == 0, gain_sum, jnp.where(row == 1, shift_sum, sums_ref[...]))
    here = table[2 * spans + 4]
    small = lax.broadcasted_iota(jnp.int32, (8, cols), 0)
    bias = jnp.where(small == 4, mixed_sums[:, :cols], jnp.where(small == 5, mixed_sums[:, 2 * cols :], 0.0))
    terms = contract(mixed, normed[...], 0, 0)
    blank = jnp.zeros((rows - 8, cols), f32)
    for c in range(n_ctx):
        part = terms[:, c * 4 * rows : (c + 1) * 4 * rows].T.astype(low)
        block = sums[:, c * cols : (c + 1) * cols] + jnp.where(here == c, bias, 0.0)
        block = jnp.concatenate([block, blank], 0).astype(low)
        for f in range(4):
            made[(c * 4 + f) * rows : (c * 4 + f + 1) * rows, : 3 * cols] = part[f * rows : (f + 1) * rows]
            made[(c * 4 + f) * rows : (c * 4 + f + 1) * rows, 3 * cols :] = block
    at = 2 * spans + 5
    for which, ref in enumerate((keep_ref, give_ref)):
        for x in range(2):
            f = lax.rem(table[at + 2] + x, 2) * 2 + lax.rem(table[at + 3] + which, 2)
            for c in range(n_ctx):
                ref[x, c] = made[pl.ds(pl.multiple_of((c * 4 + f) * rows, rows), rows), :]


def square_kernel(table, qkv_ref, ff_ref, own_out, *refs):
    f32 = jnp.float32
    others, (square_ref, out_ref, vec_ref) = refs[:-3], refs[-3:]
    n_ctx, rows, wide = qkv_ref.shape
    cols = wide // 4
    at = 4 * n_ctx + 5
    out = own_out[...].astype(f32)
    for other in others:
        out = out + other[...].astype(f32)
    out_ref[...] = out
    small = jnp.sum(qkv_ref[:, :, 3 * cols :].astype(f32), 0)[:8]
    mine = table[at + 2] * 2 + table[at + 3]
    picked = jnp.zeros((8, rows), f32)
    for f in range(4):
        picked = picked + jnp.where(mine == f, small[:, f * rows : (f + 1) * rows], 0.0)
    vec_ref[...] = picked
    n_ff = ff_ref.shape[0] - 16
    bias = ff_ref[n_ff:, : 4 * rows].astype(f32)[0:1]
    squared = jnp.sum(jnp.square(bias), keepdims=True) + jnp.sum(jnp.square(picked), keepdims=True)
    squared = squared + jnp.sum(jnp.sum(jnp.square(ff_ref[:n_ff, :].astype(f32)), 0, keepdims=True), keepdims=True)
    squared = squared + jnp.sum(jnp.sum(jnp.square(out), 0, keepdims=True), keepdims=True)
    qkv = jnp.sum(jnp.square(qkv_ref[:, :, : 3 * cols].astype(f32)), 0)
    squared = squared + jnp.sum(jnp.sum(qkv, 0, keepdims=True), keepdims=True)
    square_ref[...] = jnp.broadcast_to(squared.reshape(1, 1, 1), square_ref.shape)


def clip_of(squares):
    norm = jnp.sqrt(jnp.sum(squares[...], 0)[:, 0:1])
    return norm, jnp.minimum(1.0, max_norm / (norm + 1e-06))


def adam_put(refs, spot, grad, clip):
    weight, first, second = refs[:3]
    new = adamw(weight[spot], grad, first[spot], second[spot], clip)
    for ref, value in zip(refs[3:], (grad,) + new):
        ref[spot] = value


def adam_kernel(*refs):
    f32 = jnp.float32
    squares, qkv_ref, out_ref, ff_ref, vec_ref = refs[:5]
    items = [[refs[5 + 5 * m + n] for m in range(3)] + list(refs[21 + 4 * n : 25 + 4 * n]) for n in range(5)]
    norm, clip = clip_of(squares)
    refs[20][...] = norm
    n_ctx, rows, wide = qkv_ref.shape
    cols = wide // 4
    width = n_ctx * cols
    ff = ff_ref.shape[1]
    own = 4 * rows
    n_ff = 8 * rows
    whole = (slice(None), slice(None))
    for c in range(n_ctx):
        for k in range(3):
            spot = (slice(None), slice(k * width + c * cols, k * width + (c + 1) * cols))
            adam_put(items[0], spot, qkv_ref[c, :, k * cols : (k + 1) * cols].astype(f32), clip)
    adam_put(items[1], whole, out_ref[...], clip)
    for h in range(width // ff):
        spot = (slice(None), slice(h * ff, (h + 1) * ff))
        adam_put(items[2], spot, ff_ref[n_ff + h * own : n_ff + (h + 1) * own, :].astype(f32), clip)
    n_down = n_ff + width // ff * own
    adam_put(items[3], whole, ff_ref[n_down:, :own].astype(f32)[0:1], clip)
    adam_put(items[4], whole, vec_ref[...], clip)


def adam_up_kernel(squares, up_ref, *refs):
    _, clip = clip_of(squares)
    n_plane, rows, ff = up_ref.shape
    own = 4 * rows
    for r in range(n_plane):
        for k in range(ff // own):
            spot = (slice(None), slice((k * n_plane + r) * own, (k * n_plane + r + 1) * own))
            adam_put(refs, spot, up_ref[r, :, k * own : (k + 1) * own].astype(jnp.float32), clip)


in_smem = pl.BlockSpec(memory_space=pltpu.SMEM)
in_vmem = pl.BlockSpec(memory_space=pltpu.VMEM)


def call(kernel, n_scalar, args, shapes, scratch=(), cost=1, limit=60):
    return pl.pallas_call(
        kernel,
        out_shape=[jax.ShapeDtypeStruct(s, d) for s, d in shapes],
        in_specs=[in_smem] * n_scalar + [in_vmem] * (len(args) - n_scalar),
        out_specs=[in_vmem] * len(shapes),
        scratch_shapes=[pltpu.VMEM(s, d) for s, d in scratch],
        compiler_params=pltpu.CompilerParams(vmem_limit_bytes=limit * 1024 * 1024),
        cost_estimate=pl.CostEstimate(flops=cost, bytes_accessed=cost, transcendentals=0),
    )(*args)


def attend_forward(table, slopes, blocks, pieces, start, cols):
    tokens, width = blocks[0].shape
    seq = tokens * len(blocks)
    f32, low = jnp.float32, jnp.bfloat16
    shapes = [
        ((seq, cols), low), ((cols, seq), f32), ((seq, 3 * cols), low), ((8, seq), f32),
        ((seq, width), low), ((seq, width), low), ((width, 3 * cols), low), ((8, width), f32),
    ]
    args = [table, slopes] + list(blocks) + list(pieces) + [start]
    return call(functools.partial(forward_kernel, len(blocks)), 2, args, shapes, [((width, 128), low)], 9000000000, 60)


def local_split(
    inputs, out_grad, segments, pairs,
    w_qkv, w_out, w_up, w_down, up_bias, vectors,
    first_qkv, first_out, first_up, first_down, first_bias, first_vectors,
    second_qkv, second_out, second_up, second_down, second_bias, second_vectors,
):
    low = jnp.bfloat16
    f32 = jnp.float32
    nz = lax.axis_size("z")
    n_ctx = 2 * nz
    every = ("z", "y", "x", "c")
    ctx = ("z", "y")
    plane = ("y", "x", "c")
    zi, yi, xi, ci = (lax.axis_index(a) for a in every)
    ctx_i = zi * 2 + yi
    tokens, width = inputs.shape[1:]
    half = tokens // 2
    seq_len = tokens * n_ctx
    heads_own = HEADS // n_ctx
    cols = heads_own * HD
    rows = w_qkv.shape[0]
    ff_own = w_down.shape[0]
    ff = nz * ff_own
    n_half = width // ff
    field_low = inputs[0]
    field = field_low.astype(f32)
    cot_low = out_grad[0]

    line = [shift(field_low, "z", nz, k) for k in range(1, nz)]
    own_two = exchange(jnp.stack([field_low, cot_low]), "y")
    shapes = [((n_ctx, rows, 3 * cols + 128), low), ((8, rows, ff), low), ((n_half, ff_own, ff), low), ((tokens, width // 4), low)]
    packed = [pairs, w_qkv, vectors, segments, up_bias.reshape(1, ff_own), w_up, w_down, w_out]
    first_send, up_send, down_part, out_low = call(pack_kernel, 1, packed, shapes, limit=60)
    first_got = swap(first_send, ctx)
    up_part = swap(after(up_send, first_got), plane).reshape(8 * rows, ff)
    ff_send = jnp.concatenate([up_part, down_part.reshape(n_half * ff_own, ff)], 0)
    ff_send, first_got, own_two, out_low = gate(ff_send, first_got, own_two, out_low)
    pair_own, cot_y = own_two[0], own_two[1]

    ff_all = lax.all_gather(ff_send, "z", axis=0)
    pair_line = [exchange(v, "y") for v in line]
    rest = [shift(out_low, "z", nz, k) for k in range(1, nz)]
    first_x = exchange(first_got, "x")
    first_c = exchange(first_got, "c")
    first_cx = exchange(first_x, "c")
    cot_two = jnp.stack([cot_low, cot_y])
    cot_x = exchange(cot_two, "x")
    seg_all = first_got[:, 0:2, 3 * cols + 64 :].reshape(seq_len).astype(jnp.int32)
    up_low = []
    for got in (first_got, first_c):
        bias_all = got[:, 2:4, 3 * cols + 64 :].reshape(nz, 2, ff_own)
        bias_all = lax.dynamic_index_in_dim(bias_all, yi, 1, keepdims=False)
        up_low = up_low + [bias_all.reshape(1, ff).astype(f32)]
    pair_all = first_got[:, 4, 3 * cols + 64].astype(jnp.int32)
    start = jnp.sum((seg_all[:, None] < seg_all[None, :]).astype(jnp.int32), 0, keepdims=True)
    slot_block = jnp.stack([pair_all, 2 * n_ctx - 1 - pair_all], 1)
    near = [((zi + k) % nz) * 2 + yi for k in range(nz)]
    near = jnp.stack(near + [((zi + k) % nz) * 2 + 1 - yi for k in range(nz)])
    ids = jnp.arange(n_ctx)
    near_block = jnp.sum(jnp.where((near[:, None] == ids[None, :])[:, :, None], slot_block[None], 0), 1)
    spans = jnp.arange(2 * n_ctx)
    block_slot = jnp.sum(jnp.where(slot_block.reshape(1, -1) == spans[:, None], spans[None, :], 0), 1)
    piece_f = jnp.stack([xi * 2 + ci, (1 - xi) * 2 + ci, xi * 2 + 1 - ci, (1 - xi) * 2 + 1 - ci])
    here = jnp.stack([ctx_i, zi, yi, xi, ci])
    table = jnp.concatenate([near_block.reshape(-1), block_slot, piece_f, here]).astype(jnp.int32)
    head_ids = (ctx_i * heads_own + jnp.arange(heads_own)).astype(f32)
    slopes = jnp.exp2(-8.0 * (head_ids + 1.0) / HEADS)
    out_z = jnp.stack([out_low] + rest)
    first_x, first_c, first_cx, cot_x, table, start, slopes, out_z, *pair_line = gate(
        first_x, first_c, first_cx, cot_x, table, start, slopes, out_z, *pair_line
    )

    out_y = exchange(out_z, "y")
    pieces = (first_got, first_x, first_c, first_cx)
    blocks = [field_low, pair_own] + pair_line + line
    attended, att_t, qkv_low, lse, normed_one, seq_rows, qkv_w, vec = attend_forward(
        table, slopes, blocks, pieces, start, cols
    )
    attended, out_y = gate(attended.reshape(n_ctx, tokens, cols), out_y)

    attended_low = swap(attended, ctx)
    out_zy = jnp.stack([out_z, out_y])
    out_x = exchange(out_zy, "x")
    out_c_two = exchange(out_zy, "c")
    attended_low, out_x, out_c_two = gate(attended_low, out_x, out_c_two)
    cots = [cot_two, cot_x]
    shapes = [((tokens, width), f32), ((tokens, width), low), ((width, width), low)]
    parts = [table, attended_low, out_zy, out_x, out_c_two, exchange(out_x, "c"), field_low, vec]
    resid, mlp_low, out_w = call(project_kernel, 1, parts, shapes)

    mlp_y = exchange(mlp_low, "y")
    mlp_x = exchange(mlp_low, "x")
    mlp_y, mlp_x = gate(mlp_y, mlp_x)
    mlp_d0 = exchange(mlp_x[:half], "y")
    mlp_d1 = exchange(mlp_y[half:], "x")
    ff_other = exchange(after(ff_all, mlp_low), "c")
    mlp_d0, mlp_d1, ff_other = gate(mlp_d0, mlp_d1, ff_other)
    four = 4 * tokens
    one = ((tokens, width), low)
    shapes = [one] * 4 + [((four, 2 * ff), low)] * 2 + [((four, width), low)]
    scratch = [((2 * ff, width), low), ((width, 2 * ff), low)]
    rows_in = [mlp_low, mlp_y, mlp_x, mlp_d0, mlp_d1] + cots + [ff_all, ff_other] + up_low
    norm_own, norm_y, norm_x, norm_d, hidden, grad_pre, mlp_in = call(
        feed_kernel, 0, rows_in, shapes, scratch, limit=60
    )

    norm_d0 = exchange(norm_d[:half], "y")
    norm_d1 = exchange(norm_d[half:], "x")
    n_ff = 8 * rows + n_half * ff_own
    ff_keep, ff_give = call(
        feed_grad_kernel, 0, [mlp_in, grad_pre, hidden] + cots, [((nz, n_ff + 16, ff), low)] * 2, (), 1, 60
    )
    norm_d0, norm_d1, ff_give = gate(norm_d0, norm_d1, ff_give)
    norm_y = jnp.concatenate([norm_y[:half], add_low(norm_y[half:], norm_d1)], 0)
    norm_x = jnp.concatenate([add_low(norm_x[:half], norm_d0), norm_x[half:]], 0)
    norm_y, norm_x, ff_keep = gate(norm_y, norm_x, ff_keep)
    norm_y, norm_x = exchange(norm_y, "y"), exchange(norm_x, "x")
    ff_terms = add_low(ff_keep, exchange(ff_give, "c"))
    ff_sum = lax.psum_scatter(ff_terms, "z", scatter_dimension=0, tiled=True)[0]
    norm_x, norm_y, ff_terms = gate(norm_x, norm_y, ff_terms)
    shapes = [((tokens, width), f32), ((n_ctx, tokens, cols), low), ((8, width), f32)]
    shapes = shapes + [((2, 2, nz, rows, width), low)] * 2
    grad_resid, back_low, resid_sums, out_keep, out_give = call(
        norm_back_kernel,
        1,
        [table, norm_own, norm_x, norm_y, resid, cot_low, vec, out_w, attended_low],
        shapes,
        [((width, width), low)],
    )

    back_all = swap(back_low, ctx)
    out_c_got = exchange(out_give, "c")
    result_keep, result_give = call(
        result_kernel,
        0,
        [after(hidden, back_low), ff_all, ff_other],
        [((2, tokens, width), low)] * 2,
        [((2 * ff, width), low)],
    )
    back_all, out_c_got, result_keep, result_give = gate(back_all, out_c_got, result_keep, result_give)

    out_x_got = exchange(add_low(out_keep[1], out_c_got[1]), "x")
    shapes = [((2, n_ctx, rows, 4 * cols), low)] * 2
    shapes = shapes + [((nz, tokens, width), low)] * 2
    scratch = [((seq_len, 3 * cols), low), ((seq_len, cols), low), ((seq_len, cols), f32), ((seq_len, cols), f32)]
    scratch = scratch + [((seq_len, width), low), ((width, 4 * cols), low)]
    back_all = back_all.reshape(seq_len, cols)
    made = call(
        backward_kernel,
        2,
        [table, slopes, back_all, qkv_low, att_t, lse, start, normed_one, qkv_w, seq_rows, resid_sums],
        shapes,
        scratch,
        9000000000,
        60,
    )
    *made, out_x_got = gate(*made, out_x_got)
    qkv_keep, qkv_give, in_keep, in_give = made

    qkv_c_got = exchange(qkv_give, "c")
    qkv_c = add_low(qkv_keep[0], qkv_c_got[0])
    qkv_x_got = exchange(add_low(qkv_keep[1], qkv_c_got[1]), "x")
    out_c = add_low(out_keep[0], out_c_got[0])
    out_two = add_low(out_c[0], out_x_got[0])
    out_y_got = exchange(add_low(out_c[1], out_x_got[1]), "y")
    in_got = exchange(after(in_give, qkv_c), "y")
    result_x = exchange(after(result_give, qkv_c), "x")
    qkv_x_got, qkv_c, out_y_got = gate(qkv_x_got, qkv_c, out_y_got)
    qkv_x = add_low(qkv_c, qkv_x_got)

    qkv_got = swap(qkv_x, ctx)
    out_y_got = after(out_y_got, qkv_x)
    out_own = add_low(out_two[0], out_y_got[0])
    out_moved = [shift(add_low(out_two[k], out_y_got[k]), "z", nz, -k) for k in range(1, nz)]
    up_send = after(ff_sum, qkv_x)[: 8 * rows].reshape(8, rows, ff)
    result_x = after(result_x, qkv_x)
    result_y = exchange(add_low(result_keep[1], result_x[1]), "y")
    qkv_got, in_got, up_send, *out_moved = gate(qkv_got, in_got, up_send, *out_moved)
    shapes = [((4 * n_ctx, 1, 128), f32), ((rows, width), f32), ((8, rows), f32)]
    squared, grad_out_own, grad_vec_own = call(
        square_kernel, 1, [table, qkv_got, ff_sum, out_own, *out_moved], shapes, limit=48
    )

    squares = swap(squared, every)
    in_z = [shift(add_low(in_keep[k], in_got[k]), "z", nz, -k) for k in range(1, nz)]
    up_got = swap(after(up_send, squares), plane)
    masters = [w_qkv, w_out, w_down, up_bias.reshape(1, ff_own), vectors]
    firsts = [first_qkv, first_out, first_down, first_bias.reshape(1, ff_own), first_vectors]
    seconds = [second_qkv, second_out, second_down, second_bias.reshape(1, ff_own), second_vectors]
    shapes = [((1, 1), f32)]
    for item in masters:
        shapes = shapes + [(item.shape, f32)] * 4
    grads = [squares, qkv_got, grad_out_own, ff_sum, grad_vec_own]
    grad_norm, *results = call(adam_kernel, 0, grads + masters + firsts + seconds, shapes, limit=60)
    for k in range(12, 16):
        results[k] = results[k].reshape(ff_own)
    ups = call(adam_up_kernel, 0, [squares, up_got, w_up, first_up, second_up], [(w_up.shape, f32)] * 4, limit=60)
    results = results[:8] + list(ups) + results[8:]

    result_y = after(result_y, squares)
    result = (resid + result_keep[0].astype(f32) + result_x[0].astype(f32) + result_y.astype(f32) + vec[7]).astype(low)
    own_grads = in_keep[0].astype(f32) + in_got[0].astype(f32)
    for other in gate(*in_z, grad_norm)[:-1]:
        own_grads = own_grads + other.astype(f32)
    norm_one_back = jax.vjp(lambda v: layer_norm(v, vec[0], vec[1]), field)[1]
    in_grad = grad_resid + norm_one_back(own_grads)[0]
    return (result[None], in_grad[None], grad_norm[0, 0], *results)


def solution(mesh):
    n_ctx = mesh.shape["ctx"]
    if HEADS % n_ctx == 0 and n_ctx % 2 == 0 and mesh.shape["fsdp"] == 4:
        body = local_split
        ctx, fsdp = ("z", "y"), ("x", "c")
        mesh = Mesh(mesh.devices.reshape(n_ctx // 2, 2, 2, 2), ctx + fsdp)
    else:
        body = local
        ctx, fsdp = ("ctx",), ("fsdp",)
    rows = P(fsdp, ctx, None)
    flat = P(fsdp, ctx)
    mat = P(ctx + fsdp, None)
    vec = P(ctx + fsdp)
    wide = P(None, ctx + fsdp)
    group = (mat, mat, mat, mat, vec, wide)
    outs = ()
    for spec in group:
        outs = outs + (spec,) * 4
    return jax.shard_map(
        body,
        mesh=mesh,
        in_specs=(rows, rows, flat, flat) + group * 3,
        out_specs=(rows, rows, P()) + outs,
        check_vma=False,
    )
```

```python
import functools
import math

import jax
import jax.numpy as jnp
from jax import lax
from jax.experimental import pallas as pl
from jax.experimental.pallas import tpu as pltpu
from jax.sharding import Mesh
from jax.sharding import PartitionSpec as P

HEADS = 16
HD = 64


norm_eps = 1e-05
beta_one = 0.9
beta_two = 0.95
adam_eps = 1e-08
learn_rate = 0.02
weight_decay = 0.1
adam_step = 10
max_norm = 1.0
masked = -1e30
group_heads = 2


def layer_norm(field, gain, shift):
    center = field - jnp.mean(field, -1, keepdims=True)
    spread = jnp.mean(center * center, -1, keepdims=True)
    return center * lax.rsqrt(spread + norm_eps) * gain + shift


def gelu_exact(field):
    return jax.nn.gelu(field, approximate=False)


def contract(left, right, left_dim, right_dim):
    return lax.dot_general(
        left, right, (((left_dim,), (right_dim,)), ((), ())), preferred_element_type=jnp.float32
    )


def place(pair_ids, block, n_ctx):
    blocks = jnp.stack([pair_ids, 2 * n_ctx - 1 - pair_ids], 1).reshape(-1)
    offsets = jnp.arange(block, dtype=jnp.int32)
    return (blocks[:, None] * block + offsets[None, :]).reshape(-1)


def pick(array, first):
    return lax.dynamic_slice_in_dim(array, first, group_heads, 1)


def adamw(weight, grad, first, second, clip):
    clipped = grad * clip
    first_new = beta_one * first + (1.0 - beta_one) * clipped
    second_new = beta_two * second + (1.0 - beta_two) * clipped * clipped
    first_hat = first_new / (1.0 - beta_one**adam_step)
    second_hat = second_new / (1.0 - beta_two**adam_step)
    update = -learn_rate * (first_hat / (jnp.sqrt(second_hat) + adam_eps) + weight_decay * weight)
    return (update, first_new, second_new)


def local(
    inputs,
    out_grad,
    segments,
    pairs,
    w_qkv,
    w_out,
    w_up,
    w_down,
    up_bias,
    vectors,
    first_qkv,
    first_out,
    first_up,
    first_down,
    first_bias,
    first_vectors,
    second_qkv,
    second_out,
    second_up,
    second_down,
    second_bias,
    second_vectors,
):
    low_type = jnp.bfloat16
    n_ctx = lax.axis_size("ctx")
    field = inputs[0].astype(jnp.float32)
    tokens = field.shape[0]
    block = tokens // 2
    width = field.shape[1]
    seq_len = tokens * n_ctx
    scale = HD ** (-0.5)
    groups = HEADS // group_heads
    slope = 2.0 ** (-8.0 * (jnp.arange(HEADS, dtype=jnp.float32) + 1.0) / HEADS)
    qkv_w, out_w, vec_low = (
        lax.all_gather(w_qkv.astype(low_type), ("ctx", "fsdp"), axis=0, tiled=True),
        lax.all_gather(w_out.astype(low_type), ("ctx", "fsdp"), axis=0, tiled=True),
        lax.all_gather(vectors.astype(low_type), ("ctx", "fsdp"), axis=1, tiled=True),
    )
    vec = vec_low.astype(jnp.float32)
    gain_one, shift_one, gain_two, shift_two = (vec[0], vec[1], vec[2], vec[3])
    bias_query, bias_value, bias_out, bias_down = (vec[4], vec[5], vec[6], vec[7])
    normed_one = layer_norm(field, gain_one, shift_one)
    attn_in = normed_one.astype(low_type)
    mixed = jnp.dot(attn_in, qkv_w, preferred_element_type=jnp.float32)
    query = (mixed[:, :width] + bias_query).astype(low_type)
    keys = mixed[:, width : 2 * width].astype(low_type)
    values = (mixed[:, 2 * width :] + bias_value).astype(low_type)
    pair_ids = pairs[0]
    kv_all, pair_all, seg_all = (
        lax.all_gather(jnp.concatenate([keys, values], 1), "ctx", axis=0, tiled=True),
        lax.all_gather(pair_ids, "ctx", axis=0, tiled=True),
        lax.all_gather(segments[0], "ctx", axis=0, tiled=True),
    )
    pos_query = place(pair_ids, block, n_ctx)
    pos_key = place(pair_all, block, n_ctx)
    seg_query = jnp.take(seg_all, pos_query)
    seg_key = jnp.take(seg_all, pos_key)
    relative = (pos_key[None, :] - pos_query[:, None]).astype(jnp.float32)
    allowed = (seg_query[:, None] == seg_key[None, :]) & (pos_key[None, :] <= pos_query[:, None])
    query_heads = query.reshape(tokens, HEADS, HD)
    key_heads = kv_all[:, :width].reshape(seq_len, HEADS, HD)
    value_heads = kv_all[:, width:].reshape(seq_len, HEADS, HD)

    def scores_of(query_part, key_part, first, offsets, visible):
        slopes = lax.dynamic_slice_in_dim(slope, first, group_heads, 0)
        raw = (
            jnp.einsum("rhe,khe->hrk", query_part, key_part, preferred_element_type=jnp.float32)
            * scale
        )
        raw = raw + slopes[:, None, None] * offsets[None]
        return jnp.where(visible[None], raw, masked)

    def forward_group(index, carry):
        attended, log_total = carry
        first = index * group_heads
        scores = scores_of(
            pick(query_heads, first), pick(key_heads, first), first, relative, allowed
        )
        top = jnp.max(scores, -1, keepdims=True)
        expo = jnp.exp(scores - top)
        total = jnp.sum(expo, -1, keepdims=True)
        chance_low = (expo / total).astype(low_type)
        part_out = jnp.einsum(
            "hrk,khe->rhe", chance_low, pick(value_heads, first), preferred_element_type=jnp.float32
        )
        attended = lax.dynamic_update_slice_in_dim(attended, part_out, first, 1)
        log_total = lax.dynamic_update_slice_in_dim(
            log_total, (top + jnp.log(total))[:, :, 0].T, first, 1
        )
        return (attended, log_total)

    attended, log_total = lax.fori_loop(
        0,
        groups,
        forward_group,
        (jnp.zeros((tokens, HEADS, HD), jnp.float32), jnp.zeros((tokens, HEADS), jnp.float32)),
    )
    attended_low = attended.reshape(tokens, width).astype(low_type)
    resid = field + jnp.dot(attended_low, out_w, preferred_element_type=jnp.float32) + bias_out
    normed_two = layer_norm(resid, gain_two, shift_two)
    mlp_in = normed_two.astype(low_type)
    up_w, down_w, up_low = (
        lax.all_gather(w_up.astype(low_type), ("ctx", "fsdp"), axis=0, tiled=True),
        lax.all_gather(w_down.astype(low_type), ("ctx", "fsdp"), axis=0, tiled=True),
        lax.all_gather(up_bias.astype(low_type), ("ctx", "fsdp"), axis=0, tiled=True),
    )
    pre = jnp.dot(mlp_in, up_w, preferred_element_type=jnp.float32) + up_low.astype(jnp.float32)
    hidden = gelu_exact(pre).astype(low_type)
    result = resid + jnp.dot(hidden, down_w, preferred_element_type=jnp.float32) + bias_down
    cotangent_low = out_grad[0]
    cotangent = cotangent_low.astype(jnp.float32)
    up_back, down_back = (
        lax.all_gather(w_up.astype(low_type), ("ctx", "fsdp"), axis=0, tiled=True),
        lax.all_gather(w_down.astype(low_type), ("ctx", "fsdp"), axis=0, tiled=True),
    )
    grad_down_term = contract(hidden, cotangent_low, 0, 0)
    grad_bias_down = jnp.sum(cotangent, 0)
    grad_hidden = contract(cotangent_low, down_back, 1, 1)
    gelu_back = jax.vjp(gelu_exact, pre)[1]
    grad_pre = gelu_back(grad_hidden)[0].astype(low_type)
    grad_up_bias = jnp.sum(grad_pre.astype(jnp.float32), 0)
    grad_up_term = contract(mlp_in, grad_pre, 0, 0)
    grad_normed_two = contract(grad_pre, up_back, 1, 1)
    norm_two_back = jax.vjp(layer_norm, resid, gain_two, shift_two)[1]
    grad_resid_norm, grad_gain_two, grad_shift_two = norm_two_back(grad_normed_two)
    grad_resid = cotangent + grad_resid_norm
    grad_up_own, grad_down_own, grad_bias_own = (
        lax.psum_scatter(grad_up_term, ("ctx", "fsdp"), scatter_dimension=0, tiled=True),
        lax.psum_scatter(grad_down_term, ("ctx", "fsdp"), scatter_dimension=0, tiled=True),
        lax.psum_scatter(grad_up_bias, ("ctx", "fsdp"), scatter_dimension=0, tiled=True),
    )
    qkv_back, out_back = (
        lax.all_gather(w_qkv.astype(low_type), ("ctx", "fsdp"), axis=0, tiled=True),
        lax.all_gather(w_out.astype(low_type), ("ctx", "fsdp"), axis=0, tiled=True),
    )
    grad_bias_out = jnp.sum(grad_resid, 0)
    resid_low = grad_resid.astype(low_type)
    grad_out_term = contract(attended_low, resid_low, 0, 0)
    back_low = contract(resid_low, out_back, 1, 1).astype(low_type)
    back_heads = back_low.reshape(tokens, HEADS, HD)

    def backward_group(index, carry):
        grad_query, grad_key, grad_value = carry
        first = index * group_heads
        query_part = pick(query_heads, first)
        key_part = pick(key_heads, first)
        value_part = pick(value_heads, first)
        back_part = pick(back_heads, first)
        scores = scores_of(query_part, key_part, first, relative, allowed)
        logsum = lax.dynamic_slice_in_dim(log_total, first, group_heads, 1).T
        chance = jnp.exp(scores - logsum[:, :, None])
        pushed = jnp.einsum(
            "rhe,khe->hrk", back_part, value_part, preferred_element_type=jnp.float32
        )
        centre = jnp.sum(chance * pushed, -1, keepdims=True)
        dscore = (chance * (pushed - centre)).astype(low_type)
        chance_low = chance.astype(low_type)
        part_query = (
            jnp.einsum("hrk,khe->rhe", dscore, key_part, preferred_element_type=jnp.float32) * scale
        )
        part_key = (
            jnp.einsum("hrk,rhe->khe", dscore, query_part, preferred_element_type=jnp.float32)
            * scale
        )
        part_value = jnp.einsum(
            "hrk,rhe->khe", chance_low, back_part, preferred_element_type=jnp.float32
        )
        grad_query = lax.dynamic_update_slice_in_dim(grad_query, part_query, first, 1)
        grad_key = lax.dynamic_update_slice_in_dim(grad_key, part_key, first, 1)
        grad_value = lax.dynamic_update_slice_in_dim(grad_value, part_value, first, 1)
        return (grad_query, grad_key, grad_value)

    zero_keys = jnp.zeros((seq_len, HEADS, HD), jnp.float32)
    grad_query, grad_key, grad_value = lax.fori_loop(
        0,
        groups,
        backward_group,
        (jnp.zeros((tokens, HEADS, HD), jnp.float32), zero_keys, zero_keys),
    )
    own_key, own_value = (
        lax.psum_scatter(
            grad_key.reshape(seq_len, width).astype(jnp.bfloat16),
            "ctx",
            scatter_dimension=0,
            tiled=True,
        ).astype(jnp.float32),
        lax.psum_scatter(
            grad_value.reshape(seq_len, width).astype(jnp.bfloat16),
            "ctx",
            scatter_dimension=0,
            tiled=True,
        ).astype(jnp.float32),
    )
    grad_query_low = grad_query.reshape(tokens, width).astype(low_type)
    grad_key_low = own_key.astype(low_type)
    grad_value_low = own_value.astype(low_type)
    grad_mixed = jnp.concatenate([grad_query_low, grad_key_low, grad_value_low], 1)
    grad_bias_query = jnp.sum(grad_query_low.astype(jnp.float32), 0)
    grad_bias_value = jnp.sum(grad_value_low.astype(jnp.float32), 0)
    grad_qkv_term = contract(attn_in, grad_mixed, 0, 0)
    grad_normed_one = contract(grad_mixed, qkv_back, 1, 1)
    norm_one_back = jax.vjp(layer_norm, field, gain_one, shift_one)[1]
    grad_field_norm, grad_gain_one, grad_shift_one = norm_one_back(grad_normed_one)
    in_grad = grad_resid + grad_field_norm
    grad_vec_term = jnp.stack(
        [
            grad_gain_one,
            grad_shift_one,
            grad_gain_two,
            grad_shift_two,
            grad_bias_query,
            grad_bias_value,
            grad_bias_out,
            grad_bias_down,
        ],
        0,
    )
    grad_qkv_own, grad_out_own, grad_vec_own = (
        lax.psum_scatter(grad_qkv_term, ("ctx", "fsdp"), scatter_dimension=0, tiled=True),
        lax.psum_scatter(grad_out_term, ("ctx", "fsdp"), scatter_dimension=0, tiled=True),
        lax.psum_scatter(grad_vec_term, ("ctx", "fsdp"), scatter_dimension=1, tiled=True),
    )
    grads = (grad_qkv_own, grad_out_own, grad_up_own, grad_down_own, grad_bias_own, grad_vec_own)
    local_squares = sum([jnp.sum(item * item) for item in grads])
    grad_norm = jnp.sqrt(lax.psum(local_squares, ("ctx", "fsdp")))
    clip = jnp.minimum(1.0, max_norm / (grad_norm + 1e-06))
    masters = (w_qkv, w_out, w_up, w_down, up_bias, vectors)
    firsts = (first_qkv, first_out, first_up, first_down, first_bias, first_vectors)
    seconds = (second_qkv, second_out, second_up, second_down, second_bias, second_vectors)
    results = []
    for weight, grad, first, second in zip(masters, grads, firsts, seconds):
        update, first_new, second_new = adamw(weight, grad, first, second, clip)
        results = results + [grad, update, first_new, second_new]
    return (
        result.astype(low_type)[None],
        in_grad[None],
        grad_norm,
        results[0],
        results[1],
        results[2],
        results[3],
        results[4],
        results[5],
        results[6],
        results[7],
        results[8],
        results[9],
        results[10],
        results[11],
        results[12],
        results[13],
        results[14],
        results[15],
        results[16],
        results[17],
        results[18],
        results[19],
        results[20],
        results[21],
        results[22],
        results[23],
    )


def exchange(v, axis):
    return lax.ppermute(v, axis, [(0, 1), (1, 0)])


def shift(v, axis, n_line, k):
    return lax.ppermute(v, axis, [(i, (i - k) % n_line) for i in range(n_line)])


def swap(v, axes):
    return lax.all_to_all(v, axes, 0, 0, tiled=True)


def gate(*values):
    return lax.optimization_barrier(values)


def after(v, *others):
    return lax.optimization_barrier((v,) + others)[0]


def order_two(own, other, axis, dim):
    first = lax.axis_index(axis) == 0
    return jnp.stack([jnp.where(first, own, other), jnp.where(first, other, own)], dim)


def split_two(part, axis, dim):
    me = lax.axis_index(axis)
    keep = lax.dynamic_index_in_dim(part, me, dim, keepdims=False)
    return keep, lax.dynamic_index_in_dim(part, 1 - me, dim, keepdims=False)


def add_low(keep, got):
    return (keep.astype(jnp.float32) + got.astype(jnp.float32)).astype(jnp.bfloat16)


def line_gives(part, axis, n_line):
    me = lax.axis_index(axis)
    blocks = [lax.dynamic_index_in_dim(part, (me + k) % n_line, 0, keepdims=False) for k in range(n_line)]
    return blocks[0], [shift(blocks[k], axis, n_line, -k) for k in range(1, n_line)]


def line_order(parts, axis):
    n_line = len(parts)
    first = (n_line - lax.axis_index(axis)) % n_line
    return lax.dynamic_slice_in_dim(jnp.concatenate([jnp.stack(parts)] * 2, 0), first, n_line, 0)


def lanes_of(head, shape):
    return lax.broadcasted_iota(jnp.int32, shape, 1) // HD == head


def head_parts(query, keys, slope, head):
    seq = keys.shape[0]
    lane = lax.broadcasted_iota(jnp.int32, keys.shape, 1)
    own = lane // HD == head
    spot = lane - (1 - head) * HD
    bias = lax.broadcasted_iota(jnp.int32, (seq, 1), 0).astype(jnp.float32) * (slope * HD**0.5)
    high = bias.astype(jnp.bfloat16)
    rest = bias - high.astype(jnp.float32)
    middle = rest.astype(jnp.bfloat16)
    small = (rest - middle.astype(jnp.float32)).astype(jnp.bfloat16)
    zero = jnp.zeros_like(keys)
    extra = jnp.where(spot == 0, high, jnp.where(spot == 1, middle, jnp.where(spot == 2, small, zero)))
    ones = jnp.where((spot >= 0) & (spot <= 2), jnp.ones_like(keys), zero)
    return jnp.where(own, query, ones), jnp.where(own, keys, extra)


def visible(start, tile, at, size):
    key = lax.broadcasted_iota(jnp.int32, (size, tile), 0)
    seen = key >= start
    return seen & (key <= lax.broadcasted_iota(jnp.int32, (size, tile), 1) + at)


def forward_kernel(n_refs, meta, slopes, *refs):
    pieces = refs[n_refs : n_refs + 4]
    start_ref = refs[n_refs + 4]
    att_ref, att_t, qkv_ref, lse_ref, normed, x_ref, w_ref, vec_ref, extra = refs[n_refs + 5 :]
    n_line = n_refs // 2
    own, pair, pair_line, line = refs[0], refs[1], refs[2 : 1 + n_line], refs[1 + n_line : n_refs]
    n_blocks = 2 * n_line

    def block_part(b, span):
        z, other = b % n_line, b // n_line
        if z == 0:
            return (pair if other else own)[span, :]
        return pair_line[z - 1][span, :] if other else line[z - 1][span, :]

    f32, low = jnp.float32, jnp.bfloat16
    n_ctx, rows, _ = pieces[0].shape
    tokens, width = own.shape
    half = tokens // 2
    seq = tokens * n_blocks
    cols = qkv_ref.shape[1] // 3
    spans = 2 * n_blocks
    for c in range(n_ctx):
        for p in range(4):
            piece = pieces[p][c]
            to = pl.ds(pl.multiple_of(c * 4 * rows + meta[2 * spans + p] * rows, rows), rows)
            w_ref[to, :] = piece[:, : 3 * cols]
            extra[to, :] = piece[:, 3 * cols :]
    pick_rows = (
        lax.broadcasted_iota(jnp.int32, (8, 128), 0) == lax.broadcasted_iota(jnp.int32, (8, 128), 1)
    ).astype(low)
    vec = contract(pick_rows, extra[...], 1, 1)
    vec_ref[...] = vec
    gain, move = vec[0:1], vec[1:2]
    for j in range(spans):
        part = block_part(j // 2, slice((j % 2) * half, (j % 2 + 1) * half))
        to = pl.ds(pl.multiple_of(meta[j] * half, half), half)
        x_ref[to, :] = part
        normed[to, :] = layer_norm(part.astype(f32), gain, move).astype(low)
    at = pl.ds(pl.multiple_of(meta[2 * spans + 4] * cols, cols), cols)
    bias_q, bias_v = vec_ref[4:5, at], vec_ref[5:6, at]
    tile = min(256, seq)
    for t in range(seq // tile):
        span = pl.ds(t * tile, tile)
        mixed = jnp.dot(normed[span, :], w_ref[...], preferred_element_type=f32)
        qkv_ref[span, :cols] = (mixed[:, :cols] + bias_q).astype(low)
        qkv_ref[span, cols : 2 * cols] = mixed[:, cols : 2 * cols].astype(low)
        qkv_ref[span, 2 * cols :] = (mixed[:, 2 * cols :] + bias_v).astype(low)
    factor = HD**-0.5 * 1.4426950408889634
    query, keys, values = qkv_ref[:, :cols], qkv_ref[:, cols : 2 * cols], qkv_ref[:, 2 * cols :]
    lse_ref[...] = jnp.zeros_like(lse_ref)
    for h in range(cols // HD):
        q_h, k_h = head_parts(query, keys, slopes[h], h)
        v_h = jnp.where(lanes_of(h, values.shape), values, jnp.zeros_like(values))
        for t in range(seq // tile):
            size = (t + 1) * tile
            span = slice(t * tile, (t + 1) * tile)
            score = contract(k_h[:size], q_h[span], 1, 1) * factor
            score = jnp.where(visible(start_ref[:, span], tile, t * tile, size), score, masked)
            top = jnp.max(score, 0, keepdims=True)
            expo = jnp.exp2(score - top)
            total = jnp.sum(expo, 0, keepdims=True)
            lse_ref[h : h + 1, span] = top + jnp.log2(total)
            part = contract(v_h[:size], expo.astype(low), 0, 0) / total
            att_t[:, span] = part if h == 0 else att_t[:, span] + part
    for t in range(seq // tile):
        span = slice(t * tile, (t + 1) * tile)
        x_tile = att_t[:, span].T.astype(low)
        for u in range(tile // half):
            b = t * (tile // half) + u
            to = meta[spans + b]
            att_ref[pl.ds(pl.multiple_of(to * half, half), half), :] = x_tile[u * half : (u + 1) * half]


def pack_kernel(pairs, w_qkv, vectors, segments, up_bias, w_up, w_down, w_out, first_ref, up_ref, down_ref, out_ref):
    low, f32 = jnp.bfloat16, jnp.float32
    n_ctx, rows, wide = first_ref.shape
    cols = (wide - 128) // 3
    width = n_ctx * cols
    row = lax.broadcasted_iota(jnp.int32, (rows, 128), 0)
    lane = lax.broadcasted_iota(jnp.int32, (rows, 128), 1)
    one_hot = lax.broadcasted_iota(jnp.int32, (8, 128), 0) == lax.broadcasted_iota(jnp.int32, (8, 128), 1)
    columns = contract(vectors[...].astype(low), one_hot.astype(low), 0, 0)
    seg, bias = segments[...].astype(f32), up_bias[...]
    lines = [pltpu.roll(seg, 64, 1), seg, pltpu.roll(bias, 64, 1), bias]
    extra = jnp.where(lane < 8, columns, 0.0)
    for k in range(4):
        extra = jnp.where((row == k) & (lane >= 64), lines[k], extra)
    extra = jnp.where((row == 4) & (lane >= 64), pairs[0, 0].astype(f32), extra).astype(low)
    for c in range(n_ctx):
        for k in range(3):
            first_ref[c, :, k * cols : (k + 1) * cols] = w_qkv[:, k * width + c * cols : k * width + (c + 1) * cols].astype(low)
        first_ref[c, :, 3 * cols :] = extra
    n_plane, _, ff = up_ref.shape
    own = ff // (n_ctx // 2)
    for r in range(n_plane):
        for k in range(n_ctx // 2):
            up_ref[r, :, k * own : (k + 1) * own] = w_up[:, (k * n_plane + r) * own : (k * n_plane + r + 1) * own].astype(low)
    for k in range(down_ref.shape[0]):
        down_ref[k] = w_down[:, k * ff : (k + 1) * ff].astype(low)
    wide_out = out_ref.shape[1]
    for k in range(out_ref.shape[0] // rows):
        out_ref[k * rows : (k + 1) * rows, :] = w_out[:, k * wide_out : (k + 1) * wide_out].astype(low)


def project_kernel(table, att, own_ref, x_ref, c_ref, cx_ref, field, vec, resid_ref, mlp_ref, w_ref):
    low, f32 = jnp.bfloat16, jnp.float32
    n_ctx, tokens, cols = att.shape
    n_line = own_ref.shape[1]
    rows = w_ref.shape[0] // (8 * n_line)
    wide = own_ref.shape[3]
    at = 4 * n_ctx + 5
    zi, yi, xi, ci = (table[at + k] for k in range(4))
    for q, ref in enumerate((own_ref, x_ref, c_ref, cx_ref)):
        for p in range(2):
            for k in range(n_line):
                z = lax.rem(zi + k, n_line)
                y = lax.rem(yi + p, 2)
                x = lax.rem(xi + q % 2, 2)
                to = ((z * 2 + y) * 4 + x * 2 + lax.rem(ci + q // 2, 2)) * rows
                for part in range(tokens // rows):
                    spot = (pl.ds(pl.multiple_of(to, rows), rows), slice(part * wide, (part + 1) * wide))
                    w_ref[spot] = ref[p, k, part * rows : (part + 1) * rows, :]
    heads = jnp.concatenate([att[c] for c in range(n_ctx)], 1)
    moved = jnp.dot(heads, w_ref[...], preferred_element_type=f32)
    resid = field[...].astype(f32) + moved + vec[6:7]
    resid_ref[...] = resid
    mlp_ref[...] = layer_norm(resid, vec[2:3], vec[3:4]).astype(low)


def both_down(parts, down):
    ff = down.shape[0] // 2
    n_line = parts[0].shape[0]
    own = ff // n_line
    n_half = down.shape[1] // ff
    up_rows = parts[0].shape[1] - n_half * own
    for c, part in enumerate(parts):
        for k in range(n_line):
            for h in range(n_half):
                rows = slice(up_rows + h * own, up_rows + (h + 1) * own)
                down[c * ff + k * own : c * ff + (k + 1) * own, h * ff : (h + 1) * ff] = part[k, rows, :]


def feed_kernel(
    m_own, m_y, m_x, m_d0, m_d1, cot_0, cot_1, ff_own, ff_other, bias_own, bias_other,
    norm_own, norm_y, norm_x, norm_d, hidden_ref, pre_ref, mlp_ref, down, up,
):
    low, f32 = jnp.bfloat16, jnp.float32
    tokens, width = m_own.shape
    half = tokens // 2
    n_line, _, ff = ff_own.shape
    up_rows = width // n_line
    for c, part in enumerate((ff_own, ff_other)):
        for k in range(n_line):
            up[k * up_rows : (k + 1) * up_rows, c * ff : (c + 1) * ff] = part[k, :up_rows, :]
    both_down((ff_own, ff_other), down)
    bias = jnp.concatenate([bias_own[...], bias_other[...]], 1)
    for n, block in enumerate((m_own, m_y, m_x)):
        mlp_ref[n * tokens : (n + 1) * tokens, :] = block[...]
    mlp_ref[3 * tokens : 3 * tokens + half, :] = m_d0[...]
    mlp_ref[3 * tokens + half :, :] = m_d1[...]
    for t in range(2):
        span = slice(2 * t * tokens, 2 * (t + 1) * tokens)
        cot = (cot_0, cot_1)[t][...].reshape(2 * tokens, width)
        grads = []
        for c in range(2):
            cut = slice(c * ff, (c + 1) * ff)
            pre = jnp.dot(mlp_ref[span, :], up[:, cut], preferred_element_type=f32) + bias[:, cut]
            cdf = 0.5 * (1.0 + lax.erf(pre * 0.7071067811865476))
            pdf = jnp.exp(-0.5 * pre * pre) * 0.3989422804014327
            hidden_ref[span, cut] = (pre * cdf).astype(low)
            grad = (contract(cot, down[cut, :], 1, 1) * (cdf + pre * pdf)).astype(low)
            pre_ref[span, cut] = grad
            grads = grads + [grad]
        part = contract(jnp.concatenate(grads, 1), up[...], 1, 1).astype(low)
        first, second = ((norm_own, norm_y), (norm_x, norm_d))[t]
        first[...] = part[:tokens]
        second[...] = part[tokens:]


def feed_grad_kernel(mlp_ref, pre_ref, hidden_ref, cot_0, cot_1, keep_ref, give_ref):
    low, f32 = jnp.bfloat16, jnp.float32
    seq, width = mlp_ref.shape
    n_line, _, ff = keep_ref.shape
    own, up_rows, n_half = ff // n_line, width // n_line, width // ff
    cot = jnp.concatenate([ref[...].reshape(seq // 2, width) for ref in (cot_0, cot_1)], 0)
    for c, ref in enumerate((keep_ref, give_ref)):
        cut = slice(c * ff, (c + 1) * ff)
        down = contract(hidden_ref[:, cut], cot, 0, 0).astype(low)
        sums = jnp.sum(pre_ref[:, cut].astype(f32), 0, keepdims=True)
        pad = ref.shape[1] - up_rows - n_half * own
        up = contract(mlp_ref[...], pre_ref[:, cut], 0, 0).astype(low)
        for k in range(n_line):
            ref[k, :up_rows, :] = up[k * up_rows : (k + 1) * up_rows]
            for h in range(n_half):
                part = down[k * own : (k + 1) * own, h * ff : (h + 1) * ff]
                ref[k, up_rows + h * own : up_rows + (h + 1) * own, :] = part
            line = jnp.concatenate([sums[:, k * own : (k + 1) * own], jnp.zeros((1, ff - own), f32)], 1)
            ref[k, up_rows + n_half * own :, :] = jnp.broadcast_to(line, (pad, ff)).astype(low)


def result_kernel(hidden_ref, ff_own, ff_other, keep_ref, give_ref, down):
    both_down((ff_own, ff_other), down)
    half = hidden_ref.shape[0] // 2
    for t, ref in enumerate((keep_ref, give_ref)):
        part = jnp.dot(hidden_ref[t * half : (t + 1) * half, :], down[...], preferred_element_type=jnp.float32)
        ref[...] = part.astype(jnp.bfloat16).reshape(ref.shape)


def norm_back_kernel(
    table, own, got_x, got_y, resid_ref, cot_ref, vec, w_ref, att, grad_ref, back_ref, sums_ref, keep_ref, give_ref, terms
):
    low, f32 = jnp.bfloat16, jnp.float32
    grad = own[...].astype(f32) + got_x[...].astype(f32) + got_y[...].astype(f32)
    resid = resid_ref[...]
    center = resid - jnp.mean(resid, -1, keepdims=True)
    sharp = lax.rsqrt(jnp.mean(center * center, -1, keepdims=True) + norm_eps)
    unit = center * sharp
    scaled = grad * vec[2:3]
    inner = scaled - jnp.mean(scaled, -1, keepdims=True) - unit * jnp.mean(scaled * unit, -1, keepdims=True)
    cot = cot_ref[...].astype(f32)
    total = cot + inner * sharp
    grad_ref[...] = total
    rounded = total.astype(low)
    back = contract(rounded, w_ref[...], 1, 1).astype(low)
    n_ctx, _, cols = back_ref.shape
    for c in range(n_ctx):
        back_ref[c] = back[:, c * cols : (c + 1) * cols]
    row = lax.broadcasted_iota(jnp.int32, sums_ref.shape, 0)
    sums = jnp.where(row == 2, jnp.sum(grad * unit, 0, keepdims=True), 0.0)
    sums = jnp.where(row == 3, jnp.sum(grad, 0, keepdims=True), sums)
    sums = jnp.where(row == 6, jnp.sum(total, 0, keepdims=True), sums)
    sums_ref[...] = jnp.where(row == 7, jnp.sum(cot, 0, keepdims=True), sums)
    for c in range(n_ctx):
        terms[c * cols : (c + 1) * cols, :] = contract(att[c], rounded, 0, 0).astype(low)
    n_line, rows = keep_ref.shape[2:4]
    at = 4 * n_ctx + 5
    for which, ref in enumerate((keep_ref, give_ref)):
        for q in range(4 * n_line):
            x, y, z = q // (2 * n_line), q // n_line % 2, q % n_line
            chip = (lax.rem(table[at] + z, n_line) * 2 + lax.rem(table[at + 1] + y, 2)) * 4
            to = (chip + lax.rem(table[at + 2] + x, 2) * 2 + lax.rem(table[at + 3] + which, 2)) * rows
            ref[x, y, z] = terms[pl.ds(pl.multiple_of(to, rows), rows), :]


def backward_kernel(
    table, slopes, back_ref, qkv_ref, att_t, lse_ref, start_ref, normed, w_ref, x_ref, sums_ref,
    keep_ref, give_ref, in_keep, in_give, mixed_ref, back, d_key, d_value, moved, made,
):
    f32, low = jnp.float32, jnp.bfloat16
    seq, cols = back_ref.shape
    n_ctx, rows = keep_ref.shape[1:3]
    width = w_ref.shape[0]
    spans = 2 * n_ctx
    half = seq // spans
    for b in range(spans):
        back[b * half : (b + 1) * half, :] = back_ref[pl.ds(pl.multiple_of(table[spans + b] * half, half), half), :]
    factor = HD**-0.5 * 1.4426950408889634
    query, keys, values = qkv_ref[:, :cols], qkv_ref[:, cols : 2 * cols], qkv_ref[:, 2 * cols :]
    grads = back[...]
    product = att_t[...] * grads.astype(f32).T
    tile = min(256, seq)
    d_query = [None] * (seq // tile)
    for h in range(cols // HD):
        q_h, k_h = head_parts(query, keys, slopes[h], h)
        own = lanes_of(h, values.shape)
        zero = jnp.zeros_like(values)
        v_h, g_h = jnp.where(own, values, zero), jnp.where(own, grads, zero)
        qq_h, kk_h = jnp.where(own, query, zero), jnp.where(own, keys, zero)
        delta = jnp.sum(product[h * HD : (h + 1) * HD], 0, keepdims=True)
        for t in reversed(range(seq // tile)):
            size = (t + 1) * tile
            span = slice(t * tile, (t + 1) * tile)
            score = contract(k_h[:size], q_h[span], 1, 1) * factor
            score = jnp.where(visible(start_ref[:, span], tile, t * tile, size), score, masked)
            chance = jnp.exp2(score - lse_ref[h : h + 1, span])
            pushed = contract(v_h[:size], g_h[span], 1, 1)
            dscore = (chance * (pushed - delta[:, span])).astype(low)
            part_v = jnp.dot(chance.astype(low), g_h[span], preferred_element_type=f32)
            part_k = jnp.dot(dscore, qq_h[span], preferred_element_type=f32)
            if h == 0 and t == seq // tile - 1:
                d_value[...] = part_v
                d_key[...] = part_k
            else:
                d_value[:size, :] += part_v
                d_key[:size, :] += part_k
            part_q = contract(kk_h[:size], dscore, 0, 0)
            d_query[t] = part_q if h == 0 else d_query[t] + part_q
    scale = HD**-0.5
    for t in range(seq // tile):
        mixed_ref[t * tile : (t + 1) * tile, :cols] = (d_query[t] * scale).T.astype(low)
    mixed_ref[:, cols : 2 * cols] = (d_key[...] * scale).astype(low)
    mixed_ref[:, 2 * cols :] = d_value[...].astype(low)
    mixed = mixed_ref[...]
    mixed_sums = jnp.sum(mixed.astype(f32), 0, keepdims=True)
    gain_sum = jnp.zeros((1, width), f32)
    shift_sum = jnp.zeros((1, width), f32)
    for t in range(seq // tile):
        grad = contract(mixed_ref[t * tile : (t + 1) * tile, :], w_ref[...], 1, 1)
        field = x_ref[t * tile : (t + 1) * tile, :].astype(f32)
        center = field - jnp.mean(field, -1, keepdims=True)
        unit = center * lax.rsqrt(jnp.mean(center * center, -1, keepdims=True) + norm_eps)
        gain_sum = gain_sum + jnp.sum(grad * unit, 0, keepdims=True)
        shift_sum = shift_sum + jnp.sum(grad, 0, keepdims=True)
        moved[t * tile : (t + 1) * tile, :] = grad.astype(low)
    n_line = spans // 4
    for y, ref in enumerate((in_keep, in_give)):
        for z in range(n_line):
            for u in range(2):
                part = pl.ds(pl.multiple_of(table[(y * n_line + z) * 2 + u] * half, half), half)
                ref[z, u * half : (u + 1) * half, :] = moved[part, :]
    row = lax.broadcasted_iota(jnp.int32, (8, width), 0)
    sums = jnp.where(row == 0, gain_sum, jnp.where(row == 1, shift_sum, sums_ref[...]))
    here = table[2 * spans + 4]
    small = lax.broadcasted_iota(jnp.int32, (8, cols), 0)
    bias = jnp.where(small == 4, mixed_sums[:, :cols], jnp.where(small == 5, mixed_sums[:, 2 * cols :], 0.0))
    terms = contract(mixed, normed[...], 0, 0)
    blank = jnp.zeros((rows - 8, cols), f32)
    for c in range(n_ctx):
        part = terms[:, c * 4 * rows : (c + 1) * 4 * rows].T.astype(low)
        block = sums[:, c * cols : (c + 1) * cols] + jnp.where(here == c, bias, 0.0)
        block = jnp.concatenate([block, blank], 0).astype(low)
        for f in range(4):
            made[(c * 4 + f) * rows : (c * 4 + f + 1) * rows, : 3 * cols] = part[f * rows : (f + 1) * rows]
            made[(c * 4 + f) * rows : (c * 4 + f + 1) * rows, 3 * cols :] = block
    at = 2 * spans + 5
    for which, ref in enumerate((keep_ref, give_ref)):
        for x in range(2):
            f = lax.rem(table[at + 2] + x, 2) * 2 + lax.rem(table[at + 3] + which, 2)
            for c in range(n_ctx):
                ref[x, c] = made[pl.ds(pl.multiple_of((c * 4 + f) * rows, rows), rows), :]


def square_kernel(table, qkv_ref, ff_ref, own_out, *refs):
    f32 = jnp.float32
    others, (square_ref, out_ref, vec_ref) = refs[:-3], refs[-3:]
    n_ctx, rows, wide = qkv_ref.shape
    cols = wide // 4
    at = 4 * n_ctx + 5
    out = own_out[...].astype(f32)
    for other in others:
        out = out + other[...].astype(f32)
    out_ref[...] = out
    small = jnp.sum(qkv_ref[:, :, 3 * cols :].astype(f32), 0)[:8]
    mine = table[at + 2] * 2 + table[at + 3]
    picked = jnp.zeros((8, rows), f32)
    for f in range(4):
        picked = picked + jnp.where(mine == f, small[:, f * rows : (f + 1) * rows], 0.0)
    vec_ref[...] = picked
    n_ff = ff_ref.shape[0] - 16
    bias = ff_ref[n_ff:, : 4 * rows].astype(f32)[0:1]
    squared = jnp.sum(jnp.square(bias), keepdims=True) + jnp.sum(jnp.square(picked), keepdims=True)
    squared = squared + jnp.sum(jnp.sum(jnp.square(ff_ref[:n_ff, :].astype(f32)), 0, keepdims=True), keepdims=True)
    squared = squared + jnp.sum(jnp.sum(jnp.square(out), 0, keepdims=True), keepdims=True)
    qkv = jnp.sum(jnp.square(qkv_ref[:, :, : 3 * cols].astype(f32)), 0)
    squared = squared + jnp.sum(jnp.sum(qkv, 0, keepdims=True), keepdims=True)
    square_ref[...] = jnp.broadcast_to(squared.reshape(1, 1, 1), square_ref.shape)


def clip_of(squares):
    norm = jnp.sqrt(jnp.sum(squares[...], 0)[:, 0:1])
    return norm, jnp.minimum(1.0, max_norm / (norm + 1e-06))


def adam_put(refs, spot, grad, clip):
    weight, first, second = refs[:3]
    new = adamw(weight[spot], grad, first[spot], second[spot], clip)
    for ref, value in zip(refs[3:], (grad,) + new):
        ref[spot] = value


def adam_kernel(*refs):
    f32 = jnp.float32
    squares, qkv_ref, out_ref, ff_ref, vec_ref = refs[:5]
    items = [[refs[5 + 5 * m + n] for m in range(3)] + list(refs[21 + 4 * n : 25 + 4 * n]) for n in range(5)]
    norm, clip = clip_of(squares)
    refs[20][...] = norm
    n_ctx, rows, wide = qkv_ref.shape
    cols = wide // 4
    width = n_ctx * cols
    ff = ff_ref.shape[1]
    own = 4 * rows
    n_ff = 8 * rows
    whole = (slice(None), slice(None))
    for c in range(n_ctx):
        for k in range(3):
            spot = (slice(None), slice(k * width + c * cols, k * width + (c + 1) * cols))
            adam_put(items[0], spot, qkv_ref[c, :, k * cols : (k + 1) * cols].astype(f32), clip)
    adam_put(items[1], whole, out_ref[...], clip)
    for h in range(width // ff):
        spot = (slice(None), slice(h * ff, (h + 1) * ff))
        adam_put(items[2], spot, ff_ref[n_ff + h * own : n_ff + (h + 1) * own, :].astype(f32), clip)
    n_down = n_ff + width // ff * own
    adam_put(items[3], whole, ff_ref[n_down:, :own].astype(f32)[0:1], clip)
    adam_put(items[4], whole, vec_ref[...], clip)


def adam_up_kernel(squares, up_ref, *refs):
    _, clip = clip_of(squares)
    n_plane, rows, ff = up_ref.shape
    own = 4 * rows
    for r in range(n_plane):
        for k in range(ff // own):
            spot = (slice(None), slice((k * n_plane + r) * own, (k * n_plane + r + 1) * own))
            adam_put(refs, spot, up_ref[r, :, k * own : (k + 1) * own].astype(jnp.float32), clip)


in_smem = pl.BlockSpec(memory_space=pltpu.SMEM)
in_vmem = pl.BlockSpec(memory_space=pltpu.VMEM)


def call(kernel, n_scalar, args, shapes, scratch=(), cost=1, limit=60):
    return pl.pallas_call(
        kernel,
        out_shape=[jax.ShapeDtypeStruct(s, d) for s, d in shapes],
        in_specs=[in_smem] * n_scalar + [in_vmem] * (len(args) - n_scalar),
        out_specs=[in_vmem] * len(shapes),
        scratch_shapes=[pltpu.VMEM(s, d) for s, d in scratch],
        compiler_params=pltpu.CompilerParams(vmem_limit_bytes=limit * 1024 * 1024),
        cost_estimate=pl.CostEstimate(flops=cost, bytes_accessed=cost, transcendentals=0),
    )(*args)


def attend_forward(table, slopes, blocks, pieces, start, cols):
    tokens, width = blocks[0].shape
    seq = tokens * len(blocks)
    f32, low = jnp.float32, jnp.bfloat16
    shapes = [
        ((seq, cols), low), ((cols, seq), f32), ((seq, 3 * cols), low), ((8, seq), f32),
        ((seq, width), low), ((seq, width), low), ((width, 3 * cols), low), ((8, width), f32),
    ]
    args = [table, slopes] + list(blocks) + list(pieces) + [start]
    return call(functools.partial(forward_kernel, len(blocks)), 2, args, shapes, [((width, 128), low)], 9000000000, 60)


def local_split(
    inputs, out_grad, segments, pairs,
    w_qkv, w_out, w_up, w_down, up_bias, vectors,
    first_qkv, first_out, first_up, first_down, first_bias, first_vectors,
    second_qkv, second_out, second_up, second_down, second_bias, second_vectors,
):
    low = jnp.bfloat16
    f32 = jnp.float32
    nz = lax.axis_size("z")
    n_ctx = 2 * nz
    every = ("z", "y", "x", "c")
    ctx = ("z", "y")
    plane = ("y", "x", "c")
    zi, yi, xi, ci = (lax.axis_index(a) for a in every)
    ctx_i = zi * 2 + yi
    tokens, width = inputs.shape[1:]
    half = tokens // 2
    seq_len = tokens * n_ctx
    heads_own = HEADS // n_ctx
    cols = heads_own * HD
    rows = w_qkv.shape[0]
    ff_own = w_down.shape[0]
    ff = nz * ff_own
    n_half = width // ff
    field_low = inputs[0]
    field = field_low.astype(f32)
    cot_low = out_grad[0]

    line = [shift(field_low, "z", nz, k) for k in range(1, nz)]
    own_two = exchange(jnp.stack([field_low, cot_low]), "y")
    shapes = [((n_ctx, rows, 3 * cols + 128), low), ((8, rows, ff), low), ((n_half, ff_own, ff), low), ((tokens, width // 4), low)]
    packed = [pairs, w_qkv, vectors, segments, up_bias.reshape(1, ff_own), w_up, w_down, w_out]
    first_send, up_send, down_part, out_low = call(pack_kernel, 1, packed, shapes, limit=60)
    first_got = swap(first_send, ctx)
    up_part = swap(after(up_send, first_got), plane).reshape(8 * rows, ff)
    ff_send = jnp.concatenate([up_part, down_part.reshape(n_half * ff_own, ff)], 0)
    ff_send, first_got, own_two, out_low = gate(ff_send, first_got, own_two, out_low)
    pair_own, cot_y = own_two[0], own_two[1]

    ff_all = lax.all_gather(ff_send, "z", axis=0)
    pair_line = [exchange(v, "y") for v in line]
    rest = [shift(out_low, "z", nz, k) for k in range(1, nz)]
    first_x = exchange(first_got, "x")
    first_c = exchange(first_got, "c")
    first_cx = exchange(first_x, "c")
    cot_two = jnp.stack([cot_low, cot_y])
    cot_x = exchange(cot_two, "x")
    seg_all = first_got[:, 0:2, 3 * cols + 64 :].reshape(seq_len).astype(jnp.int32)
    up_low = []
    for got in (first_got, first_c):
        bias_all = got[:, 2:4, 3 * cols + 64 :].reshape(nz, 2, ff_own)
        bias_all = lax.dynamic_index_in_dim(bias_all, yi, 1, keepdims=False)
        up_low = up_low + [bias_all.reshape(1, ff).astype(f32)]
    pair_all = first_got[:, 4, 3 * cols + 64].astype(jnp.int32)
    start = jnp.sum((seg_all[:, None] < seg_all[None, :]).astype(jnp.int32), 0, keepdims=True)
    slot_block = jnp.stack([pair_all, 2 * n_ctx - 1 - pair_all], 1)
    near = [((zi + k) % nz) * 2 + yi for k in range(nz)]
    near = jnp.stack(near + [((zi + k) % nz) * 2 + 1 - yi for k in range(nz)])
    ids = jnp.arange(n_ctx)
    near_block = jnp.sum(jnp.where((near[:, None] == ids[None, :])[:, :, None], slot_block[None], 0), 1)
    spans = jnp.arange(2 * n_ctx)
    block_slot = jnp.sum(jnp.where(slot_block.reshape(1, -1) == spans[:, None], spans[None, :], 0), 1)
    piece_f = jnp.stack([xi * 2 + ci, (1 - xi) * 2 + ci, xi * 2 + 1 - ci, (1 - xi) * 2 + 1 - ci])
    here = jnp.stack([ctx_i, zi, yi, xi, ci])
    table = jnp.concatenate([near_block.reshape(-1), block_slot, piece_f, here]).astype(jnp.int32)
    head_ids = (ctx_i * heads_own + jnp.arange(heads_own)).astype(f32)
    slopes = jnp.exp2(-8.0 * (head_ids + 1.0) / HEADS)
    out_z = jnp.stack([out_low] + rest)
    first_x, first_c, first_cx, cot_x, table, start, slopes, out_z, *pair_line = gate(
        first_x, first_c, first_cx, cot_x, table, start, slopes, out_z, *pair_line
    )

    out_y = exchange(out_z, "y")
    pieces = (first_got, first_x, first_c, first_cx)
    blocks = [field_low, pair_own] + pair_line + line
    attended, att_t, qkv_low, lse, normed_one, seq_rows, qkv_w, vec = attend_forward(
        table, slopes, blocks, pieces, start, cols
    )
    attended, out_y = gate(attended.reshape(n_ctx, tokens, cols), out_y)

    attended_low = swap(attended, ctx)
    out_zy = jnp.stack([out_z, out_y])
    out_x = exchange(out_zy, "x")
    out_c_two = exchange(out_zy, "c")
    attended_low, out_x, out_c_two = gate(attended_low, out_x, out_c_two)
    cots = [cot_two, cot_x]
    shapes = [((tokens, width), f32), ((tokens, width), low), ((width, width), low)]
    parts = [table, attended_low, out_zy, out_x, out_c_two, exchange(out_x, "c"), field_low, vec]
    resid, mlp_low, out_w = call(project_kernel, 1, parts, shapes)

    mlp_y = exchange(mlp_low, "y")
    mlp_x = exchange(mlp_low, "x")
    mlp_d0 = exchange(mlp_x[:half], "y")
    mlp_d1 = exchange(mlp_y[half:], "x")
    ff_other = exchange(after(ff_all, mlp_low), "c")
    mlp_d0, mlp_d1, ff_other = gate(mlp_d0, mlp_d1, ff_other)
    four = 4 * tokens
    one = ((tokens, width), low)
    shapes = [one] * 4 + [((four, 2 * ff), low)] * 2 + [((four, width), low)]
    scratch = [((2 * ff, width), low), ((width, 2 * ff), low)]
    rows_in = [mlp_low, mlp_y, mlp_x, mlp_d0, mlp_d1] + cots + [ff_all, ff_other] + up_low
    norm_own, norm_y, norm_x, norm_d, hidden, grad_pre, mlp_in = call(
        feed_kernel, 0, rows_in, shapes, scratch, limit=60
    )

    norm_d0 = exchange(norm_d[:half], "y")
    norm_d1 = exchange(norm_d[half:], "x")
    n_ff = 8 * rows + n_half * ff_own
    ff_keep, ff_give = call(
        feed_grad_kernel, 0, [mlp_in, grad_pre, hidden] + cots, [((nz, n_ff + 16, ff), low)] * 2, (), 1, 60
    )
    norm_d0, norm_d1, ff_give = gate(norm_d0, norm_d1, ff_give)
    norm_y = jnp.concatenate([norm_y[:half], add_low(norm_y[half:], norm_d1)], 0)
    norm_x = jnp.concatenate([add_low(norm_x[:half], norm_d0), norm_x[half:]], 0)
    norm_y, norm_x, ff_keep = gate(norm_y, norm_x, ff_keep)
    norm_y, norm_x = exchange(norm_y, "y"), exchange(norm_x, "x")
    ff_terms = add_low(ff_keep, exchange(ff_give, "c"))
    ff_sum = lax.psum_scatter(ff_terms, "z", scatter_dimension=0, tiled=True)[0]
    norm_x, norm_y, ff_terms = gate(norm_x, norm_y, ff_terms)
    shapes = [((tokens, width), f32), ((n_ctx, tokens, cols), low), ((8, width), f32)]
    shapes = shapes + [((2, 2, nz, rows, width), low)] * 2
    grad_resid, back_low, resid_sums, out_keep, out_give = call(
        norm_back_kernel,
        1,
        [table, norm_own, norm_x, norm_y, resid, cot_low, vec, out_w, attended_low],
        shapes,
        [((width, width), low)],
    )

    back_all = swap(back_low, ctx)
    out_c_got = exchange(out_give, "c")
    result_keep, result_give = call(
        result_kernel,
        0,
        [after(hidden, back_low), ff_all, ff_other],
        [((2, tokens, width), low)] * 2,
        [((2 * ff, width), low)],
    )
    back_all, out_c_got, result_keep, result_give = gate(back_all, out_c_got, result_keep, result_give)

    out_x_got = exchange(add_low(out_keep[1], out_c_got[1]), "x")
    shapes = [((2, n_ctx, rows, 4 * cols), low)] * 2
    shapes = shapes + [((nz, tokens, width), low)] * 2
    scratch = [((seq_len, 3 * cols), low), ((seq_len, cols), low), ((seq_len, cols), f32), ((seq_len, cols), f32)]
    scratch = scratch + [((seq_len, width), low), ((width, 4 * cols), low)]
    back_all = back_all.reshape(seq_len, cols)
    made = call(
        backward_kernel,
        2,
        [table, slopes, back_all, qkv_low, att_t, lse, start, normed_one, qkv_w, seq_rows, resid_sums],
        shapes,
        scratch,
        9000000000,
        60,
    )
    *made, out_x_got = gate(*made, out_x_got)
    qkv_keep, qkv_give, in_keep, in_give = made

    qkv_c_got = exchange(qkv_give, "c")
    qkv_c = add_low(qkv_keep[0], qkv_c_got[0])
    qkv_x_got = exchange(add_low(qkv_keep[1], qkv_c_got[1]), "x")
    out_c = add_low(out_keep[0], out_c_got[0])
    out_two = add_low(out_c[0], out_x_got[0])
    out_y_got = exchange(add_low(out_c[1], out_x_got[1]), "y")
    in_got = exchange(after(in_give, qkv_c), "y")
    qkv_x_got, qkv_c, out_y_got = gate(qkv_x_got, qkv_c, out_y_got)
    qkv_x = add_low(qkv_c, qkv_x_got)

    qkv_got = swap(qkv_x, ctx)
    out_y_got = after(out_y_got, qkv_x)
    out_own = add_low(out_two[0], out_y_got[0])
    out_moved = [shift(add_low(out_two[k], out_y_got[k]), "z", nz, -k) for k in range(1, nz)]
    up_send = after(ff_sum, qkv_x)[: 8 * rows].reshape(8, rows, ff)
    result_x = exchange(after(result_give, qkv_x), "x")
    result_y = exchange(add_low(result_keep[1], result_x[1]), "y")
    qkv_got, in_got, up_send, *out_moved = gate(qkv_got, in_got, up_send, *out_moved)
    shapes = [((4 * n_ctx, 1, 128), f32), ((rows, width), f32), ((8, rows), f32)]
    squared, grad_out_own, grad_vec_own = call(
        square_kernel, 1, [table, qkv_got, ff_sum, out_own, *out_moved], shapes, limit=48
    )

    squares = swap(squared, every)
    in_z = [shift(add_low(in_keep[k], in_got[k]), "z", nz, -k) for k in range(1, nz)]
    up_got = swap(after(up_send, squares), plane)
    masters = [w_qkv, w_out, w_down, up_bias.reshape(1, ff_own), vectors]
    firsts = [first_qkv, first_out, first_down, first_bias.reshape(1, ff_own), first_vectors]
    seconds = [second_qkv, second_out, second_down, second_bias.reshape(1, ff_own), second_vectors]
    shapes = [((1, 1), f32)]
    for item in masters:
        shapes = shapes + [(item.shape, f32)] * 4
    grads = [squares, qkv_got, grad_out_own, ff_sum, grad_vec_own]
    grad_norm, *results = call(adam_kernel, 0, grads + masters + firsts + seconds, shapes, limit=60)
    for k in range(12, 16):
        results[k] = results[k].reshape(ff_own)
    ups = call(adam_up_kernel, 0, [squares, up_got, w_up, first_up, second_up], [(w_up.shape, f32)] * 4, limit=60)
    results = results[:8] + list(ups) + results[8:]

    result_y = after(result_y, squares)
    result = (resid + result_keep[0].astype(f32) + result_x[0].astype(f32) + result_y.astype(f32) + vec[7]).astype(low)
    own_grads = in_keep[0].astype(f32) + in_got[0].astype(f32)
    for other in gate(*in_z, grad_norm)[:-1]:
        own_grads = own_grads + other.astype(f32)
    norm_one_back = jax.vjp(lambda v: layer_norm(v, vec[0], vec[1]), field)[1]
    in_grad = grad_resid + norm_one_back(own_grads)[0]
    return (result[None], in_grad[None], grad_norm[0, 0], *results)


def solution(mesh):
    n_ctx = mesh.shape["ctx"]
    if HEADS % n_ctx == 0 and n_ctx % 2 == 0 and mesh.shape["fsdp"] == 4:
        body = local_split
        ctx, fsdp = ("z", "y"), ("x", "c")
        mesh = Mesh(mesh.devices.reshape(n_ctx // 2, 2, 2, 2), ctx + fsdp)
    else:
        body = local
        ctx, fsdp = ("ctx",), ("fsdp",)
    rows = P(fsdp, ctx, None)
    flat = P(fsdp, ctx)
    mat = P(ctx + fsdp, None)
    vec = P(ctx + fsdp)
    wide = P(None, ctx + fsdp)
    group = (mat, mat, mat, mat, vec, wide)
    outs = ()
    for spec in group:
        outs = outs + (spec,) * 4
    return jax.shard_map(
        body,
        mesh=mesh,
        in_specs=(rows, rows, flat, flat) + group * 3,
        out_specs=(rows, rows, P()) + outs,
        check_vma=False,
    )
```
